32 devices in a mesh: seq: 4 (over x, core), exp: 8 (over z, y).
Axes of the slice: x: 2, y: 2, z: 4, core: 2. Of those that a mesh axis runs over, the one named last changes fastest.
Arguments:
- queries: bfloat16 [8, 256, 4096], P('exp', 'seq'), may hold values from -130 to 130
- new_keys: bfloat16 [8, 256, 512], P('exp', 'seq'), may hold values from -6 to 6
- new_values: bfloat16 [8, 256, 512], P('exp', 'seq'), may hold values from -6 to 6
- cache_keys: bfloat16 [8, 2048, 512], P('exp', 'seq'), may hold values from -7 to 7
- cache_values: bfloat16 [8, 2048, 512], P('exp', 'seq'), may hold values from -6 to 6
- cache_len: int32 [8], P('exp'), may hold values from 512 to 2048, as said below
- residual_in: bfloat16 [8, 256, 2048], P('exp', 'seq'), may hold values from -6 to 6
- out_weight: bfloat16 [4096, 2048], P('seq'), may hold values from -0.09375 to 0.09375
- norm_gain: float32 [2048], replicated, may hold values from 0.25 to 1.75
- router_weight: bfloat16 [2048, 32], replicated, may hold values from -0.125 to 0.125
- expert_ids: int32 [8, 256, 8], P('exp', 'seq'), may hold values from 0 to 31, all different within a row; in each aligned block of 64 rows (0 to 63, 64 to 127, ..., all dimensions but the last counted through in order) at most 24 rows name the same one
- gate_proj: bfloat16 [32, 2048, 768], P(('seq', 'exp')), may hold values from -0.125 to 0.125
- up_proj: bfloat16 [32, 2048, 768], P(('seq', 'exp')), may hold values from -0.125 to 0.125
- down_proj: bfloat16 [32, 768, 2048], P(('seq', 'exp')), may hold values from -0.21875 to 0.21875
Outputs:
- layer_out: bfloat16 [8, 256, 2048], P('exp', 'seq')
The draws below stay inside these ranges and needn't reach their ends.
Inputs may be any that keep to these rules, and one draw needn't show every extreme that they name: `expert_ids`: among the rows of one device (aligned blocks of 64 tokens of one document) no expert is chosen more than 24 times; every token chooses 8 different experts. `cache_len`: some document fills its whole cache.
All inputs are finite; a program needn't handle non-finite values.
Results may differ from the reference program's by a relative error of at most 0.0042.
Values may be sent and summed in bfloat16 or wider, within the bound.
No kernel may reach another device: no remote copies, remote signals or barrier semaphores. Data moves between devices by JAX's collectives and lax.ppermute only.
A program may use at most 128 MiB of HBM per device.

```python
import math
import jax
import jax.numpy as jnp
import numpy as np
from jax import lax

D = 2048
QH = 32
KVH = 4
HD = 128
F = 768
TOPK = 8
TOK_DEV = 64
EXPERTS = 32
DOCS = 8
QTOK = 256
CACHE = 2048
CAP = 24


def shared_draw(key):
    keys = jnp.clip(jax.random.normal(jax.random.fold_in(key, 11), (DOCS, CACHE, KVH * HD), jnp.float32), -6.0, 6.0)
    rows = jnp.clip(jax.random.normal(jax.random.fold_in(key, 12), (DOCS, QTOK, QH * HD), jnp.float32), -6.0, 6.0)
    return (keys, rows)


def draw_queries(key, part):
    return shared_draw(key)[1].astype(jnp.bfloat16)


def draw_cache_keys(key, part):
    return shared_draw(key)[0].astype(jnp.bfloat16)


def draw_cache_len(key, part):
    lengths = jax.random.randint(jax.random.fold_in(key, 3), (DOCS,), CACHE // 4, CACHE + 1)
    pick = jax.random.randint(jax.random.fold_in(key, 4), (), 0, DOCS)
    return lengths.at[pick].set(CACHE).astype(jnp.int32)


def shard_levels(rng, extent, split, smallest, top_value):
    factor_of, own = 1.0, jax.random.fold_in(rng, 6)
    for axis_at, blocks in split:
        steps = jnp.exp(jax.random.uniform(jax.random.fold_in(own, axis_at), (blocks,), jnp.float32, smallest / len(split), top_value / len(split)))
        factor_of = factor_of * jnp.repeat(steps, extent[axis_at] // blocks).reshape([-1 if axis == axis_at else 1 for axis in range(len(extent))])
    return factor_of


def shared_out(stream_key, own, number, rows, amount, top, bound, lean):
    order = jax.random.permutation(stream_key, amount)
    packed, common = shares(amount, rows * top, bound, lean, True), shares(amount, rows * top, bound, lean, False)
    places = jnp.arange(amount)

    def named(sizes, offset_by):
        used = int((sizes > 0).sum())
        fixed = max(1, used // 4)
        passed = fixed + (places - fixed + offset_by * (used - fixed)) % max(1, amount - fixed)
        return jnp.zeros((amount,), jnp.int32).at[order[jnp.where(places < fixed, places, passed)]].set(jnp.asarray(sizes, jnp.int32))

    sizes = jnp.where(number % 4 == 0, named(packed, number // 4), named(common, number - number // 4 - 1))
    mixed = jax.random.permutation(jax.random.fold_in(own, 3), amount)
    giver, taker = mixed[0:amount // 2 * 2:2], mixed[1:amount // 2 * 2:2]
    slack = jnp.minimum(sizes[giver] - 1, bound - sizes[taker]) // 2
    slack = jnp.where((giver == order[0]) | (taker == order[0]) | (sizes[taker] == 0), 0, jnp.maximum(slack, 0))
    passed = jax.random.randint(jax.random.fold_in(own, 4), (amount // 2,), 0, 1 << 20) % (slack + 1)
    sizes = sizes.at[giver].add(-passed).at[taker].add(passed)
    labels = jnp.searchsorted(jnp.cumsum(sizes), jnp.arange(rows * top), side="right").astype(jnp.int32)
    grid = labels.reshape(top, rows).T
    grid = grid[jax.random.permutation(jax.random.fold_in(own, 1), rows)]
    offset_by = jax.random.randint(jax.random.fold_in(own, 2), (rows, 1), 0, top)
    return jnp.take_along_axis(grid, (jnp.arange(top)[None, :] + offset_by) % top, axis=1)


def shares(number_of, total, bound, slope, full):
    loads = [(1 << 20) // math.isqrt(rank ** slope) + 1 for rank in range(1, number_of + 1)]
    largest = bound if full else min(bound, max(-(-total // number_of), total * loads[0] // sum(loads)))
    least = 1 if total - largest >= number_of - 1 else 0
    given, rest = [largest] + [least] * (number_of - 1), total - largest - least * (number_of - 1)
    while rest > 0:
        free = [i for i in range(1, number_of) if given[i] < largest] or [i for i in range(1, number_of) if given[i] < bound]
        pool, budget = sum([loads[i] for i in free]), rest
        for i in free:
            more = min(bound - given[i], max(1, budget * loads[i] // pool), rest)
            given[i] = given[i] + more
            rest = rest - more
    return np.array(given)


def scatter_about(stream_key, dims, scale, bound, shards=(), kind=jnp.bfloat16):
    array = jax.random.normal(stream_key, dims, jnp.float32) * scale
    if len(shards) > 0:
        array = shard_levels(stream_key, dims, shards, -0.22, 0.18) * array
    return jnp.clip(array, min=-bound, max=bound).astype(kind)


def setup_inputs(seed: int = 0) -> dict:
    key_list = jax.random.split(jax.random.key(seed), 15)
    queries = draw_queries(jax.random.fold_in(key_list[14], 71), 0)
    new_keys = scatter_about(key_list[1], (DOCS, QTOK, KVH * HD), 1.0, 6.0, ((0, 8), (1, 4)))
    new_values = scatter_about(key_list[2], (DOCS, QTOK, KVH * HD), 1.0, 6.0, ((0, 8), (1, 4)))
    cache_keys = draw_cache_keys(jax.random.fold_in(key_list[14], 71), 0)
    cache_values = scatter_about(key_list[4], (DOCS, CACHE, KVH * HD), 1.0, 6.0, ((0, 8), (1, 4)))
    cache_len = draw_cache_len(jax.random.fold_in(key_list[14], 71), 0)
    residual_in = scatter_about(key_list[6], (DOCS, QTOK, D), 1.0, 6.0, ((0, 8), (1, 4)))
    out_weight = scatter_about(key_list[7], (QH * HD, D), (QH * HD) ** -0.5, 0.09375, ((0, 4),))
    norm_gain = jnp.clip(1.0 + 0.15 * jax.random.normal(key_list[8], (D,), jnp.float32), 0.25, 1.75)
    router_weight = scatter_about(key_list[9], (D, EXPERTS), D ** -0.5, 0.125)
    expert_ids_keys = jax.random.split(jax.random.fold_in(key_list[10], 1), DOCS * QTOK // TOK_DEV)
    expert_ids_turns = jax.random.permutation(jax.random.fold_in(key_list[10], 3), DOCS * QTOK // TOK_DEV)
    expert_ids = jax.vmap(lambda own, number: shared_out(jax.random.fold_in(key_list[10], 2), own, number, TOK_DEV, EXPERTS, TOPK, CAP, 2))(expert_ids_keys, expert_ids_turns).reshape((DOCS, QTOK, TOPK))
    gate_proj = scatter_about(key_list[11], (EXPERTS, D, F), D ** -0.5, 0.125, ((0, 32),))
    up_proj = scatter_about(key_list[12], (EXPERTS, D, F), D ** -0.5, 0.125, ((0, 32),))
    down_proj = scatter_about(key_list[13], (EXPERTS, F, D), F ** -0.5, 0.21875, ((0, 32),))
    return {"queries": queries, "new_keys": new_keys, "new_values": new_values, "cache_keys": cache_keys, "cache_values": cache_values, "cache_len": cache_len, "residual_in": residual_in, "out_weight": out_weight, "norm_gain": norm_gain, "router_weight": router_weight, "expert_ids": expert_ids, "gate_proj": gate_proj, "up_proj": up_proj, "down_proj": down_proj}


def attend_doc(args):
    qrow, ckey, cval, nkey, nval, length = args
    group = QH // KVH
    total = CACHE + QTOK
    keys = jnp.concatenate([ckey, nkey], 0).reshape(total, KVH, HD).astype(jnp.float32)
    value_entries = jnp.concatenate([cval, nval], 0).reshape(total, KVH, HD).astype(jnp.float32)
    qheads = qrow.reshape(QTOK, KVH, group, HD).astype(jnp.float32)
    kpos = jnp.arange(total, dtype=jnp.int32)[None, :]
    qpos = jnp.arange(QTOK, dtype=jnp.int32)[:, None]
    visible = jnp.where(kpos < CACHE, kpos < length, kpos - CACHE <= qpos)

    def one_head(index_lookup):
        qsel = lax.dynamic_index_in_dim(qheads, index_lookup, 1, keepdims=False)
        ksel = lax.dynamic_index_in_dim(keys, index_lookup, 1, keepdims=False)
        selected_values = lax.dynamic_index_in_dim(value_entries, index_lookup, 1, keepdims=False)
        scores = jnp.einsum('qgd,kd->gqk', qsel, ksel) / jnp.sqrt(jnp.float32(HD))
        scores = jnp.where(visible[None], scores, jnp.float32(-1e+30))
        peak = lax.optimization_barrier(jnp.max(scores, axis=-1, keepdims=True))
        expo = jnp.exp(scores - peak)
        weight_matrices = (expo / lax.optimization_barrier(jnp.sum(expo, axis=-1, keepdims=True))).astype(jnp.bfloat16)
        return jnp.einsum('rxl,lc->xrc', weight_matrices.astype(jnp.float32), selected_values).astype(jnp.bfloat16)
    outs = lax.map(one_head, jnp.arange(KVH, dtype=jnp.int32))
    return jnp.transpose(outs, (1, 0, 2, 3)).reshape(QTOK, QH * HD)

def reference(queries, new_keys, new_values, cache_keys, cache_values, cache_len, residual_in, out_weight, norm_gain, router_weight, expert_ids, gate_proj, up_proj, down_proj):
    attn = lax.map(attend_doc, (queries, cache_keys, cache_values, new_keys, new_values, cache_len))
    count = DOCS * QTOK
    attn = attn.reshape(count, QH * HD)
    mixed = residual_in.reshape(count, D).astype(jnp.float32) + jnp.dot(attn, out_weight, preferred_element_type=jnp.float32)
    meansq = lax.optimization_barrier(jnp.mean(mixed * mixed, axis=-1, keepdims=True))
    normed = (mixed / jnp.sqrt(meansq + 1e-06) * norm_gain).astype(jnp.bfloat16)
    logits = jnp.dot(normed, router_weight, preferred_element_type=jnp.float32)
    chosen = expert_ids.reshape(count, TOPK)
    picked = jnp.take_along_axis(logits, chosen, axis=1)
    expo = jnp.exp(picked)
    gates = expo / lax.optimization_barrier(jnp.sum(expo, axis=1, keepdims=True))
    padded = jnp.concatenate([normed, jnp.zeros((1, D), jnp.bfloat16)], 0)
    slots = count // TOK_DEV * CAP

    def expert_step(acc, xs):
        wgate, wup, wdown, index_lookup = xs
        hit = chosen == index_lookup
        weight = lax.optimization_barrier(jnp.sum(jnp.where(hit, gates, jnp.float32(0.0)), axis=1))
        weight = jnp.concatenate([weight, jnp.zeros((1,), jnp.float32)], 0)
        rows = jnp.nonzero(jnp.any(hit, axis=1), size=slots, fill_value=count)[0].astype(jnp.int32)
        taken = padded[rows]
        gate = jnp.dot(taken, wgate, preferred_element_type=jnp.float32)
        upv = jnp.dot(taken, wup, preferred_element_type=jnp.float32)
        act = (jax.nn.silu(gate) * upv).astype(jnp.bfloat16)
        result = jnp.dot(act, wdown, preferred_element_type=jnp.float32).astype(jnp.bfloat16)
        acc = acc.at[rows].add(weight[rows][:, None] * result.astype(jnp.float32))
        return (acc, None)
    start = jnp.zeros((count + 1, D), jnp.float32)
    total, _ = lax.scan(expert_step, start, (gate_proj, up_proj, down_proj, jnp.arange(EXPERTS, dtype=jnp.int32)))
    out = mixed + total[:count]
    return out.astype(jnp.bfloat16).reshape(DOCS, QTOK, D)
```

```python
import functools
import math

import jax
import jax.numpy as jnp
from jax import lax
from jax.experimental import pallas as pl
from jax.experimental.pallas import tpu as pltpu
from jax.sharding import PartitionSpec as P

QH = 32
KVH = 4
HD = 128
TOPK = 8
MASKED = -1e30
EXP2_SCALE = math.log2(math.e) / math.sqrt(HD)
NT = (((1,), (1,)), ((), ()))
TN = (((0,), (0,)), ((), ()))
VMEM = pl.BlockSpec(memory_space=pltpu.VMEM)
SMEM = pl.BlockSpec(memory_space=pltpu.SMEM)
f32 = jnp.float32
bf16 = jnp.bfloat16


def swap(rows, axis, bits):
    return lax.ppermute(rows, axis, [(i, i ^ bits) for i in range(lax.axis_size(axis))])


def params(mib):
    return pltpu.CompilerParams(vmem_limit_bytes=mib << 20)


def pack_kernel(nseq, me_ref, q_ref, nk_ref, nv_ref, ck_ref, cv_ref, *outs):
    qcols = QH // nseq * HD
    for k in range(nseq):
        dest = me_ref[0] ^ k
        qat = pl.ds(pl.multiple_of(dest * qcols, HD), qcols)
        kvat = pl.ds(pl.multiple_of(dest * KVH // nseq * HD, HD), HD)
        head, cache = outs[k], outs[nseq + k]
        head[:, :qcols] = q_ref[:, qat]
        head[:, qcols : qcols + HD] = nk_ref[:, kvat]
        head[:, qcols + HD :] = nv_ref[:, kvat]
        cache[:, :HD] = ck_ref[:, kvat]
        cache[:, HD:] = cv_ref[:, kvat]


def pack(me, queries, new_keys, new_values, cache_keys, cache_values, nseq):
    tokens, slots = queries.shape[0], cache_keys.shape[0]
    qcols = QH // nseq * HD
    shapes = [jax.ShapeDtypeStruct((tokens, qcols + 2 * HD), bf16)] * nseq
    shapes += [jax.ShapeDtypeStruct((slots, 2 * HD), bf16)] * nseq
    outs = pl.pallas_call(
        functools.partial(pack_kernel, nseq),
        out_shape=shapes,
        in_specs=[SMEM] + [VMEM] * 5,
        out_specs=[VMEM] * (2 * nseq),
        compiler_params=params(24),
        name="pack_heads",
    )(me, queries, new_keys, new_values, cache_keys, cache_values)
    return outs[:nseq], outs[nseq:]


def head_rows(heads, start):
    return jnp.concatenate([ref[:, start : start + HD] for ref in heads], 0)


def slot_bias(me, length, ks, slots):
    parts = []
    for k in ks:
        pos = (me ^ k) * slots + lax.broadcasted_iota(jnp.int32, (1, slots), 1)
        parts.append(jnp.where(pos < length, f32(0.0), f32(MASKED)))
    return jnp.concatenate(parts, 1)


def near_kernel(nseq, me_ref, len_ref, *refs):
    heads, caches = refs[:nseq], refs[nseq : nseq + 2]
    peak_ref, sum_ref, acc_ref = refs[nseq + 2 :]
    group = QH // nseq
    slots = caches[0].shape[0]
    bias = slot_bias(me_ref[0], len_ref[0], (0, 1), slots)
    keys = jnp.concatenate([ref[:, :HD] for ref in caches], 0)
    vals = jnp.concatenate([ref[:, HD:] for ref in caches], 0)
    for g in range(group):
        q = head_rows(heads, g * HD)
        s = lax.dot_general(q, keys, NT, preferred_element_type=f32) + bias
        peak = jnp.max(s, axis=1, keepdims=True)
        p = jnp.exp2((s - peak) * f32(EXP2_SCALE))
        peak_ref[:, g : g + 1] = peak
        sum_ref[:, g : g + 1] = jnp.sum(p, axis=1, keepdims=True)
        acc_ref[:, g * HD : (g + 1) * HD] = jnp.dot(
            p.astype(bf16), vals, preferred_element_type=f32
        )


def far_kernel(nseq, me_ref, len_ref, *refs):
    heads, caches = refs[:nseq], refs[nseq : 2 * nseq - 2]
    peak_ref, sum_ref, acc_ref, w_ref, keep_ref, send_ref, attn_ref = refs[2 * nseq - 2 :]
    group = QH // nseq
    qcols = group * HD
    me = me_ref[0]
    slots, tokens = caches[0].shape[0], heads[0].shape[0]
    qtok = nseq * tokens
    bias = slot_bias(me, len_ref[0], range(2, nseq), slots)
    keys = jnp.concatenate([ref[:, :HD] for ref in caches], 0)
    vals = jnp.concatenate([ref[:, HD:] for ref in caches], 0)
    new_keys, new_vals = head_rows(heads, qcols), head_rows(heads, qcols + HD)
    row = lax.broadcasted_iota(jnp.int32, (qtok, qtok), 0)
    col = lax.broadcasted_iota(jnp.int32, (qtok, qtok), 1)
    qpos = (me ^ (row // tokens)) * tokens + row % tokens
    kpos = (me ^ (col // tokens)) * tokens + col % tokens
    new_bias = jnp.where(kpos <= qpos, f32(0.0), f32(MASKED))
    for g in range(group):
        at = slice(g * HD, (g + 1) * HD)
        q = head_rows(heads, g * HD)
        s = lax.dot_general(q, keys, NT, preferred_element_type=f32) + bias
        t = lax.dot_general(q, new_keys, NT, preferred_element_type=f32) + new_bias
        old = peak_ref[:, g : g + 1]
        peak = jnp.maximum(jnp.max(s, axis=1, keepdims=True), jnp.max(t, axis=1, keepdims=True))
        peak = jnp.maximum(peak, old)
        fade = jnp.exp2((old - peak) * f32(EXP2_SCALE))
        p = jnp.exp2((s - peak) * f32(EXP2_SCALE))
        r = jnp.exp2((t - peak) * f32(EXP2_SCALE))
        total = sum_ref[:, g : g + 1] * fade
        total += jnp.sum(p, axis=1, keepdims=True) + jnp.sum(r, axis=1, keepdims=True)
        acc = acc_ref[:, at] * fade
        acc += jnp.dot(p.astype(bf16), vals, preferred_element_type=f32)
        acc += jnp.dot(r.astype(bf16), new_vals, preferred_element_type=f32)
        attn_ref[:, at] = (acc / total).astype(bf16)
    for k in range(nseq):
        rows = attn_ref[k * tokens : (k + 1) * tokens, :]
        out = keep_ref if k % 2 == 0 else send_ref
        out[k // 2 * tokens : (k // 2 + 1) * tokens, :] = jnp.dot(
            rows, w_ref[...], preferred_element_type=f32
        )


def project_attention(me, length, queries, new_keys, new_values, cache_keys, cache_values, out_weight):
    nseq = lax.axis_size("seq")
    tokens, slots = queries.shape[0], cache_keys.shape[0]
    width = out_weight.shape[1]
    group = QH // nseq
    qtok = nseq * tokens
    heads, caches = pack(me, queries, new_keys, new_values, cache_keys, cache_values, nseq)
    order = sorted(range(1, nseq), reverse=True)
    heads = {0: heads[0]} | {k: swap(heads[k], "seq", k) for k in order}
    caches = {0: caches[0]} | {k: swap(caches[k], "seq", k) for k in order}
    heads = [heads[k] for k in range(nseq)]
    caches = [caches[k] for k in range(nseq)]
    state = pl.pallas_call(
        functools.partial(near_kernel, nseq),
        out_shape=[
            jax.ShapeDtypeStruct((qtok, HD), f32),
            jax.ShapeDtypeStruct((qtok, HD), f32),
            jax.ShapeDtypeStruct((qtok, group * HD), f32),
        ],
        in_specs=[SMEM] * 2 + [VMEM] * (nseq + 2),
        out_specs=[VMEM] * 3,
        compiler_params=params(32),
        name="attend_near",
    )(me, length, *heads, *caches[:2])
    half = nseq // 2 * tokens
    keep, send = pl.pallas_call(
        functools.partial(far_kernel, nseq),
        out_shape=[jax.ShapeDtypeStruct((half, width), f32)] * 2,
        in_specs=[SMEM] * 2 + [VMEM] * (2 * nseq + 2),
        out_specs=[VMEM] * 2,
        scratch_shapes=[pltpu.VMEM((qtok, group * HD), bf16)],
        compiler_params=params(48),
        name="attend_far",
    )(me, length, *heads, *caches[2:], *state, out_weight)
    got = swap(send, "seq", 1)
    others = []
    for k in range(2, nseq, 2):
        at = slice(k // 2 * tokens, (k // 2 + 1) * tokens)
        others.append(swap((keep[at] + got[at]).astype(bf16), "seq", k))
    return keep, got, others


def norm_kernel(others, res_ref, keep_ref, got_ref, *refs):
    gain_ref, router_ref, ids_ref, mixed_ref, rows_ref = refs[others:]
    tokens, width = res_ref.shape
    mixed = res_ref[...].astype(f32) + keep_ref[:tokens, :] + got_ref[:tokens, :]
    for ref in refs[:others]:
        mixed += ref[...].astype(f32)
    mixed_ref[...] = mixed
    meansq = jnp.mean(mixed * mixed, axis=1, keepdims=True)
    normed = (mixed / jnp.sqrt(meansq + 1e-06) * gain_ref[...]).astype(bf16)
    rows_ref[:, :width] = normed
    logits = jnp.dot(normed, router_ref[...], preferred_element_type=f32)
    nexp = logits.shape[1]
    expert = lax.broadcasted_iota(jnp.int32, (tokens, nexp), 1)
    chosen = expert == ids_ref[:, 0:1]
    for k in range(1, ids_ref.shape[1]):
        chosen = jnp.logical_or(chosen, expert == ids_ref[:, k : k + 1])
    expo = jnp.where(chosen, jnp.exp(logits), f32(0.0))
    gates = expo / jnp.sum(expo, axis=1, keepdims=True)
    high = gates.astype(bf16)
    low = (gates - high.astype(f32)).astype(bf16)
    extra = rows_ref.shape[1] - width
    row = lax.broadcasted_iota(jnp.int32, (nexp, extra), 0)
    col = lax.broadcasted_iota(jnp.int32, (nexp, extra), 1)
    spread = jnp.dot(high, (col == row).astype(bf16), preferred_element_type=f32)
    spread += jnp.dot(low, (col == row + nexp).astype(bf16), preferred_element_type=f32)
    rows_ref[:, width:] = spread.astype(bf16)


def norm_rows(residual, keep, got, others, gain, router, ids):
    tokens, width = residual.shape
    extra = -(-2 * router.shape[1] // 128) * 128
    return pl.pallas_call(
        functools.partial(norm_kernel, len(others)),
        out_shape=[
            jax.ShapeDtypeStruct((tokens, width), f32),
            jax.ShapeDtypeStruct((tokens, width + extra), bf16),
        ],
        in_specs=[VMEM] * (6 + len(others)),
        out_specs=[VMEM] * 2,
        compiler_params=params(24),
        name="norm_and_route",
    )(residual, keep, got, *others, gain.reshape(1, width), router, ids)


def gather_rows(rows, planes, sides):
    half = rows.shape[0] // 2
    columns = [rows] + [swap(rows, "exp", 2 * kz) for kz in range(1, planes)]
    blocks = []
    for col in columns:
        right = [swap(col, "seq", 2 * kx) for kx in range(1, sides)]
        up = swap(col, "exp", 1)
        over = [
            (swap(up[:half], "seq", 2 * kx), swap(right[kx - 1][half:], "exp", 1))
            for kx in range(1, sides)
        ]
        blocks.append([[(col,)] + [(r,) for r in right], [(up,)] + over])
    return blocks


def expert_kernel(planes, sides, cap, gtiles, dtiles, pieces, places, *refs):
    mine_ref = refs[0]
    blocks = refs[1 : 1 + pieces]
    (g0, u0, d0, g1, u1, d1) = refs[1 + pieces : 7 + pieces]
    nout = planes * 4
    outs = refs[7 + pieces : 7 + pieces + nout]
    x_ref, act_ref, y_ref, hot_ref, gate_ref = refs[7 + pieces + nout :]
    e, j = pl.program_id(0), pl.program_id(1)
    width = x_ref.shape[2]
    ext = blocks[0].shape[1] - width
    tokens = places["tokens"]
    per_group = 2 * sides
    gtok = per_group * tokens
    grows = per_group * cap
    step = 256

    @pl.when(jnp.logical_and(e == 0, j == 0))
    def gather():
        ecol = lax.broadcasted_iota(jnp.int32, (8, ext), 1)
        erow = lax.broadcasted_iota(jnp.int32, (8, ext), 0)
        want = jnp.where(erow == 0, mine_ref[0], jnp.where(erow == 1, mine_ref[1], -ext))
        nexp = places["nexp"]
        pick = jnp.logical_or(ecol == want, ecol == want + nexp).astype(bf16)
        trow = lax.broadcasted_iota(jnp.int32, (gtok, gtok), 0)
        tcol = lax.broadcasted_iota(jnp.int32, (gtok, gtok), 1)
        before = jnp.logical_and(trow < tcol, trow // tokens == tcol // tokens).astype(bf16)
        block = lax.broadcasted_iota(jnp.int32, (8, gtok), 1) // tokens
        slot = lax.broadcasted_iota(jnp.int32, (grows, gtok), 0).astype(f32)
        for g in range(planes):
            mine = [blocks[i] for i in places["blocks"][g]]
            tail = jnp.concatenate([ref[:, width:] for ref in mine], 0)
            gates = lax.dot_general(pick, tail, NT, preferred_element_type=f32)
            chosen = gates > 0.0
            rank = jnp.dot(chosen.astype(bf16), before, preferred_element_type=f32)
            target = jnp.where(chosen, (block * cap).astype(f32) + rank, f32(-1.0))
            hot = jnp.concatenate(
                [(slot == target[i : i + 1, :]).astype(f32) for i in range(2)], 0
            ).astype(bf16)
            hot_ref[g] = hot
            for at in range(0, width, step):
                part = jnp.concatenate([ref[:, at : at + step] for ref in mine], 0)
                got = jnp.dot(hot, part, preferred_element_type=f32).astype(bf16)
                for i in range(2):
                    x_ref[i, g * grows : (g + 1) * grows, at : at + step] = got[
                        i * grows : (i + 1) * grows
                    ]
            got = jnp.dot(hot, tail, preferred_element_type=f32)
            for i in range(2):
                sel = pick[i : i + 1, :].astype(f32)
                gate = jnp.sum(got[i * grows : (i + 1) * grows] * sel, axis=1, keepdims=True)
                gate_ref[i, g * grows : (g + 1) * grows, :] = jnp.broadcast_to(gate, (grows, 128))

    def expert(i, gate_w, up_w, down_w):
        @pl.when(jnp.logical_and(e == i, j < gtiles))
        def _():
            x = x_ref[i]
            tile = gate_w.shape[2]
            gate = jnp.dot(x, gate_w[0], preferred_element_type=f32)
            upv = jnp.dot(x, up_w[0], preferred_element_type=f32)
            act_ref[:, pl.ds(pl.multiple_of(j * tile, 128), tile)] = (
                gate / (1.0 + jnp.exp(-gate)) * upv
            ).astype(bf16)

        @pl.when(jnp.logical_and(e == i, j >= gtiles))
        def _():
            tile = down_w.shape[2]
            y = jnp.dot(act_ref[...], down_w[0], preferred_element_type=f32)
            y = y * gate_ref[i][:, 0:1]
            y_ref[i, :, pl.ds(pl.multiple_of((j - gtiles) * tile, 128), tile)] = y.astype(bf16)

    expert(0, g0, u0, d0)
    expert(1, g1, u1, d1)

    @pl.when(jnp.logical_and(e == 1, j == gtiles + dtiles - 1))
    def scatter():
        half = tokens // 2
        for g in range(planes):
            hot = hot_ref[g]
            keep_a, keep_b, send_a, send_b = outs[4 * g : 4 * g + 4]
            for at in range(0, width, step):
                y = jnp.concatenate(
                    [y_ref[i, g * grows : (g + 1) * grows, at : at + step] for i in range(2)], 0
                )
                total = lax.dot_general(hot, y, TN, preferred_element_type=f32).astype(bf16)
                cols = slice(at, at + step)
                for ky in range(2):
                    for kx in range(sides):
                        row = (ky * sides + kx) * tokens
                        low, high = total[row : row + half], total[row + half : row + tokens]
                        if kx == 0:
                            keep_a[ky * half : (ky + 1) * half, cols] = low
                        else:
                            a = ((kx - 1) * 2 + ky) * half
                            send_a[a : a + half, cols] = low
                        b = keep_b if ky == 0 else send_b
                        b[kx * half : (kx + 1) * half, cols] = high


def expert_terms(blocks, mine, weights, cap, nexp):
    planes, sides = len(blocks), len(blocks[0][0])
    tokens = blocks[0][0][0][0].shape[0]
    flat, index = [], []
    for plane in blocks:
        at = []
        for line in plane:
            for pieces in line:
                at += range(len(flat), len(flat) + len(pieces))
                flat += pieces
        index.append(at)
    gate0, up0, down0, gate1, up1, down1 = weights
    _, width, hidden = gate0.shape
    gtiles, dtiles = hidden // 256, width // 1024
    grows = 2 * sides * cap
    rows = planes * grows
    half = tokens // 2

    def first(e, j, tiles, base):
        t = jnp.clip(j - base, 0, tiles - 1)
        return jnp.where(e == 0, t, tiles - 1)

    def second(e, j, tiles, base):
        t = jnp.clip(j - base, 0, tiles - 1)
        return jnp.where(e == 1, t, 0)

    def specs(which):
        wide = pl.BlockSpec((1, width, 256), lambda e, j: (0, 0, which(e, j, gtiles, 0)))
        down = pl.BlockSpec((1, hidden, 1024), lambda e, j: (0, 0, which(e, j, dtiles, gtiles)))
        return [wide, wide, down]

    out_shape = []
    for _ in range(planes):
        out_shape += [
            jax.ShapeDtypeStruct((2 * half, width), bf16),
            jax.ShapeDtypeStruct((sides * half, width), bf16),
            jax.ShapeDtypeStruct(((sides - 1) * 2 * half, width), bf16),
            jax.ShapeDtypeStruct((sides * half, width), bf16),
        ]
    places = {"tokens": tokens, "blocks": index, "nexp": nexp}
    kernel = functools.partial(
        expert_kernel, planes, sides, cap, gtiles, dtiles, len(flat), places
    )
    outs = pl.pallas_call(
        kernel,
        grid=(2, gtiles + dtiles),
        out_shape=out_shape,
        in_specs=[SMEM] + [VMEM] * len(flat) + specs(first) + specs(second),
        out_specs=[VMEM] * len(out_shape),
        scratch_shapes=[
            pltpu.VMEM((2, rows, width), bf16),
            pltpu.VMEM((rows, hidden), bf16),
            pltpu.VMEM((2, rows, width), bf16),
            pltpu.VMEM((planes, 2 * grows, 2 * sides * tokens), bf16),
            pltpu.VMEM((2, rows, 128), f32),
        ],
        compiler_params=params(52),
        name="experts",
    )(mine, *flat, *weights)
    return [outs[4 * g : 4 * g + 4] for g in range(planes)]


def add(*terms):
    total = terms[0].astype(f32)
    for term in terms[1:]:
        total = total + term.astype(f32)
    return total


def return_terms(terms, sides):
    own = []
    for kz in reversed(range(len(terms))):
        keep_a, keep_b, send_a, send_b = terms[kz]
        half = keep_a.shape[0] // 2
        got_a = [
            swap(send_a[(kx - 1) * 2 * half : kx * 2 * half], "seq", 2 * kx)
            for kx in range(1, sides)
        ]
        got_b = swap(send_b, "exp", 1)
        next_a = swap(
            add(keep_a[half:], *[a[half:] for a in got_a]).astype(bf16), "exp", 1
        )
        next_b = [
            swap(
                add(keep_b[kx * half : (kx + 1) * half], got_b[kx * half : (kx + 1) * half]).astype(bf16),
                "seq",
                2 * kx,
            )
            for kx in range(1, sides)
        ]
        top = add(keep_a[:half], *[a[:half] for a in got_a], next_a)
        low = add(keep_b[:half], got_b[:half], *next_b)
        if kz == 0:
            own.append(jnp.concatenate([top, low], 0))
        else:
            both = jnp.concatenate([top.astype(bf16), low.astype(bf16)], 0)
            own.append(swap(both, "exp", 2 * kz).astype(f32))
    return own


def experts_by_chip(rows, width, weights, nexp):
    nseq, nplace = lax.axis_size("seq"), lax.axis_size("exp")
    cap = 3 * rows.shape[0] * TOPK // (2 * nexp)
    planes, sides = nplace // 2, nseq // 2
    me = lax.axis_index("seq") * nplace + lax.axis_index("exp")
    other = (lax.axis_index("seq") ^ 1) * nplace + lax.axis_index("exp")
    mine = jnp.stack([me, other]).astype(jnp.int32)
    blocks = gather_rows(rows, planes, sides)
    return return_terms(expert_terms(blocks, mine, weights, cap, nexp), sides)


def experts_by_device(rows, width, ids, gate_proj, up_proj, down_proj, nexp):
    tokens = rows.shape[0]
    normed = rows[:, :width]
    gates = rows[:, width : width + nexp].astype(f32) + rows[
        :, width + nexp : width + 2 * nexp
    ].astype(f32)
    gates = jnp.take_along_axis(gates, ids, axis=1)
    capacity = 3 * tokens * TOPK // (2 * nexp)
    flat = ids.reshape(-1)
    member = (flat[:, None] == jnp.arange(nexp, dtype=jnp.int32)[None, :]).astype(jnp.int32)
    rank = jnp.sum((jnp.cumsum(member, axis=0) - 1) * member, axis=1)
    slot = flat * capacity + rank
    place = slot[:, None] == jnp.arange(nexp * capacity, dtype=jnp.int32)[None, :]
    route = jnp.any(place.reshape(tokens, TOPK, nexp * capacity), axis=1).astype(bf16)
    packed = jnp.einsum("ts,td->sd", route, normed, preferred_element_type=f32).astype(bf16)
    outgoing = packed.reshape(nexp, capacity, width)
    taken = lax.all_to_all(outgoing, ("seq", "exp"), split_axis=0, concat_axis=0, tiled=True)
    taken = taken.reshape(-1, width)
    gate = jnp.dot(taken, gate_proj[0], preferred_element_type=f32)
    upv = jnp.dot(taken, up_proj[0], preferred_element_type=f32)
    act = (jax.nn.silu(gate) * upv).astype(bf16)
    result = jnp.dot(act, down_proj[0], preferred_element_type=f32).astype(bf16)
    result = result.reshape(nexp, capacity, width)
    back = lax.all_to_all(result, ("seq", "exp"), split_axis=0, concat_axis=0, tiled=True)
    gathered = back.reshape(nexp * capacity, width)[slot].reshape(tokens, TOPK, width)
    return [jnp.sum(gates[:, :, None] * gathered.astype(f32), axis=1)]


def body(
    queries,
    new_keys,
    new_values,
    cache_keys,
    cache_values,
    cache_len,
    residual_in,
    out_weight,
    norm_gain,
    router_weight,
    expert_ids,
    gate_proj,
    up_proj,
    down_proj,
):
    nseq, nplace = lax.axis_size("seq"), lax.axis_size("exp")
    tokens, width = residual_in.shape[1:]
    nexp = router_weight.shape[1]
    by_chip = nseq * nplace <= 32
    me = lax.axis_index("seq").astype(jnp.int32).reshape(1)
    keep, got, others = project_attention(
        me,
        cache_len,
        queries[0],
        new_keys[0],
        new_values[0],
        cache_keys[0],
        cache_values[0],
        out_weight,
    )
    mixed, rows = norm_rows(
        residual_in[0], keep, got, others, norm_gain, router_weight, expert_ids[0]
    )
    if by_chip:
        weights = [gate_proj, up_proj, down_proj]
        weights += [swap(w, "seq", 1) for w in weights]
        terms = experts_by_chip(rows, width, weights, nexp)
    else:
        terms = experts_by_device(
            rows, width, expert_ids[0], gate_proj, up_proj, down_proj, nexp
        )
    return add(mixed, *terms).astype(bf16).reshape(1, tokens, width)


def solution(mesh):
    in_specs = (
        P("exp", "seq", None),
        P("exp", "seq", None),
        P("exp", "seq", None),
        P("exp", "seq", None),
        P("exp", "seq", None),
        P("exp"),
        P("exp", "seq", None),
        P("seq", None),
        P(),
        P(),
        P("exp", "seq", None),
        P(("seq", "exp"), None, None),
        P(("seq", "exp"), None, None),
        P(("seq", "exp"), None, None),
    )
    out_specs = P("exp", "seq", None)
    return jax.shard_map(body, mesh=mesh, in_specs=in_specs, out_specs=out_specs, check_vma=False)
```

```python
import functools
import math

import jax
import jax.numpy as jnp
from jax import lax
from jax.experimental import pallas as pl
from jax.experimental.pallas import tpu as pltpu
from jax.sharding import PartitionSpec as P

QH = 32
KVH = 4
HD = 128
TOPK = 8
MASKED = -1e30
EXPERT_MIB = 46
NEAR_MIB = 58
FAR_MIB = 54
EXP2_SCALE = math.log2(math.e) / math.sqrt(HD)
NT = (((1,), (1,)), ((), ()))
TN = (((0,), (0,)), ((), ()))
VMEM = pl.BlockSpec(memory_space=pltpu.VMEM)
SMEM = pl.BlockSpec(memory_space=pltpu.SMEM)
ANY = pl.BlockSpec(memory_space=pl.ANY)
f32 = jnp.float32
bf16 = jnp.bfloat16


def swap(rows, axis, bits):
    return lax.ppermute(rows, axis, [(i, i ^ bits) for i in range(lax.axis_size(axis))])


def params(mib):
    return pltpu.CompilerParams(vmem_limit_bytes=mib << 20)


def pack_kernel(nseq, me_ref, q_ref, nk_ref, nv_ref, ck_ref, cv_ref, *refs):
    heads, caches, sem = refs[:nseq], refs[nseq : 2 * nseq], refs[-1]
    qcols = QH // nseq * HD
    copies = []
    for k in range(nseq):
        dest = me_ref[0] ^ k
        qat = pl.ds(pl.multiple_of(dest * qcols, HD), qcols)
        kvat = pl.ds(pl.multiple_of(dest * KVH // nseq * HD, HD), HD)
        pairs = (
            (q_ref.at[:, qat], heads[k].at[:, :qcols]),
            (nk_ref.at[:, kvat], heads[k].at[:, qcols : qcols + HD]),
            (nv_ref.at[:, kvat], heads[k].at[:, qcols + HD :]),
            (ck_ref.at[:, kvat], caches[k].at[:, :HD]),
            (cv_ref.at[:, kvat], caches[k].at[:, HD:]),
        )
        copies += [pltpu.make_async_copy(a, b, sem.at[k, i]) for i, (a, b) in enumerate(pairs)]
    for copy in copies:
        copy.start()
    for copy in copies:
        copy.wait()


def pack(me, arrays, nseq):
    tokens, slots = arrays[0].shape[0], arrays[-1].shape[0]
    shapes = [jax.ShapeDtypeStruct((tokens, (QH // nseq + 2) * HD), bf16)] * nseq
    shapes += [jax.ShapeDtypeStruct((slots, 2 * HD), bf16)] * nseq
    outs = pl.pallas_call(
        functools.partial(pack_kernel, nseq),
        out_shape=shapes,
        in_specs=[SMEM] + [ANY] * len(arrays),
        out_specs=[VMEM] * len(shapes),
        scratch_shapes=[pltpu.SemaphoreType.DMA((nseq, len(arrays)))],
        compiler_params=params(61),
        name="pack_heads",
    )(me, *arrays)
    return outs[:nseq], outs[nseq:]


def head_rows(heads, start):
    return jnp.concatenate([ref[:, start : start + HD] for ref in heads], 0)


def slot_bias(me, length, ks, slots):
    parts = []
    for k in ks:
        pos = (me ^ k) * slots + lax.broadcasted_iota(jnp.int32, (1, slots), 1)
        parts.append(jnp.where(pos < length, f32(0.0), f32(MASKED)))
    return jnp.concatenate(parts, 1)


def near_kernel(nseq, me_ref, len_ref, *refs):
    heads, caches = refs[:nseq], refs[nseq : nseq + 2]
    peak_ref, sum_ref, acc_ref = refs[nseq + 2 :]
    group = QH // nseq
    qcols = group * HD
    me = me_ref[0]
    slots, tokens = caches[0].shape[0], heads[0].shape[0]
    qtok = nseq * tokens
    bias = slot_bias(me, len_ref[0], (0, 1), slots)
    keys = jnp.concatenate([ref[:, :HD] for ref in caches], 0)
    vals = jnp.concatenate([ref[:, HD:] for ref in caches], 0)
    new_keys, new_vals = head_rows(heads, qcols), head_rows(heads, qcols + HD)
    row = lax.broadcasted_iota(jnp.int32, (qtok, qtok), 0)
    col = lax.broadcasted_iota(jnp.int32, (qtok, qtok), 1)
    qpos = (me ^ (row // tokens)) * tokens + row % tokens
    kpos = (me ^ (col // tokens)) * tokens + col % tokens
    new_bias = jnp.where(kpos <= qpos, f32(0.0), f32(MASKED))
    for g in range(group):
        q = head_rows(heads, g * HD)
        s = lax.dot_general(q, keys, NT, preferred_element_type=f32) + bias
        t = lax.dot_general(q, new_keys, NT, preferred_element_type=f32) + new_bias
        peak = jnp.maximum(jnp.max(s, axis=1, keepdims=True), jnp.max(t, axis=1, keepdims=True))
        p = jnp.exp2((s - peak) * f32(EXP2_SCALE))
        r = jnp.exp2((t - peak) * f32(EXP2_SCALE))
        peak_ref[:, g : g + 1] = peak
        sum_ref[:, g : g + 1] = jnp.sum(p, axis=1, keepdims=True) + jnp.sum(r, axis=1, keepdims=True)
        acc = jnp.dot(p.astype(bf16), vals, preferred_element_type=f32)
        acc += jnp.dot(r.astype(bf16), new_vals, preferred_element_type=f32)
        acc_ref[:, g * HD : (g + 1) * HD] = acc


def far_kernel(nseq, me_ref, len_ref, *refs):
    heads, caches = refs[:nseq], refs[nseq : 2 * nseq - 2]
    peak_ref, sum_ref, acc_ref, w_hbm = refs[2 * nseq - 2 : 2 * nseq + 2]
    outs = refs[2 * nseq + 2 : -3]
    attn_ref, w_ref, sem = refs[-3:]
    load = pltpu.make_async_copy(w_hbm, w_ref, sem)
    load.start()
    group = QH // nseq
    slots, tokens = caches[0].shape[0], heads[0].shape[0]
    bias = slot_bias(me_ref[0], len_ref[0], range(2, nseq), slots)
    keys = jnp.concatenate([ref[:, :HD] for ref in caches], 0)
    vals = jnp.concatenate([ref[:, HD:] for ref in caches], 0)
    for g in range(group):
        at = slice(g * HD, (g + 1) * HD)
        q = head_rows(heads, g * HD)
        s = lax.dot_general(q, keys, NT, preferred_element_type=f32) + bias
        old = peak_ref[:, g : g + 1]
        peak = jnp.maximum(jnp.max(s, axis=1, keepdims=True), old)
        fade = jnp.exp2((old - peak) * f32(EXP2_SCALE))
        p = jnp.exp2((s - peak) * f32(EXP2_SCALE))
        total = sum_ref[:, g : g + 1] * fade + jnp.sum(p, axis=1, keepdims=True)
        acc = acc_ref[:, at] * fade + jnp.dot(p.astype(bf16), vals, preferred_element_type=f32)
        attn_ref[:, at] = (acc / total).astype(bf16)
    load.wait()
    send, near, far = outs
    places = []
    for k in range(nseq):
        if k % 2:
            places.append((send, k // 2 * tokens))
        else:
            places.append((far, (k // 2 - 1) * tokens) if k else (near, 0))
    step = 512
    for at in range(0, w_ref.shape[1], step):
        cols = slice(at, at + step)
        total = jnp.dot(attn_ref[...], w_ref[:, cols], preferred_element_type=f32)
        for k, (out, row) in enumerate(places):
            out[row : row + tokens, cols] = total[k * tokens : (k + 1) * tokens]


def project_attention(
    me, length, queries, new_keys, new_values, cache_keys, cache_values, out_weight, weights
):
    nseq = lax.axis_size("seq")
    tokens = queries.shape[0]
    width = out_weight.shape[1]
    group = QH // nseq
    qtok = nseq * tokens
    heads, caches = pack(me, (queries, new_keys, new_values, cache_keys, cache_values), nseq)
    order = sorted(range(1, nseq), reverse=True)
    heads = {0: heads[0]} | {k: swap(heads[k], "seq", k) for k in order}
    caches = {0: caches[0]} | {k: swap(caches[k], "seq", k) for k in order}
    heads, weights = lax.optimization_barrier((heads, weights))
    others = [swap(w, "seq", 1) for w in weights[:2]]
    heads = [heads[k] for k in range(nseq)]
    caches = [caches[k] for k in range(nseq)]
    state = pl.pallas_call(
        functools.partial(near_kernel, nseq),
        out_shape=[
            jax.ShapeDtypeStruct((qtok, HD), f32),
            jax.ShapeDtypeStruct((qtok, HD), f32),
            jax.ShapeDtypeStruct((qtok, group * HD), f32),
        ],
        in_specs=[SMEM] * 2 + [VMEM] * (nseq + 2),
        out_specs=[VMEM] * 3,
        compiler_params=params(NEAR_MIB),
        name="attend_near",
    )(me, length, *heads, *caches[:2])
    half = nseq // 2 * tokens
    parts = pl.pallas_call(
        functools.partial(far_kernel, nseq),
        out_shape=[
            jax.ShapeDtypeStruct((half, width), f32),
            jax.ShapeDtypeStruct((tokens, width), f32),
            jax.ShapeDtypeStruct((half - tokens, width), f32),
        ],
        in_specs=[SMEM] * 2 + [VMEM] * (2 * nseq + 1) + [ANY],
        out_specs=[VMEM] * 3,
        scratch_shapes=[
            pltpu.VMEM((qtok, group * HD), bf16),
            pltpu.VMEM(out_weight.shape, bf16),
            pltpu.SemaphoreType.DMA,
        ],
        compiler_params=params(FAR_MIB),
        name="attend_far",
    )(me, length, *heads, *caches[2:], *state, out_weight)
    (send, near, far), others = lax.optimization_barrier((parts, others))
    got = swap(send, "seq", 1)
    if weights:
        got, last = lax.optimization_barrier((got, weights[2]))
        others.append(swap(last, "seq", 1))
    terms = [near, got[:tokens]]
    for at in range(tokens, half, tokens):
        both = far[at - tokens : at] + got[at : at + tokens]
        terms.append(swap(both.astype(bf16), "seq", 2 * at // tokens))
    return terms, [*weights, *others]


def norm_kernel(nterms, res_ref, *refs):
    gain_ref, router_ref, ids_ref, mixed_ref, rows_ref = refs[nterms:]
    tokens, width = res_ref.shape
    mixed = res_ref[...].astype(f32)
    for ref in refs[:nterms]:
        mixed += ref[...].astype(f32)
    mixed_ref[...] = mixed
    meansq = jnp.mean(mixed * mixed, axis=1, keepdims=True)
    normed = (mixed / jnp.sqrt(meansq + 1e-06) * gain_ref[...]).astype(bf16)
    rows_ref[:, :width] = normed
    logits = lax.dot_general(router_ref[...], normed, NT, preferred_element_type=f32)
    nexp = logits.shape[0]
    expert = lax.broadcasted_iota(jnp.int32, (nexp, tokens), 0)
    chosen = expert == ids_ref[0:1, :]
    for k in range(1, ids_ref.shape[0]):
        chosen = jnp.logical_or(chosen, expert == ids_ref[k : k + 1, :])
    expo = jnp.where(chosen, jnp.exp(logits), f32(0.0))
    gates = expo / jnp.sum(expo, axis=0, keepdims=True)
    high = gates.astype(bf16)
    low = (gates - high.astype(f32)).astype(bf16)
    extra = rows_ref.shape[1] - width
    row = lax.broadcasted_iota(jnp.int32, (nexp, extra), 0)
    col = lax.broadcasted_iota(jnp.int32, (nexp, extra), 1)
    spread = lax.dot_general(high, (col == row).astype(bf16), TN, preferred_element_type=f32)
    spread += lax.dot_general(low, (col == row + nexp).astype(bf16), TN, preferred_element_type=f32)
    rows_ref[:, width:] = spread.astype(bf16)


def norm_rows(residual, terms, gain, router, ids):
    tokens, width = residual.shape
    extra = -(-2 * router.shape[1] // 128) * 128
    return pl.pallas_call(
        functools.partial(norm_kernel, len(terms)),
        out_shape=[
            jax.ShapeDtypeStruct((tokens, width), f32),
            jax.ShapeDtypeStruct((tokens, width + extra), bf16),
        ],
        in_specs=[VMEM] * (4 + len(terms)),
        out_specs=[VMEM] * 2,
        compiler_params=params(16),
        name="norm_and_route",
    )(residual, *terms, gain.reshape(1, width), router.T, ids.T)


def gather_plane(col, kz, sides, first=None):
    right = [swap(col, "seq", 2 * kx) for kx in range(1, sides)]
    up = swap(col, "exp", 1)
    if first:
        right, up, first = lax.optimization_barrier((right, up, first))
    if kz % 2:
        over = [swap(r, "exp", 1) for r in right]
    else:
        over = [swap(up, "seq", 2 * kx) for kx in range(1, sides)]
    return [col, *right, up, *over], first


def plane_layout(mode, sides, tokens):
    half = tokens // 2
    rows, moves = [], []
    if mode == "halves":
        rows = [2 * half, sides * half, (sides - 1) * 2 * half, sides * half]
        for ky in range(2):
            for kx in range(sides):
                row = (ky * sides + kx) * tokens
                top = (2, ((kx - 1) * 2 + ky) * half) if kx else (0, ky * half)
                moves.append((row, half, *top))
                moves.append((row + half, half, 3 if ky else 1, kx * half))
    elif mode == "x":
        rows = [2 * tokens, (sides - 1) * 2 * tokens]
        for ky in range(2):
            for kx in range(sides):
                to = (1, ((kx - 1) * 2 + ky) * tokens) if kx else (0, ky * tokens)
                moves.append(((ky * sides + kx) * tokens, tokens, *to))
    else:
        rows = [sides * tokens, sides * tokens]
        for ky in range(2):
            for kx in range(sides):
                moves.append(((ky * sides + kx) * tokens, tokens, ky, kx * tokens))
    return rows, moves


def expert_kernel(layouts, per_group, tokens, cap, nexp, mine_ref, *refs):
    planes = len(layouts)
    pieces = planes * per_group
    blocks = refs[:pieces]
    weights = (refs[pieces : pieces + 3], refs[pieces + 3 : pieces + 6])
    nouts = sum(len(rows) for rows, _ in layouts)
    outs = refs[pieces + 6 : pieces + 6 + nouts]
    got_ref, x_ref, act_ref, hot_ref, wide_ref, down_ref, sem, got_sem = refs[pieces + 6 + nouts :]
    copies = [
        pltpu.make_async_copy(
            blocks[g * per_group + i],
            got_ref.at[g, i * tokens : (i + 1) * tokens],
            got_sem.at[g, i],
        )
        for g in range(planes)
        for i in range(per_group)
    ]
    for copy in copies:
        copy.start()
    loads = [
        [
            pltpu.make_async_copy(ws[0].at[0], wide_ref.at[i, 0], sem.at[i, 0]),
            pltpu.make_async_copy(ws[1].at[0], wide_ref.at[i, 1], sem.at[i, 1]),
            pltpu.make_async_copy(ws[2].at[0], down_ref.at[i], sem.at[i, 2]),
        ]
        for i, ws in enumerate(weights)
    ]
    loads[0][0].start()
    loads[0][1].start()
    width = x_ref.shape[2]
    hidden = act_ref.shape[1]
    ext = got_ref.shape[2] - width
    gtok = per_group * tokens
    grows = per_group * cap
    step = 256
    ecol = lax.broadcasted_iota(jnp.int32, (8, ext), 1)
    erow = lax.broadcasted_iota(jnp.int32, (8, ext), 0)
    want = jnp.where(erow == 0, mine_ref[0], jnp.where(erow == 1, mine_ref[1], -ext))
    pick = jnp.logical_or(ecol == want, ecol == want + nexp).astype(bf16)
    trow = lax.broadcasted_iota(jnp.int32, (gtok, gtok), 0)
    tcol = lax.broadcasted_iota(jnp.int32, (gtok, gtok), 1)
    before = jnp.logical_and(trow < tcol, trow // tokens == tcol // tokens).astype(bf16)
    block = lax.broadcasted_iota(jnp.int32, (8, gtok), 1) // tokens
    slot = lax.broadcasted_iota(jnp.int32, (grows, gtok), 0).astype(f32)
    row_gates = [[], []]
    for g in range(planes):
        for copy in copies[g * per_group : (g + 1) * per_group]:
            copy.wait()
        tail = got_ref[g, :, width:]
        gates = lax.dot_general(pick, tail, NT, preferred_element_type=f32)
        chosen = gates > 0.0
        rank = jnp.dot(chosen.astype(bf16), before, preferred_element_type=f32)
        target = jnp.where(chosen, (block * cap).astype(f32) + rank, f32(-1.0))
        hot = jnp.concatenate(
            [(slot == target[i : i + 1, :]).astype(f32) for i in range(2)], 0
        ).astype(bf16)
        hot_ref[g] = hot
        for at in range(0, width, step):
            part = got_ref[g, :, at : at + step]
            got = jnp.dot(hot, part, preferred_element_type=f32).astype(bf16)
            for i in range(2):
                x_ref[i, g * grows : (g + 1) * grows, at : at + step] = got[
                    i * grows : (i + 1) * grows
                ]
        got = jnp.dot(hot, tail, preferred_element_type=f32)
        for i in range(2):
            sel = pick[i : i + 1, :].astype(f32)
            row_gates[i].append(
                jnp.sum(got[i * grows : (i + 1) * grows] * sel, axis=1, keepdims=True)
            )
    loads[0][2].start()
    for i in range(2):
        x = x_ref[i]
        loads[i][0].wait()
        loads[i][1].wait()
        if i == 0:
            loads[1][0].start()
            loads[1][1].start()
        for at in range(0, hidden, step):
            cols = slice(at, at + step)
            gate = jnp.dot(x, wide_ref[i, 0, :, cols], preferred_element_type=f32)
            upv = jnp.dot(x, wide_ref[i, 1, :, cols], preferred_element_type=f32)
            act_ref[:, cols] = (gate / (1.0 + jnp.exp(-gate)) * upv).astype(bf16)
        loads[i][2].wait()
        if i == 0:
            loads[1][2].start()
        row_gate = jnp.concatenate(row_gates[i], 0)
        for at in range(0, width, step):
            cols = slice(at, at + step)
            y = jnp.dot(act_ref[...], down_ref[i, :, cols], preferred_element_type=f32)
            x_ref[i, :, cols] = (y * row_gate).astype(bf16)
    first = 0
    for g, (rows, moves) in enumerate(layouts):
        for at in range(0, width, step):
            cols = slice(at, at + step)
            y = jnp.concatenate(
                [x_ref[i, g * grows : (g + 1) * grows, cols] for i in range(2)], 0
            )
            total = lax.dot_general(hot_ref[g], y, TN, preferred_element_type=f32).astype(bf16)
            for row, count, out, to in moves:
                outs[first + out][to : to + count, cols] = total[row : row + count]
        first += len(rows)


def expert_terms(blocks, modes, sides, mine, weights, cap, nexp):
    planes, per_group = len(blocks), len(blocks[0])
    tokens, wide = blocks[0][0].shape
    _, width, hidden = weights[0].shape
    grows = per_group * cap
    rows = planes * grows
    layouts = [plane_layout(mode, sides, tokens) for mode in modes]
    out_shape = [jax.ShapeDtypeStruct((n, width), bf16) for ns, _ in layouts for n in ns]
    outs = pl.pallas_call(
        functools.partial(expert_kernel, layouts, per_group, tokens, cap, nexp),
        out_shape=out_shape,
        in_specs=[SMEM] + [ANY] * (planes * per_group + len(weights)),
        out_specs=[VMEM] * len(out_shape),
        scratch_shapes=[
            pltpu.VMEM((planes, per_group * tokens, wide), bf16),
            pltpu.VMEM((2, rows, width), bf16),
            pltpu.VMEM((rows, hidden), bf16),
            pltpu.VMEM((planes, 2 * grows, per_group * tokens), bf16),
            pltpu.VMEM((2, 2, width, hidden), bf16),
            pltpu.VMEM((2, hidden, width), bf16),
            pltpu.SemaphoreType.DMA((2, 3)),
            pltpu.SemaphoreType.DMA((planes, per_group)),
        ],
        compiler_params=params(EXPERT_MIB),
        cost_estimate=pl.CostEstimate(
            flops=12 * rows * width * hidden, bytes_accessed=8 * rows * width, transcendentals=0
        ),
        name="experts",
    )(mine, *[block for plane in blocks for block in plane], *weights)
    terms, at = [], 0
    for ns, _ in layouts:
        terms.append(outs[at : at + len(ns)])
        at += len(ns)
    return terms


def add(*terms):
    total = terms[0].astype(f32)
    for term in terms[1:]:
        total = total + term.astype(f32)
    return total


def plane_sum(term, mode, sides):
    if mode == "halves":
        top = plane_sum(term[::2], "x", sides)
        low = plane_sum(term[1::2], "y", sides)
        return jnp.concatenate([top, low], 0)
    keep, send = term
    if mode == "x":
        size = keep.shape[0] // 2
        got = [swap(send[i * 2 * size : (i + 1) * 2 * size], "seq", 2 * i + 2) for i in range(sides - 1)]
        last = swap(add(keep[size:], *[g[size:] for g in got]).astype(bf16), "exp", 1)
        return add(keep[:size], *[g[:size] for g in got], last)
    size = keep.shape[0] // sides
    got = swap(send, "exp", 1)
    last = []
    for kx in range(1, sides):
        at = slice(kx * size, (kx + 1) * size)
        last.append(swap(add(keep[at], got[at]).astype(bf16), "seq", 2 * kx))
    return add(keep[:size], got[:size], *last)


def return_terms(terms, modes, sides):
    sums = [None] * len(terms)
    for kz in reversed(range(len(terms))):
        sums[kz] = plane_sum(terms[kz], modes[kz], sides)
    own = [sums[0]]
    for kz in range(1, len(terms)):
        if kz == 1 or kz % 2 == 0:
            part = sums[kz]
            if kz > 1 and kz + 1 < len(terms):
                part = add(part, swap(sums[kz + 1].astype(bf16), "exp", 2))
            own.append(swap(part.astype(bf16), "exp", 2 * kz))
    return own


def experts_by_chip(rows, width, weights, nexp):
    nseq, nplace = lax.axis_size("seq"), lax.axis_size("exp")
    cap = 3 * rows.shape[0] * TOPK // (2 * nexp)
    planes, sides = nplace // 2, nseq // 2
    me = lax.axis_index("seq") * nplace + lax.axis_index("exp")
    other = (lax.axis_index("seq") ^ 1) * nplace + lax.axis_index("exp")
    mine = jnp.stack([me, other]).astype(jnp.int32)
    columns = [rows]
    for kz in range(1, planes):
        odd = kz > 1 and kz % 2
        columns.append(swap(columns[kz - 1], "exp", 2) if odd else swap(rows, "exp", 2 * kz))
    modes = ["y", "x"] + ["halves"] * (planes - 2)
    terms = []
    for at in range(0, planes, 2):
        even, _ = gather_plane(columns[at], at, sides)
        odd, terms = gather_plane(columns[at + 1], at + 1, sides, terms)
        two = modes[at : at + 2]
        terms = [*terms, *expert_terms([even, odd], two, sides, mine, weights, cap, nexp)]
    return return_terms(terms, modes, sides)


def experts_by_device(rows, width, ids, gate_proj, up_proj, down_proj, nexp):
    tokens = rows.shape[0]
    normed = rows[:, :width]
    gates = rows[:, width : width + nexp].astype(f32) + rows[
        :, width + nexp : width + 2 * nexp
    ].astype(f32)
    gates = jnp.take_along_axis(gates, ids, axis=1)
    capacity = 3 * tokens * TOPK // (2 * nexp)
    flat = ids.reshape(-1)
    member = (flat[:, None] == jnp.arange(nexp, dtype=jnp.int32)[None, :]).astype(jnp.int32)
    rank = jnp.sum((jnp.cumsum(member, axis=0) - 1) * member, axis=1)
    slot = flat * capacity + rank
    place = slot[:, None] == jnp.arange(nexp * capacity, dtype=jnp.int32)[None, :]
    route = jnp.any(place.reshape(tokens, TOPK, nexp * capacity), axis=1).astype(bf16)
    packed = jnp.einsum("ts,td->sd", route, normed, preferred_element_type=f32).astype(bf16)
    outgoing = packed.reshape(nexp, capacity, width)
    taken = lax.all_to_all(outgoing, ("seq", "exp"), split_axis=0, concat_axis=0, tiled=True)
    taken = taken.reshape(-1, width)
    gate = jnp.dot(taken, gate_proj[0], preferred_element_type=f32)
    upv = jnp.dot(taken, up_proj[0], preferred_element_type=f32)
    act = (jax.nn.silu(gate) * upv).astype(bf16)
    result = jnp.dot(act, down_proj[0], preferred_element_type=f32).astype(bf16)
    result = result.reshape(nexp, capacity, width)
    back = lax.all_to_all(result, ("seq", "exp"), split_axis=0, concat_axis=0, tiled=True)
    gathered = back.reshape(nexp * capacity, width)[slot].reshape(tokens, TOPK, width)
    return [jnp.sum(gates[:, :, None] * gathered.astype(f32), axis=1)]


def body(
    queries,
    new_keys,
    new_values,
    cache_keys,
    cache_values,
    cache_len,
    residual_in,
    out_weight,
    norm_gain,
    router_weight,
    expert_ids,
    gate_proj,
    up_proj,
    down_proj,
):
    nseq, nplace = lax.axis_size("seq"), lax.axis_size("exp")
    tokens, width = residual_in.shape[1:]
    nexp = router_weight.shape[1]
    by_chip = nseq * nplace <= 32
    me = lax.axis_index("seq").astype(jnp.int32).reshape(1)
    weights = [gate_proj, up_proj, down_proj]
    parts, pairs = project_attention(
        me,
        cache_len,
        queries[0],
        new_keys[0],
        new_values[0],
        cache_keys[0],
        cache_values[0],
        out_weight,
        weights if by_chip else [],
    )
    mixed, rows = norm_rows(
        residual_in[0], parts, norm_gain, router_weight, expert_ids[0]
    )
    if by_chip:
        rows, pairs = lax.optimization_barrier((rows, pairs))
        terms = experts_by_chip(rows, width, pairs, nexp)
    else:
        terms = experts_by_device(rows, width, expert_ids[0], *weights, nexp)
    return add(mixed, *terms).astype(bf16).reshape(1, tokens, width)


def solution(mesh):
    in_specs = (
        P("exp", "seq", None),
        P("exp", "seq", None),
        P("exp", "seq", None),
        P("exp", "seq", None),
        P("exp", "seq", None),
        P("exp"),
        P("exp", "seq", None),
        P("seq", None),
        P(),
        P(),
        P("exp", "seq", None),
        P(("seq", "exp"), None, None),
        P(("seq", "exp"), None, None),
        P(("seq", "exp"), None, None),
    )
    out_specs = P("exp", "seq", None)
    return jax.shard_map(body, mesh=mesh, in_specs=in_specs, out_specs=out_specs, check_vma=False)
```

```python
import functools
import math

import jax
import jax.numpy as jnp
from jax import lax
from jax.experimental import pallas as pl
from jax.experimental.pallas import tpu as pltpu
from jax.sharding import PartitionSpec as P

QH = 32
KVH = 4
HD = 128
TOPK = 8
MASKED = -1e30
EXPERT_MIB = 46
CLOSE = 0
CALL = 4
NEAR_MIB = 14
FAR_MIB = 14
NORM_MIB = 16
EXP2_SCALE = math.log2(math.e) / math.sqrt(HD)
NT = (((1,), (1,)), ((), ()))
TN = (((0,), (0,)), ((), ()))
VMEM = pl.BlockSpec(memory_space=pltpu.VMEM)
SMEM = pl.BlockSpec(memory_space=pltpu.SMEM)
ANY = pl.BlockSpec(memory_space=pl.ANY)
f32 = jnp.float32
bf16 = jnp.bfloat16


def swap(rows, axis, bits):
    return lax.ppermute(rows, axis, [(i, i ^ bits) for i in range(lax.axis_size(axis))])


def params(mib):
    return pltpu.CompilerParams(vmem_limit_bytes=mib << 20)


def pack_kernel(nseq, me_ref, q_ref, nk_ref, nv_ref, ck_ref, cv_ref, *refs):
    heads, caches, sem = refs[:nseq], refs[nseq : 2 * nseq], refs[-1]
    qcols = QH // nseq * HD
    copies = []
    for k in range(nseq):
        dest = me_ref[0] ^ k
        qat = pl.ds(pl.multiple_of(dest * qcols, HD), qcols)
        kvat = pl.ds(pl.multiple_of(dest * KVH // nseq * HD, HD), HD)
        pairs = (
            (q_ref.at[:, qat], heads[k].at[:, :qcols]),
            (nk_ref.at[:, kvat], heads[k].at[:, qcols : qcols + HD]),
            (nv_ref.at[:, kvat], heads[k].at[:, qcols + HD :]),
            (ck_ref.at[:, kvat], caches[k].at[:, :HD]),
            (cv_ref.at[:, kvat], caches[k].at[:, HD:]),
        )
        copies += [pltpu.make_async_copy(a, b, sem.at[k, i]) for i, (a, b) in enumerate(pairs)]
    for copy in copies:
        copy.start()
    for copy in copies:
        copy.wait()


def pack(me, arrays, nseq):
    tokens, slots = arrays[0].shape[0], arrays[-1].shape[0]
    shapes = [jax.ShapeDtypeStruct((tokens, (QH // nseq + 2) * HD), bf16)] * nseq
    shapes += [jax.ShapeDtypeStruct((slots, 2 * HD), bf16)] * nseq
    outs = pl.pallas_call(
        functools.partial(pack_kernel, nseq),
        out_shape=shapes,
        in_specs=[SMEM] + [ANY] * len(arrays),
        out_specs=[VMEM] * len(shapes),
        scratch_shapes=[pltpu.SemaphoreType.DMA((nseq, len(arrays)))],
        compiler_params=params(61),
        name="pack_heads",
    )(me, *arrays)
    return outs[:nseq], outs[nseq:]


def head_rows(heads, start):
    return jnp.concatenate([ref[:, start : start + HD] for ref in heads], 0)


def slot_bias(me, length, ks, slots):
    parts = []
    for k in ks:
        pos = (me ^ k) * slots + lax.broadcasted_iota(jnp.int32, (1, slots), 1)
        parts.append(jnp.where(pos < length, f32(0.0), f32(MASKED)))
    return jnp.concatenate(parts, 1)


def near_kernel(nseq, me_ref, len_ref, *refs):
    heads, caches = refs[:nseq], refs[nseq : nseq + 2]
    peak_ref, sum_ref, acc_ref = refs[nseq + 3 :]
    group = QH // nseq
    qcols = group * HD
    me = me_ref[0]
    slots, tokens = caches[0].shape[0], heads[0].shape[0]
    qtok = nseq * tokens
    bias = slot_bias(me, len_ref[0], (0, 1), slots)
    keys = jnp.concatenate([ref[:, :HD] for ref in caches], 0)
    vals = jnp.concatenate([ref[:, HD:] for ref in caches], 0)
    new_keys, new_vals = head_rows(heads, qcols), head_rows(heads, qcols + HD)
    row = lax.broadcasted_iota(jnp.int32, (qtok, qtok), 0)
    col = lax.broadcasted_iota(jnp.int32, (qtok, qtok), 1)
    qpos = (me ^ (row // tokens)) * tokens + row % tokens
    kpos = (me ^ (col // tokens)) * tokens + col % tokens
    new_bias = jnp.where(kpos <= qpos, f32(0.0), f32(MASKED))
    for g in range(group):
        q = head_rows(heads, g * HD)
        s = lax.dot_general(q, keys, NT, preferred_element_type=f32) + bias
        t = lax.dot_general(q, new_keys, NT, preferred_element_type=f32) + new_bias
        peak = jnp.maximum(jnp.max(s, axis=1, keepdims=True), jnp.max(t, axis=1, keepdims=True))
        p = jnp.exp2((s - peak) * f32(EXP2_SCALE))
        r = jnp.exp2((t - peak) * f32(EXP2_SCALE))
        peak_ref[:, g : g + 1] = peak
        sum_ref[:, g : g + 1] = jnp.sum(p, axis=1, keepdims=True) + jnp.sum(r, axis=1, keepdims=True)
        acc = jnp.dot(p.astype(bf16), vals, preferred_element_type=f32)
        acc += jnp.dot(r.astype(bf16), new_vals, preferred_element_type=f32)
        acc_ref[:, g * HD : (g + 1) * HD] = acc


def far_kernel(nseq, me_ref, len_ref, *refs):
    heads, caches = refs[:nseq], refs[nseq : 2 * nseq - 2]
    peak_ref, sum_ref, acc_ref, w_ref = refs[2 * nseq - 2 : 2 * nseq + 2]
    outs = refs[2 * nseq + 2 : -1]
    attn_ref = refs[-1]
    group = QH // nseq
    slots, tokens = caches[0].shape[0], heads[0].shape[0]
    bias = slot_bias(me_ref[0], len_ref[0], range(2, nseq), slots)
    keys = jnp.concatenate([ref[:, :HD] for ref in caches], 0)
    vals = jnp.concatenate([ref[:, HD:] for ref in caches], 0)
    for g in range(group):
        at = slice(g * HD, (g + 1) * HD)
        q = head_rows(heads, g * HD)
        s = lax.dot_general(q, keys, NT, preferred_element_type=f32) + bias
        old = peak_ref[:, g : g + 1]
        peak = jnp.maximum(jnp.max(s, axis=1, keepdims=True), old)
        fade = jnp.exp2((old - peak) * f32(EXP2_SCALE))
        p = jnp.exp2((s - peak) * f32(EXP2_SCALE))
        total = sum_ref[:, g : g + 1] * fade + jnp.sum(p, axis=1, keepdims=True)
        acc = acc_ref[:, at] * fade + jnp.dot(p.astype(bf16), vals, preferred_element_type=f32)
        attn_ref[:, at] = (acc / total).astype(bf16)
    send, near, far = outs
    places = []
    for k in range(nseq):
        if k % 2:
            places.append((send, k // 2 * tokens))
        else:
            places.append((far, (k // 2 - 1) * tokens) if k else (near, 0))
    step = 512
    for at in range(0, w_ref.shape[1], step):
        cols = slice(at, at + step)
        total = jnp.dot(attn_ref[...], w_ref[:, cols], preferred_element_type=f32)
        for k, (out, row) in enumerate(places):
            out[row : row + tokens, cols] = total[k * tokens : (k + 1) * tokens]


def project_attention(
    me, length, queries, new_keys, new_values, cache_keys, cache_values, out_weight, weights
):
    nseq = lax.axis_size("seq")
    tokens = queries.shape[0]
    width = out_weight.shape[1]
    group = QH // nseq
    qtok = nseq * tokens
    heads, caches = pack(me, (queries, new_keys, new_values, cache_keys, cache_values), nseq)
    order = sorted(range(1, nseq), reverse=True)
    heads = {0: heads[0]} | {k: swap(heads[k], "seq", k) for k in order}
    others = [swap(w, "seq", 1) for w in weights[:2]]
    caches = {0: caches[0], 1: swap(caches[1], "seq", 1)} | dict(enumerate(caches[2:], 2))
    far_heads = [heads[k] for k in range(2, nseq)]
    far_caches = [caches[k] for k in range(2, nseq)]
    far_heads, far_caches, others = lax.optimization_barrier((far_heads, far_caches, others))
    for k in range(2, nseq):
        heads[k], caches[k] = far_heads[k - 2], swap(far_caches[k - 2], "seq", k)
    heads = [heads[k] for k in range(nseq)]
    caches = [caches[k] for k in range(nseq)]
    state = pl.pallas_call(
        functools.partial(near_kernel, nseq),
        out_shape=[
            jax.ShapeDtypeStruct((qtok, HD), f32),
            jax.ShapeDtypeStruct((qtok, HD), f32),
            jax.ShapeDtypeStruct((qtok, group * HD), f32),
        ],
        in_specs=[SMEM] * 2 + [VMEM] * (nseq + 3),
        out_specs=[VMEM] * 3,
        compiler_params=params(NEAR_MIB),
        name="attend_near",
    )(me, length, *heads, *caches[:2], out_weight)
    half = nseq // 2 * tokens
    parts = pl.pallas_call(
        functools.partial(far_kernel, nseq),
        out_shape=[
            jax.ShapeDtypeStruct((half, width), f32),
            jax.ShapeDtypeStruct((tokens, width), f32),
            jax.ShapeDtypeStruct((half - tokens, width), f32),
        ],
        in_specs=[SMEM] * 2 + [VMEM] * (2 * nseq + 2),
        out_specs=[VMEM] * 3,
        scratch_shapes=[pltpu.VMEM((qtok, group * HD), bf16)],
        compiler_params=params(FAR_MIB),
        name="attend_far",
    )(me, length, *heads, *caches[2:], *state, out_weight)
    send, near, far = parts
    got = swap(send, "seq", 1)
    got, rest = lax.optimization_barrier((got, weights[2:]))
    others += [swap(w, "seq", 1) for w in rest]
    terms = [near, got[:tokens]]
    for at in range(tokens, half, tokens):
        both = far[at - tokens : at] + got[at : at + tokens]
        terms.append(swap(both.astype(bf16), "seq", 2 * at // tokens))
    return terms, [*weights, *others]


def norm_kernel(nterms, res_ref, *refs):
    gain_ref, router_ref, ids_ref, mixed_ref, rows_ref = refs[nterms:]
    tokens, width = res_ref.shape
    mixed = res_ref[...].astype(f32)
    for ref in refs[:nterms]:
        mixed += ref[...].astype(f32)
    mixed_ref[...] = mixed
    meansq = jnp.mean(mixed * mixed, axis=1, keepdims=True)
    normed = (mixed / jnp.sqrt(meansq + 1e-06) * gain_ref[...]).astype(bf16)
    rows_ref[:, :width] = normed
    logits = lax.dot_general(router_ref[...], normed, NT, preferred_element_type=f32)
    nexp = logits.shape[0]
    expert = lax.broadcasted_iota(jnp.int32, (nexp, tokens), 0)
    chosen = expert == ids_ref[0:1, :]
    for k in range(1, ids_ref.shape[0]):
        chosen = jnp.logical_or(chosen, expert == ids_ref[k : k + 1, :])
    expo = jnp.where(chosen, jnp.exp(logits), f32(0.0))
    gates = expo / jnp.sum(expo, axis=0, keepdims=True)
    high = gates.astype(bf16)
    low = (gates - high.astype(f32)).astype(bf16)
    extra = rows_ref.shape[1] - width
    row = lax.broadcasted_iota(jnp.int32, (nexp, extra), 0)
    col = lax.broadcasted_iota(jnp.int32, (nexp, extra), 1)
    spread = lax.dot_general(high, (col == row).astype(bf16), TN, preferred_element_type=f32)
    spread += lax.dot_general(low, (col == row + nexp).astype(bf16), TN, preferred_element_type=f32)
    rows_ref[:, width:] = spread.astype(bf16)


def norm_rows(residual, terms, gain, router, ids):
    tokens, width = residual.shape
    extra = -(-2 * router.shape[1] // 128) * 128
    return pl.pallas_call(
        functools.partial(norm_kernel, len(terms)),
        out_shape=[
            jax.ShapeDtypeStruct((tokens, width), f32),
            jax.ShapeDtypeStruct((tokens, width + extra), bf16),
        ],
        in_specs=[VMEM] * (4 + len(terms)),
        out_specs=[VMEM] * 2,
        compiler_params=params(NORM_MIB),
        name="norm_and_route",
    )(residual, *terms, gain.reshape(1, width), router.T, ids.T)


def gather_rows(rows, weights, planes, sides):
    columns = [rows]
    for kz in range(1, planes):
        odd = kz > 1 and kz % 2
        columns.append(swap(columns[kz - 1], "exp", 2) if odd else swap(rows, "exp", 2 * kz))
        if kz == CLOSE:
            columns[kz], weights = lax.optimization_barrier((columns[kz], weights))
    blocks = []
    for kz, col in enumerate(columns):
        right = [swap(col, "seq", 2 * kx) for kx in range(1, sides)]
        up = swap(col, "exp", 1)
        if kz % 2:
            over = [swap(block, "exp", 2) for block in blocks[-1][sides + 1 :]]
        elif kz % 4:
            over = [swap(block, "exp", 1) for block in right]
        else:
            over = [swap(up, "seq", 2 * kx) for kx in range(1, sides)]
        blocks.append([col, *right, up, *over])
    return blocks, weights


def plane_layout(odd, sides, tokens):
    half = tokens // 2
    moves = []
    if odd:
        rows = [tokens, (sides - 1) * tokens, tokens, (sides - 1) * tokens]
        for ky in range(2):
            for kx in range(sides):
                to = (2 * ky + (kx > 0), max(kx - 1, 0) * tokens)
                moves.append(((ky * sides + kx) * tokens, tokens, *to))
        return rows, moves
    rows = [2 * half, sides * half, (sides - 1) * half, half, (sides - 1) * tokens]
    for ky in range(2):
        for kx in range(sides):
            row = (ky * sides + kx) * tokens
            if ky and kx:
                moves.append((row, tokens, 4, (kx - 1) * tokens))
                continue
            top = (2, (kx - 1) * half) if kx else (0, ky * half)
            low = (3, 0) if ky else (1, kx * half)
            moves.append((row, half, *top))
            moves.append((row + half, half, *low))
    return rows, moves


def expert_kernel(layouts, per_group, tokens, cap, nexp, mine_ref, *refs):
    planes = len(layouts)
    pieces = planes * per_group
    blocks = refs[:pieces]
    weights = (refs[pieces : pieces + 3], refs[pieces + 3 : pieces + 6])
    nouts = sum(len(rows) for rows, _ in layouts)
    outs = refs[pieces + 6 : pieces + 6 + nouts]
    got_ref, x_ref, act_ref, hot_ref, wide_ref, down_ref, sem, got_sem = refs[pieces + 6 + nouts :]
    copies = [
        pltpu.make_async_copy(
            blocks[g * per_group + i],
            got_ref.at[g, i * tokens : (i + 1) * tokens],
            got_sem.at[g, i],
        )
        for g in range(planes)
        for i in range(per_group)
    ]
    for copy in copies:
        copy.start()
    loads = [
        [
            pltpu.make_async_copy(ws[0].at[0], wide_ref.at[i, 0], sem.at[i, 0]),
            pltpu.make_async_copy(ws[1].at[0], wide_ref.at[i, 1], sem.at[i, 1]),
            pltpu.make_async_copy(ws[2].at[0], down_ref.at[i], sem.at[i, 2]),
        ]
        for i, ws in enumerate(weights)
    ]
    loads[0][0].start()
    loads[0][1].start()
    width = x_ref.shape[2]
    hidden = act_ref.shape[1]
    ext = got_ref.shape[2] - width
    gtok = per_group * tokens
    grows = per_group * cap
    step = 256
    ecol = lax.broadcasted_iota(jnp.int32, (8, ext), 1)
    erow = lax.broadcasted_iota(jnp.int32, (8, ext), 0)
    want = jnp.where(erow == 0, mine_ref[0], jnp.where(erow == 1, mine_ref[1], -ext))
    pick = jnp.logical_or(ecol == want, ecol == want + nexp).astype(bf16)
    trow = lax.broadcasted_iota(jnp.int32, (gtok, gtok), 0)
    tcol = lax.broadcasted_iota(jnp.int32, (gtok, gtok), 1)
    before = jnp.logical_and(trow < tcol, trow // tokens == tcol // tokens).astype(bf16)
    block = lax.broadcasted_iota(jnp.int32, (8, gtok), 1) // tokens
    slot = lax.broadcasted_iota(jnp.int32, (grows, gtok), 0).astype(f32)
    row_gates = [[], []]
    for g in range(planes):
        for copy in copies[g * per_group : (g + 1) * per_group]:
            copy.wait()
        tail = got_ref[g, :, width:]
        gates = lax.dot_general(pick, tail, NT, preferred_element_type=f32)
        chosen = gates > 0.0
        rank = jnp.dot(chosen.astype(bf16), before, preferred_element_type=f32)
        target = jnp.where(chosen, (block * cap).astype(f32) + rank, f32(-1.0))
        hot = jnp.concatenate(
            [(slot == target[i : i + 1, :]).astype(f32) for i in range(2)], 0
        ).astype(bf16)
        hot_ref[g] = hot
        for at in range(0, width, step):
            part = got_ref[g, :, at : at + step]
            got = jnp.dot(hot, part, preferred_element_type=f32).astype(bf16)
            for i in range(2):
                x_ref[i, g * grows : (g + 1) * grows, at : at + step] = got[
                    i * grows : (i + 1) * grows
                ]
        got = jnp.dot(hot, tail, preferred_element_type=f32)
        for i in range(2):
            sel = pick[i : i + 1, :].astype(f32)
            row_gates[i].append(
                jnp.sum(got[i * grows : (i + 1) * grows] * sel, axis=1, keepdims=True)
            )
    loads[0][2].start()
    for i in range(2):
        x = x_ref[i]
        loads[i][0].wait()
        loads[i][1].wait()
        if i == 0:
            loads[1][0].start()
            loads[1][1].start()
        for at in range(0, hidden, step):
            cols = slice(at, at + step)
            gate = jnp.dot(x, wide_ref[i, 0, :, cols], preferred_element_type=f32)
            upv = jnp.dot(x, wide_ref[i, 1, :, cols], preferred_element_type=f32)
            act_ref[:, cols] = (gate / (1.0 + jnp.exp(-gate)) * upv).astype(bf16)
        loads[i][2].wait()
        if i == 0:
            loads[1][2].start()
        row_gate = jnp.concatenate(row_gates[i], 0)
        for at in range(0, width, step):
            cols = slice(at, at + step)
            y = jnp.dot(act_ref[...], down_ref[i, :, cols], preferred_element_type=f32)
            x_ref[i, :, cols] = (y * row_gate).astype(bf16)
    first = 0
    for g, (rows, moves) in enumerate(layouts):
        for at in range(0, width, step):
            cols = slice(at, at + step)
            y = jnp.concatenate(
                [x_ref[i, g * grows : (g + 1) * grows, cols] for i in range(2)], 0
            )
            total = lax.dot_general(hot_ref[g], y, TN, preferred_element_type=f32).astype(bf16)
            for row, count, out, to in moves:
                outs[first + out][to : to + count, cols] = total[row : row + count]
        first += len(rows)


def expert_terms(blocks, sides, mine, weights, cap, nexp):
    planes, per_group = len(blocks), len(blocks[0])
    tokens, wide = blocks[0][0].shape
    _, width, hidden = weights[0].shape
    grows = per_group * cap
    rows = planes * grows
    layouts = [plane_layout(g % 2, sides, tokens) for g in range(planes)]
    out_shape = [jax.ShapeDtypeStruct((n, width), bf16) for ns, _ in layouts for n in ns]
    outs = pl.pallas_call(
        functools.partial(expert_kernel, layouts, per_group, tokens, cap, nexp),
        out_shape=out_shape,
        in_specs=[SMEM] + [ANY] * (planes * per_group + len(weights)),
        out_specs=[VMEM] * len(out_shape),
        scratch_shapes=[
            pltpu.VMEM((planes, per_group * tokens, wide), bf16),
            pltpu.VMEM((2, rows, width), bf16),
            pltpu.VMEM((rows, hidden), bf16),
            pltpu.VMEM((planes, 2 * grows, per_group * tokens), bf16),
            pltpu.VMEM((2, 2, width, hidden), bf16),
            pltpu.VMEM((2, hidden, width), bf16),
            pltpu.SemaphoreType.DMA((2, 3)),
            pltpu.SemaphoreType.DMA((planes, per_group)),
        ],
        compiler_params=params(EXPERT_MIB),
        cost_estimate=pl.CostEstimate(
            flops=12 * rows * width * hidden, bytes_accessed=8 * rows * width, transcendentals=0
        ),
        name="experts",
    )(mine, *[block for plane in blocks for block in plane], *weights)
    terms, at = [], 0
    for ns, _ in layouts:
        terms.append(outs[at : at + len(ns)])
        at += len(ns)
    return terms


def add(*terms):
    total = terms[0].astype(f32)
    for term in terms[1:]:
        total = total + term.astype(f32)
    return total


def even_sum(term, over, sides):
    keep_a, keep_b, send_a, send_b, own_over = term
    half = send_b.shape[0]
    over = [
        add(own_over[i * 2 * half : (i + 1) * 2 * half], o).astype(bf16) for i, o in enumerate(over)
    ]
    got_a = [
        swap(jnp.concatenate([send_a[i * half : (i + 1) * half], o[:half]], 0), "seq", 2 * i + 2)
        for i, o in enumerate(over)
    ]
    got_b = swap(jnp.concatenate([send_b, *[o[half:] for o in over]], 0), "exp", 1)
    next_a = swap(add(keep_a[half:], *[g[half:] for g in got_a]).astype(bf16), "exp", 1)
    next_b = []
    for kx in range(1, sides):
        at = slice(kx * half, (kx + 1) * half)
        next_b.append(swap(add(keep_b[at], got_b[at]).astype(bf16), "seq", 2 * kx))
    top = add(keep_a[:half], *[g[:half] for g in got_a], next_a)
    low = add(keep_b[:half], got_b[:half], *next_b)
    return jnp.concatenate([top, low], 0)


def pair_sum(even, odd, sides):
    keep, right, up, over = odd
    size = keep.shape[0]
    parts = [slice(i * size, (i + 1) * size) for i in range(sides - 1)]
    over = [swap(over[at], "exp", 2) for at in parts]
    got = [swap(right[at], "seq", 2 * i + 2) for i, at in enumerate(parts)]
    got.append(swap(up, "exp", 1))
    return even_sum(even, over, sides), add(keep, *got)


def return_terms(terms, sides):
    own = []
    for kz in reversed(range(0, len(terms), 2)):
        even, odd = pair_sum(terms[kz], terms[kz + 1], sides)
        got = swap(odd.astype(bf16), "exp", 2)
        own += [swap(add(even, got).astype(bf16), "exp", 2 * kz)] if kz else [even, got]
    return own


def experts_by_chip(rows, width, weights, nexp):
    nseq, nplace = lax.axis_size("seq"), lax.axis_size("exp")
    cap = 3 * rows.shape[0] * TOPK // (2 * nexp)
    planes, sides = nplace // 2, nseq // 2
    me = lax.axis_index("seq") * nplace + lax.axis_index("exp")
    other = (lax.axis_index("seq") ^ 1) * nplace + lax.axis_index("exp")
    mine = jnp.stack([me, other]).astype(jnp.int32)
    blocks, weights = gather_rows(rows, weights, planes, sides)
    terms = []
    for at in range(0, planes, CALL):
        terms += expert_terms(blocks[at : at + CALL], sides, mine, weights, cap, nexp)
    return return_terms(terms, sides)


def experts_by_device(rows, width, ids, gate_proj, up_proj, down_proj, nexp):
    tokens = rows.shape[0]
    normed = rows[:, :width]
    gates = rows[:, width : width + nexp].astype(f32) + rows[
        :, width + nexp : width + 2 * nexp
    ].astype(f32)
    gates = jnp.take_along_axis(gates, ids, axis=1)
    capacity = 3 * tokens * TOPK // (2 * nexp)
    flat = ids.reshape(-1)
    member = (flat[:, None] == jnp.arange(nexp, dtype=jnp.int32)[None, :]).astype(jnp.int32)
    rank = jnp.sum((jnp.cumsum(member, axis=0) - 1) * member, axis=1)
    slot = flat * capacity + rank
    place = slot[:, None] == jnp.arange(nexp * capacity, dtype=jnp.int32)[None, :]
    route = jnp.any(place.reshape(tokens, TOPK, nexp * capacity), axis=1).astype(bf16)
    packed = jnp.einsum("ts,td->sd", route, normed, preferred_element_type=f32).astype(bf16)
    outgoing = packed.reshape(nexp, capacity, width)
    taken = lax.all_to_all(outgoing, ("seq", "exp"), split_axis=0, concat_axis=0, tiled=True)
    taken = taken.reshape(-1, width)
    gate = jnp.dot(taken, gate_proj[0], preferred_element_type=f32)
    upv = jnp.dot(taken, up_proj[0], preferred_element_type=f32)
    act = (jax.nn.silu(gate) * upv).astype(bf16)
    result = jnp.dot(act, down_proj[0], preferred_element_type=f32).astype(bf16)
    result = result.reshape(nexp, capacity, width)
    back = lax.all_to_all(result, ("seq", "exp"), split_axis=0, concat_axis=0, tiled=True)
    gathered = back.reshape(nexp * capacity, width)[slot].reshape(tokens, TOPK, width)
    return [jnp.sum(gates[:, :, None] * gathered.astype(f32), axis=1)]


def body(
    queries,
    new_keys,
    new_values,
    cache_keys,
    cache_values,
    cache_len,
    residual_in,
    out_weight,
    norm_gain,
    router_weight,
    expert_ids,
    gate_proj,
    up_proj,
    down_proj,
):
    nseq, nplace = lax.axis_size("seq"), lax.axis_size("exp")
    tokens, width = residual_in.shape[1:]
    nexp = router_weight.shape[1]
    by_chip = nseq * nplace <= 32
    me = lax.axis_index("seq").astype(jnp.int32).reshape(1)
    weights = [gate_proj, up_proj, down_proj]
    parts, pairs = project_attention(
        me,
        cache_len,
        queries[0],
        new_keys[0],
        new_values[0],
        cache_keys[0],
        cache_values[0],
        out_weight,
        weights if by_chip else [],
    )
    mixed, rows = norm_rows(
        residual_in[0], parts, norm_gain, router_weight, expert_ids[0]
    )
    if by_chip:
        rows, pairs = lax.optimization_barrier((rows, pairs))
        terms = experts_by_chip(rows, width, pairs, nexp)
    else:
        terms = experts_by_device(rows, width, expert_ids[0], *weights, nexp)
    return add(mixed, *terms).astype(bf16).reshape(1, tokens, width)


def solution(mesh):
    in_specs = (
        P("exp", "seq", None),
        P("exp", "seq", None),
        P("exp", "seq", None),
        P("exp", "seq", None),
        P("exp", "seq", None),
        P("exp"),
        P("exp", "seq", None),
        P("seq", None),
        P(),
        P(),
        P("exp", "seq", None),
        P(("seq", "exp"), None, None),
        P(("seq", "exp"), None, None),
        P(("seq", "exp"), None, None),
    )
    out_specs = P("exp", "seq", None)
    return jax.shard_map(body, mesh=mesh, in_specs=in_specs, out_specs=out_specs, check_vma=False)
```

```python
import functools
import math

import jax
import jax.numpy as jnp
from jax import lax
from jax.experimental import pallas as pl
from jax.experimental.pallas import tpu as pltpu
from jax.sharding import PartitionSpec as P

QH = 32
KVH = 4
HD = 128
TOPK = 8
MASKED = -1e30
EXPERT_MIB = 46
GATHER = ("c2", "c1", "y0", "x0", "x2", "c3", "y2", "y1", "d0", "d2", "x1", "y3", "x3", "d1", "d3")
TAKE = tuple(range(16))
CALL = 4
HOLD = 3
GATE = 0
WAIT = 0
DIRECT = ()
NEAR_MIB = 14
FAR_MIB = 14
NORM_MIB = 16
EXP2_SCALE = math.log2(math.e) / math.sqrt(HD)
NT = (((1,), (1,)), ((), ()))
TN = (((0,), (0,)), ((), ()))
VMEM = pl.BlockSpec(memory_space=pltpu.VMEM)
SMEM = pl.BlockSpec(memory_space=pltpu.SMEM)
ANY = pl.BlockSpec(memory_space=pl.ANY)
f32 = jnp.float32
bf16 = jnp.bfloat16


def swap(rows, axis, bits):
    return lax.ppermute(rows, axis, [(i, i ^ bits) for i in range(lax.axis_size(axis))])


def swap_both(rows, seq_bits, exp_bits):
    nseq, nplace = lax.axis_size("seq"), lax.axis_size("exp")
    bits = seq_bits * nplace + exp_bits
    return lax.ppermute(rows, ("seq", "exp"), [(i, i ^ bits) for i in range(nseq * nplace)])


def params(mib):
    return pltpu.CompilerParams(vmem_limit_bytes=mib << 20)


def pack_kernel(nseq, widths, me_ref, *refs):
    ins, outs, sem = refs[: len(widths)], refs[len(widths) : -1], refs[-1]
    copies = []
    for k in range(nseq):
        dest, to = me_ref[0] ^ k, 0
        for i, cols in enumerate(widths):
            start = dest * cols if ins[i].shape[1] == cols * nseq else dest * KVH // nseq * HD
            start = pl.ds(pl.multiple_of(start, HD), cols)
            pair = ins[i].at[:, start], outs[k].at[:, to : to + cols]
            copies.append(pltpu.make_async_copy(*pair, sem.at[k, i]))
            to += cols
    for copy in copies:
        copy.start()
    for copy in copies:
        copy.wait()


def pack(me, arrays, widths, nseq):
    shape = jax.ShapeDtypeStruct((arrays[0].shape[0], sum(widths)), bf16)
    return pl.pallas_call(
        functools.partial(pack_kernel, nseq, widths),
        out_shape=[shape] * nseq,
        in_specs=[SMEM] + [ANY] * len(arrays),
        out_specs=[VMEM] * nseq,
        scratch_shapes=[pltpu.SemaphoreType.DMA((nseq, len(arrays)))],
        compiler_params=params(61),
        name="pack_heads",
    )(me, *arrays)


def head_rows(heads, start):
    return jnp.concatenate([ref[:, start : start + HD] for ref in heads], 0)


def slot_bias(me, length, ks, slots):
    parts = []
    for k in ks:
        pos = (me ^ k) * slots + lax.broadcasted_iota(jnp.int32, (1, slots), 1)
        parts.append(jnp.where(pos < length, f32(0.0), f32(MASKED)))
    return jnp.concatenate(parts, 1)


def near_kernel(nseq, me_ref, len_ref, *refs):
    heads, caches = refs[:nseq], refs[nseq : nseq + 2]
    peak_ref, sum_ref, acc_ref = refs[nseq + 3 :]
    group = QH // nseq
    qcols = group * HD
    me = me_ref[0]
    slots, tokens = caches[0].shape[0], heads[0].shape[0]
    qtok = nseq * tokens
    bias = slot_bias(me, len_ref[0], (0, 1), slots)
    keys = jnp.concatenate([ref[:, :HD] for ref in caches], 0)
    vals = jnp.concatenate([ref[:, HD:] for ref in caches], 0)
    new_keys, new_vals = head_rows(heads, qcols), head_rows(heads, qcols + HD)
    row = lax.broadcasted_iota(jnp.int32, (qtok, qtok), 0)
    col = lax.broadcasted_iota(jnp.int32, (qtok, qtok), 1)
    qpos = (me ^ (row // tokens)) * tokens + row % tokens
    kpos = (me ^ (col // tokens)) * tokens + col % tokens
    new_bias = jnp.where(kpos <= qpos, f32(0.0), f32(MASKED))
    for g in range(group):
        q = head_rows(heads, g * HD)
        s = lax.dot_general(q, keys, NT, preferred_element_type=f32) + bias
        t = lax.dot_general(q, new_keys, NT, preferred_element_type=f32) + new_bias
        peak = jnp.maximum(jnp.max(s, axis=1, keepdims=True), jnp.max(t, axis=1, keepdims=True))
        p = jnp.exp2((s - peak) * f32(EXP2_SCALE))
        r = jnp.exp2((t - peak) * f32(EXP2_SCALE))
        peak_ref[:, g : g + 1] = peak
        sum_ref[:, g : g + 1] = jnp.sum(p, axis=1, keepdims=True) + jnp.sum(r, axis=1, keepdims=True)
        acc = jnp.dot(p.astype(bf16), vals, preferred_element_type=f32)
        acc += jnp.dot(r.astype(bf16), new_vals, preferred_element_type=f32)
        acc_ref[:, g * HD : (g + 1) * HD] = acc


def far_kernel(nseq, ks, me_ref, len_ref, *refs):
    heads, caches = refs[: len(ks)], refs[len(ks) : len(ks) + nseq - 2]
    peak_ref, sum_ref, acc_ref, w_ref, even_ref, odd_ref, attn_ref = refs[len(ks) + nseq - 2 :]
    group = QH // nseq
    slots, tokens = caches[0].shape[0], heads[0].shape[0]
    mine = slice(ks[0] * tokens, (ks[-1] + 1) * tokens)
    bias = slot_bias(me_ref[0], len_ref[0], range(2, nseq), slots)
    keys = jnp.concatenate([ref[:, :HD] for ref in caches], 0)
    vals = jnp.concatenate([ref[:, HD:] for ref in caches], 0)
    for g in range(group):
        at = slice(g * HD, (g + 1) * HD)
        q = head_rows(heads, g * HD)
        s = lax.dot_general(q, keys, NT, preferred_element_type=f32) + bias
        old = peak_ref[mine, g : g + 1]
        peak = jnp.maximum(jnp.max(s, axis=1, keepdims=True), old)
        fade = jnp.exp2((old - peak) * f32(EXP2_SCALE))
        p = jnp.exp2((s - peak) * f32(EXP2_SCALE))
        total = sum_ref[mine, g : g + 1] * fade + jnp.sum(p, axis=1, keepdims=True)
        acc = acc_ref[mine, at] * fade + jnp.dot(p.astype(bf16), vals, preferred_element_type=f32)
        attn_ref[:, at] = (acc / total).astype(bf16)
    step = 512
    for at in range(0, w_ref.shape[1], step):
        cols = slice(at, at + step)
        total = jnp.dot(attn_ref[...], w_ref[:, cols], preferred_element_type=f32)
        for i in range(len(ks)):
            to = slice(i // 2 * tokens, (i // 2 + 1) * tokens)
            out = odd_ref if i % 2 else even_ref
            out[to, cols] = total[i * tokens : (i + 1) * tokens].astype(out.dtype)


def project_attention(
    me, length, queries, new_keys, new_values, cache_keys, cache_values, out_weight, weights
):
    nseq = lax.axis_size("seq")
    tokens = queries.shape[0]
    width = out_weight.shape[1]
    group = QH // nseq
    qtok = nseq * tokens
    heads = pack(me, (queries, new_keys, new_values), (group * HD, HD, HD), nseq)
    order = sorted(range(1, nseq), reverse=True)
    heads = {0: heads[0]} | {k: swap(heads[k], "seq", k) for k in order}
    others = [swap(w, "seq", 1) for w in weights[:2]]
    held = heads[1], cache_keys, cache_values
    heads[1], cache_keys, cache_values = lax.optimization_barrier(held)
    caches = pack(me, (cache_keys, cache_values), (HD, HD), nseq)
    caches = {0: caches[0], 1: swap(caches[1], "seq", 1)} | dict(enumerate(caches[2:], 2))
    for k in range(2, nseq):
        hold = (heads[k], caches[k], others if k == HOLD else [])
        heads[k], cache, held = lax.optimization_barrier(hold)
        others = held or others
        caches[k] = swap(cache, "seq", k)
    heads = [heads[k] for k in range(nseq)]
    caches = [caches[k] for k in range(nseq)]
    state = pl.pallas_call(
        functools.partial(near_kernel, nseq),
        out_shape=[
            jax.ShapeDtypeStruct((qtok, HD), f32),
            jax.ShapeDtypeStruct((qtok, HD), f32),
            jax.ShapeDtypeStruct((qtok, group * HD), f32),
        ],
        in_specs=[SMEM] * 2 + [VMEM] * (nseq + 3),
        out_specs=[VMEM] * 3,
        compiler_params=params(NEAR_MIB),
        name="attend_near",
    )(me, length, *heads, *caches[:2], out_weight)

    def project(ks, state):
        shape = (len(ks) // 2 * tokens, width)
        return pl.pallas_call(
            functools.partial(far_kernel, nseq, ks),
            out_shape=[jax.ShapeDtypeStruct(shape, f32), jax.ShapeDtypeStruct(shape, bf16)],
            in_specs=[SMEM] * 2 + [VMEM] * (len(ks) + nseq + 2),
            out_specs=[VMEM] * 2,
            scratch_shapes=[pltpu.VMEM((len(ks) * tokens, group * HD), bf16)],
            compiler_params=params(FAR_MIB),
            name="attend_far",
        )(me, length, *[heads[k] for k in ks], *caches[2:], *state, out_weight)

    even, odd = project(list(range(nseq)), state)
    got = swap(odd, "seq", 1)
    got, rest = lax.optimization_barrier((got, weights[2:]))
    others += [swap(w, "seq", 1) for w in rest]
    terms = [even[:tokens], got[:tokens]]
    for at in range(tokens, got.shape[0], tokens):
        both = add(even[at : at + tokens], got[at : at + tokens])
        terms.append(swap(both.astype(bf16), "seq", 2 * at // tokens))
    return terms, [*weights, *others]


def norm_kernel(nterms, res_ref, *refs):
    gain_ref, router_ref, ids_ref, mixed_ref, rows_ref = refs[nterms:]
    tokens, width = res_ref.shape
    mixed = res_ref[...].astype(f32)
    for ref in refs[:nterms]:
        mixed += ref[...].astype(f32)
    mixed_ref[...] = mixed
    meansq = jnp.mean(mixed * mixed, axis=1, keepdims=True)
    normed = (mixed / jnp.sqrt(meansq + 1e-06) * gain_ref[...]).astype(bf16)
    rows_ref[:, :width] = normed
    logits = lax.dot_general(router_ref[...], normed, NT, preferred_element_type=f32)
    nexp = logits.shape[0]
    expert = lax.broadcasted_iota(jnp.int32, (nexp, tokens), 0)
    chosen = expert == ids_ref[0:1, :]
    for k in range(1, ids_ref.shape[0]):
        chosen = jnp.logical_or(chosen, expert == ids_ref[k : k + 1, :])
    expo = jnp.where(chosen, jnp.exp(logits), f32(0.0))
    gates = expo / jnp.sum(expo, axis=0, keepdims=True)
    high = gates.astype(bf16)
    low = (gates - high.astype(f32)).astype(bf16)
    extra = rows_ref.shape[1] - width
    row = lax.broadcasted_iota(jnp.int32, (nexp, extra), 0)
    col = lax.broadcasted_iota(jnp.int32, (nexp, extra), 1)
    spread = lax.dot_general(high, (col == row).astype(bf16), TN, preferred_element_type=f32)
    spread += lax.dot_general(low, (col == row + nexp).astype(bf16), TN, preferred_element_type=f32)
    rows_ref[:, width:] = spread.astype(bf16)


def norm_rows(residual, terms, gain, router, ids):
    tokens, width = residual.shape
    extra = -(-2 * router.shape[1] // 128) * 128
    return pl.pallas_call(
        functools.partial(norm_kernel, len(terms)),
        out_shape=[
            jax.ShapeDtypeStruct((tokens, width), f32),
            jax.ShapeDtypeStruct((tokens, width + extra), bf16),
        ],
        in_specs=[VMEM] * (4 + len(terms)),
        out_specs=[VMEM] * 2,
        compiler_params=params(NORM_MIB),
        name="norm_and_route",
    )(residual, *terms, gain.reshape(1, width), router.T, ids.T)


def gather_rows(rows, planes, sides):
    at = {("c", 0): [rows]}
    steps = [(kind, kz) for kz in range(planes) for kind in "cxyd" if (kind, kz) not in at]
    if planes == 4:
        steps = [(step[0], int(step[1])) for step in GATHER]
    for kind, kz in steps:
        if kind == "c":
            near = kz > 1 and kz % 2
            got = [swap(at["c", kz - 1][0], "exp", 2) if near else swap(rows, "exp", 2 * kz)]
        elif kind == "x":
            got = [swap(at["c", kz][0], "seq", 2 * kx) for kx in range(1, sides)]
        elif kind == "y":
            got = [swap(at["c", kz][0], "exp", 1)]
        elif kz % 2:
            got = [swap(block, "exp", 2) for block in at["d", kz - 1]]
        elif kz in DIRECT:
            got = [swap_both(at["c", kz][0], 2 * kx, 1) for kx in range(1, sides)]
        elif kz % 4 == 0:
            got = [swap(at["y", kz][0], "seq", 2 * kx) for kx in range(1, sides)]
        else:
            got = [swap(block, "exp", 1) for block in at["x", kz]]
        at[kind, kz] = got
    return [[block for kind in "cxyd" for block in at[kind, kz]] for kz in range(planes)]


def plane_layout(sides, tokens):
    rows = [tokens, (sides - 1) * tokens, tokens, (sides - 1) * tokens]
    moves = []
    for ky in range(2):
        for kx in range(sides):
            to = (2 * ky + (kx > 0), max(kx - 1, 0) * tokens)
            moves.append(((ky * sides + kx) * tokens, tokens, *to))
    return rows, moves


def expert_kernel(layouts, take, per_group, tokens, cap, nexp, mine_ref, *refs):
    planes = len(layouts)
    pieces = planes * per_group
    blocks = [refs[take.index(i)] for i in range(pieces)]
    weights = (refs[pieces : pieces + 3], refs[pieces + 3 : pieces + 6])
    nouts = sum(len(rows) for rows, _ in layouts)
    outs = refs[pieces + 6 : pieces + 6 + nouts]
    got_ref, x_ref, act_ref, hot_ref, wide_ref, down_ref, sem, got_sem = refs[pieces + 6 + nouts :]
    copies = [
        pltpu.make_async_copy(
            blocks[g * per_group + i],
            got_ref.at[g, i * tokens : (i + 1) * tokens],
            got_sem.at[g, i],
        )
        for g in range(planes)
        for i in range(per_group)
    ]
    for copy in copies:
        copy.start()
    loads = [
        [
            pltpu.make_async_copy(ws[0].at[0], wide_ref.at[i, 0], sem.at[i, 0]),
            pltpu.make_async_copy(ws[1].at[0], wide_ref.at[i, 1], sem.at[i, 1]),
            pltpu.make_async_copy(ws[2].at[0], down_ref.at[i], sem.at[i, 2]),
        ]
        for i, ws in enumerate(weights)
    ]
    loads[0][0].start()
    loads[0][1].start()
    width = x_ref.shape[2]
    hidden = act_ref.shape[1]
    ext = got_ref.shape[2] - width
    gtok = per_group * tokens
    grows = per_group * cap
    step = 256
    ecol = lax.broadcasted_iota(jnp.int32, (8, ext), 1)
    erow = lax.broadcasted_iota(jnp.int32, (8, ext), 0)
    want = jnp.where(erow == 0, mine_ref[0], jnp.where(erow == 1, mine_ref[1], -ext))
    pick = jnp.logical_or(ecol == want, ecol == want + nexp).astype(bf16)
    trow = lax.broadcasted_iota(jnp.int32, (gtok, gtok), 0)
    tcol = lax.broadcasted_iota(jnp.int32, (gtok, gtok), 1)
    before = jnp.logical_and(trow < tcol, trow // tokens == tcol // tokens).astype(bf16)
    block = lax.broadcasted_iota(jnp.int32, (8, gtok), 1) // tokens
    slot = lax.broadcasted_iota(jnp.int32, (grows, gtok), 0).astype(f32)
    row_gates = [[], []]
    for g in range(planes):
        for copy in copies[g * per_group : (g + 1) * per_group]:
            copy.wait()
        tail = got_ref[g, :, width:]
        gates = lax.dot_general(pick, tail, NT, preferred_element_type=f32)
        chosen = gates > 0.0
        rank = jnp.dot(chosen.astype(bf16), before, preferred_element_type=f32)
        target = jnp.where(chosen, (block * cap).astype(f32) + rank, f32(-1.0))
        hot = jnp.concatenate(
            [(slot == target[i : i + 1, :]).astype(f32) for i in range(2)], 0
        ).astype(bf16)
        hot_ref[g] = hot
        for at in range(0, width, step):
            part = got_ref[g, :, at : at + step]
            got = jnp.dot(hot, part, preferred_element_type=f32).astype(bf16)
            for i in range(2):
                x_ref[i, g * grows : (g + 1) * grows, at : at + step] = got[
                    i * grows : (i + 1) * grows
                ]
        got = jnp.dot(hot, tail, preferred_element_type=f32)
        for i in range(2):
            sel = pick[i : i + 1, :].astype(f32)
            row_gates[i].append(
                jnp.sum(got[i * grows : (i + 1) * grows] * sel, axis=1, keepdims=True)
            )
    loads[0][2].start()
    for i in range(2):
        x = x_ref[i]
        loads[i][0].wait()
        loads[i][1].wait()
        if i == 0:
            loads[1][0].start()
            loads[1][1].start()
        for at in range(0, hidden, step):
            cols = slice(at, at + step)
            gate = jnp.dot(x, wide_ref[i, 0, :, cols], preferred_element_type=f32)
            upv = jnp.dot(x, wide_ref[i, 1, :, cols], preferred_element_type=f32)
            act_ref[:, cols] = (gate / (1.0 + jnp.exp(-gate)) * upv).astype(bf16)
        loads[i][2].wait()
        if i == 0:
            loads[1][2].start()
        row_gate = jnp.concatenate(row_gates[i], 0)
        for at in range(0, width, step):
            cols = slice(at, at + step)
            y = jnp.dot(act_ref[...], down_ref[i, :, cols], preferred_element_type=f32)
            x_ref[i, :, cols] = (y * row_gate).astype(bf16)
    first = 0
    for g, (rows, moves) in enumerate(layouts):
        for at in range(0, width, step):
            cols = slice(at, at + step)
            y = jnp.concatenate(
                [x_ref[i, g * grows : (g + 1) * grows, cols] for i in range(2)], 0
            )
            total = lax.dot_general(hot_ref[g], y, TN, preferred_element_type=f32).astype(bf16)
            for row, count, out, to in moves:
                outs[first + out][to : to + count, cols] = total[row : row + count]
        first += len(rows)


def expert_terms(blocks, sides, mine, weights, cap, nexp):
    planes, per_group = len(blocks), len(blocks[0])
    tokens, wide = blocks[0][0].shape
    _, width, hidden = weights[0].shape
    grows = per_group * cap
    rows = planes * grows
    layouts = [plane_layout(sides, tokens)] * planes
    out_shape = [jax.ShapeDtypeStruct((n, width), bf16) for ns, _ in layouts for n in ns]
    flat = [block for plane in blocks for block in plane]
    take = TAKE if len(flat) == len(TAKE) else tuple(range(len(flat)))
    outs = pl.pallas_call(
        functools.partial(expert_kernel, layouts, take, per_group, tokens, cap, nexp),
        out_shape=out_shape,
        in_specs=[SMEM] + [ANY] * (planes * per_group + len(weights)),
        out_specs=[VMEM] * len(out_shape),
        scratch_shapes=[
            pltpu.VMEM((planes, per_group * tokens, wide), bf16),
            pltpu.VMEM((2, rows, width), bf16),
            pltpu.VMEM((rows, hidden), bf16),
            pltpu.VMEM((planes, 2 * grows, per_group * tokens), bf16),
            pltpu.VMEM((2, 2, width, hidden), bf16),
            pltpu.VMEM((2, hidden, width), bf16),
            pltpu.SemaphoreType.DMA((2, 3)),
            pltpu.SemaphoreType.DMA((planes, per_group)),
        ],
        compiler_params=params(EXPERT_MIB),
        cost_estimate=pl.CostEstimate(
            flops=12 * rows * width * hidden, bytes_accessed=8 * rows * width, transcendentals=0
        ),
        name="experts",
    )(mine, *[flat[i] for i in take], *weights)
    terms, at = [], 0
    for ns, _ in layouts:
        terms.append(outs[at : at + len(ns)])
        at += len(ns)
    return terms


def add(*terms):
    total = terms[0].astype(f32)
    for term in terms[1:]:
        total = total + term.astype(f32)
    return total


def pair_sum(even, odd, later, sides):
    size = even[0].shape[0]
    parts = [slice(i * size, (i + 1) * size) for i in range(sides - 1)]
    over = [swap(odd[3][at], "exp", 2) for at in parts]
    odd_got = [swap(odd[1][at], "seq", 2 * i + 2) for i, at in enumerate(parts)]
    odd_got.append(swap(odd[2], "exp", 1))
    even_got = [swap(even[1][at], "seq", 2 * i + 2) for i, at in enumerate(parts)]
    even_got.append(swap(even[2], "exp", 1))
    if later:
        over, odd_got, later = lax.optimization_barrier((over, odd_got, later))
    over = [add(even[3][at], o).astype(bf16) for at, o in zip(parts, over)]
    if WAIT and later:
        over, later = lax.optimization_barrier((over, later))
    even_got += [swap_both(o, 2 * i + 2, 1) for i, o in enumerate(over)]
    return add(even[0], *even_got), add(odd[0], *odd_got), later


def return_terms(terms, sides):
    own = []
    for kz in reversed(range(0, len(terms), 2)):
        even, odd, terms[:kz] = pair_sum(terms[kz], terms[kz + 1], terms[:kz], sides)
        got = swap(odd.astype(bf16), "exp", 2)
        if kz and GATE:
            got, terms[:kz] = lax.optimization_barrier((got, terms[:kz]))
        own += [swap(add(even, got).astype(bf16), "exp", 2 * kz)] if kz else [even, got]
    return own


def experts_by_chip(rows, width, weights, nexp):
    nseq, nplace = lax.axis_size("seq"), lax.axis_size("exp")
    cap = 3 * rows.shape[0] * TOPK // (2 * nexp)
    planes, sides = nplace // 2, nseq // 2
    me = lax.axis_index("seq") * nplace + lax.axis_index("exp")
    other = (lax.axis_index("seq") ^ 1) * nplace + lax.axis_index("exp")
    mine = jnp.stack([me, other]).astype(jnp.int32)
    blocks = gather_rows(rows, planes, sides)
    terms = []
    for at in range(0, planes, CALL):
        terms += expert_terms(blocks[at : at + CALL], sides, mine, weights, cap, nexp)
    return return_terms(terms, sides)


def experts_by_device(rows, width, ids, gate_proj, up_proj, down_proj, nexp):
    tokens = rows.shape[0]
    normed = rows[:, :width]
    gates = rows[:, width : width + nexp].astype(f32) + rows[
        :, width + nexp : width + 2 * nexp
    ].astype(f32)
    gates = jnp.take_along_axis(gates, ids, axis=1)
    capacity = 3 * tokens * TOPK // (2 * nexp)
    flat = ids.reshape(-1)
    member = (flat[:, None] == jnp.arange(nexp, dtype=jnp.int32)[None, :]).astype(jnp.int32)
    rank = jnp.sum((jnp.cumsum(member, axis=0) - 1) * member, axis=1)
    slot = flat * capacity + rank
    place = slot[:, None] == jnp.arange(nexp * capacity, dtype=jnp.int32)[None, :]
    route = jnp.any(place.reshape(tokens, TOPK, nexp * capacity), axis=1).astype(bf16)
    packed = jnp.einsum("ts,td->sd", route, normed, preferred_element_type=f32).astype(bf16)
    outgoing = packed.reshape(nexp, capacity, width)
    taken = lax.all_to_all(outgoing, ("seq", "exp"), split_axis=0, concat_axis=0, tiled=True)
    taken = taken.reshape(-1, width)
    gate = jnp.dot(taken, gate_proj[0], preferred_element_type=f32)
    upv = jnp.dot(taken, up_proj[0], preferred_element_type=f32)
    act = (jax.nn.silu(gate) * upv).astype(bf16)
    result = jnp.dot(act, down_proj[0], preferred_element_type=f32).astype(bf16)
    result = result.reshape(nexp, capacity, width)
    back = lax.all_to_all(result, ("seq", "exp"), split_axis=0, concat_axis=0, tiled=True)
    gathered = back.reshape(nexp * capacity, width)[slot].reshape(tokens, TOPK, width)
    return [jnp.sum(gates[:, :, None] * gathered.astype(f32), axis=1)]


def body(
    queries,
    new_keys,
    new_values,
    cache_keys,
    cache_values,
    cache_len,
    residual_in,
    out_weight,
    norm_gain,
    router_weight,
    expert_ids,
    gate_proj,
    up_proj,
    down_proj,
):
    nseq, nplace = lax.axis_size("seq"), lax.axis_size("exp")
    tokens, width = residual_in.shape[1:]
    nexp = router_weight.shape[1]
    by_chip = nseq * nplace <= 32
    me = lax.axis_index("seq").astype(jnp.int32).reshape(1)
    weights = [gate_proj, up_proj, down_proj]
    parts, pairs = project_attention(
        me,
        cache_len,
        queries[0],
        new_keys[0],
        new_values[0],
        cache_keys[0],
        cache_values[0],
        out_weight,
        weights if by_chip else [],
    )
    mixed, rows = norm_rows(
        residual_in[0], parts, norm_gain, router_weight, expert_ids[0]
    )
    if by_chip:
        rows, pairs = lax.optimization_barrier((rows, pairs))
        terms = experts_by_chip(rows, width, pairs, nexp)
    else:
        terms = experts_by_device(rows, width, expert_ids[0], *weights, nexp)
    return add(mixed, *terms).astype(bf16).reshape(1, tokens, width)


def solution(mesh):
    in_specs = (
        P("exp", "seq", None),
        P("exp", "seq", None),
        P("exp", "seq", None),
        P("exp", "seq", None),
        P("exp", "seq", None),
        P("exp"),
        P("exp", "seq", None),
        P("seq", None),
        P(),
        P(),
        P("exp", "seq", None),
        P(("seq", "exp"), None, None),
        P(("seq", "exp"), None, None),
        P(("seq", "exp"), None, None),
    )
    out_specs = P("exp", "seq", None)
    return jax.shard_map(body, mesh=mesh, in_specs=in_specs, out_specs=out_specs, check_vma=False)
```

```python
import functools
import math

import jax
import jax.numpy as jnp
from jax import lax
from jax.experimental import pallas as pl
from jax.experimental.pallas import tpu as pltpu
from jax.sharding import PartitionSpec as P

QH = 32
KVH = 4
HD = 128
TOPK = 8
MASKED = -1e30
EXPERT_MIB = 46
GATHER = ("c2", "c1", "d0", "y0", "x0", "c3", "d2", "x2", "y2", "y1", "x1", "d1", "y3", "x3", "d3")
TAKE = tuple(range(16))
CALL = 4
HOLD = 3
GATE = 0
WAIT = 0
DIRECT = (0,)
RELAY = 0
FIRST = -1
NEAR_MIB = 14
FAR_MIB = 14
NORM_MIB = 16
EXP2_SCALE = math.log2(math.e) / math.sqrt(HD)
NT = (((1,), (1,)), ((), ()))
TN = (((0,), (0,)), ((), ()))
VMEM = pl.BlockSpec(memory_space=pltpu.VMEM)
SMEM = pl.BlockSpec(memory_space=pltpu.SMEM)
ANY = pl.BlockSpec(memory_space=pl.ANY)
f32 = jnp.float32
bf16 = jnp.bfloat16


def swap(rows, axis, bits):
    return lax.ppermute(rows, axis, [(i, i ^ bits) for i in range(lax.axis_size(axis))])


def swap_both(rows, seq_bits, exp_bits):
    nseq, nplace = lax.axis_size("seq"), lax.axis_size("exp")
    bits = seq_bits * nplace + exp_bits
    return lax.ppermute(rows, ("seq", "exp"), [(i, i ^ bits) for i in range(nseq * nplace)])


def params(mib):
    return pltpu.CompilerParams(vmem_limit_bytes=mib << 20)


def pack_kernel(nseq, widths, me_ref, *refs):
    ins, outs, sem = refs[: len(widths)], refs[len(widths) : -1], refs[-1]
    copies = []
    for k in range(nseq):
        dest, to = me_ref[0] ^ k, 0
        for i, cols in enumerate(widths):
            start = dest * cols if ins[i].shape[1] == cols * nseq else dest * KVH // nseq * HD
            start = pl.ds(pl.multiple_of(start, HD), cols)
            pair = ins[i].at[:, start], outs[k].at[:, to : to + cols]
            copies.append(pltpu.make_async_copy(*pair, sem.at[k, i]))
            to += cols
    for copy in copies:
        copy.start()
    for copy in copies:
        copy.wait()


def pack(me, arrays, widths, nseq):
    shape = jax.ShapeDtypeStruct((arrays[0].shape[0], sum(widths)), bf16)
    return pl.pallas_call(
        functools.partial(pack_kernel, nseq, widths),
        out_shape=[shape] * nseq,
        in_specs=[SMEM] + [ANY] * len(arrays),
        out_specs=[VMEM] * nseq,
        scratch_shapes=[pltpu.SemaphoreType.DMA((nseq, len(arrays)))],
        compiler_params=params(61),
        name="pack_heads",
    )(me, *arrays)


def head_rows(heads, start):
    return jnp.concatenate([ref[:, start : start + HD] for ref in heads], 0)


def slot_bias(me, length, ks, slots):
    parts = []
    for k in ks:
        pos = (me ^ k) * slots + lax.broadcasted_iota(jnp.int32, (1, slots), 1)
        parts.append(jnp.where(pos < length, f32(0.0), f32(MASKED)))
    return jnp.concatenate(parts, 1)


def near_kernel(nseq, me_ref, len_ref, *refs):
    heads, caches = refs[:nseq], refs[nseq : nseq + 2]
    peak_ref, sum_ref, acc_ref = refs[nseq + 3 :]
    group = QH // nseq
    qcols = group * HD
    me = me_ref[0]
    slots, tokens = caches[0].shape[0], heads[0].shape[0]
    qtok = nseq * tokens
    bias = slot_bias(me, len_ref[0], (0, 1), slots)
    keys = jnp.concatenate([ref[:, :HD] for ref in caches], 0)
    vals = jnp.concatenate([ref[:, HD:] for ref in caches], 0)
    new_keys, new_vals = head_rows(heads, qcols), head_rows(heads, qcols + HD)
    row = lax.broadcasted_iota(jnp.int32, (qtok, qtok), 0)
    col = lax.broadcasted_iota(jnp.int32, (qtok, qtok), 1)
    qpos = (me ^ (row // tokens)) * tokens + row % tokens
    kpos = (me ^ (col // tokens)) * tokens + col % tokens
    new_bias = jnp.where(kpos <= qpos, f32(0.0), f32(MASKED))
    for g in range(group):
        q = head_rows(heads, g * HD)
        s = lax.dot_general(q, keys, NT, preferred_element_type=f32) + bias
        t = lax.dot_general(q, new_keys, NT, preferred_element_type=f32) + new_bias
        peak = jnp.maximum(jnp.max(s, axis=1, keepdims=True), jnp.max(t, axis=1, keepdims=True))
        p = jnp.exp2((s - peak) * f32(EXP2_SCALE))
        r = jnp.exp2((t - peak) * f32(EXP2_SCALE))
        peak_ref[:, g : g + 1] = peak
        sum_ref[:, g : g + 1] = jnp.sum(p, axis=1, keepdims=True) + jnp.sum(r, axis=1, keepdims=True)
        acc = jnp.dot(p.astype(bf16), vals, preferred_element_type=f32)
        acc += jnp.dot(r.astype(bf16), new_vals, preferred_element_type=f32)
        acc_ref[:, g * HD : (g + 1) * HD] = acc


def far_kernel(nseq, ks, me_ref, len_ref, *refs):
    heads, caches = refs[: len(ks)], refs[len(ks) : len(ks) + nseq - 2]
    peak_ref, sum_ref, acc_ref, w_ref, even_ref, odd_ref, attn_ref = refs[len(ks) + nseq - 2 :]
    group = QH // nseq
    slots, tokens = caches[0].shape[0], heads[0].shape[0]
    mine = slice(ks[0] * tokens, (ks[-1] + 1) * tokens)
    bias = slot_bias(me_ref[0], len_ref[0], range(2, nseq), slots)
    keys = jnp.concatenate([ref[:, :HD] for ref in caches], 0)
    vals = jnp.concatenate([ref[:, HD:] for ref in caches], 0)
    for g in range(group):
        at = slice(g * HD, (g + 1) * HD)
        q = head_rows(heads, g * HD)
        s = lax.dot_general(q, keys, NT, preferred_element_type=f32) + bias
        old = peak_ref[mine, g : g + 1]
        peak = jnp.maximum(jnp.max(s, axis=1, keepdims=True), old)
        fade = jnp.exp2((old - peak) * f32(EXP2_SCALE))
        p = jnp.exp2((s - peak) * f32(EXP2_SCALE))
        total = sum_ref[mine, g : g + 1] * fade + jnp.sum(p, axis=1, keepdims=True)
        acc = acc_ref[mine, at] * fade + jnp.dot(p.astype(bf16), vals, preferred_element_type=f32)
        attn_ref[:, at] = (acc / total).astype(bf16)
    step = 512
    for at in range(0, w_ref.shape[1], step):
        cols = slice(at, at + step)
        total = jnp.dot(attn_ref[...], w_ref[:, cols], preferred_element_type=f32)
        for i in range(len(ks)):
            to = slice(i // 2 * tokens, (i // 2 + 1) * tokens)
            out = odd_ref if i % 2 else even_ref
            out[to, cols] = total[i * tokens : (i + 1) * tokens].astype(out.dtype)


def project_attention(
    me, length, queries, new_keys, new_values, cache_keys, cache_values, out_weight, weights
):
    nseq = lax.axis_size("seq")
    tokens = queries.shape[0]
    width = out_weight.shape[1]
    group = QH // nseq
    qtok = nseq * tokens
    heads = pack(me, (queries, new_keys, new_values), (group * HD, HD, HD), nseq)
    order = sorted(range(1, nseq), reverse=True)
    heads = {0: heads[0]} | {k: swap(heads[k], "seq", k) for k in order}
    others = [swap(w, "seq", 1) for w in weights[:2]]
    held = heads[1], cache_keys, cache_values
    heads[1], cache_keys, cache_values = lax.optimization_barrier(held)
    caches = pack(me, (cache_keys, cache_values), (HD, HD), nseq)
    caches = {0: caches[0], 1: swap(caches[1], "seq", 1)} | dict(enumerate(caches[2:], 2))
    for k in range(2, nseq):
        hold = (heads[k], caches[k], others if k == HOLD else [])
        heads[k], cache, held = lax.optimization_barrier(hold)
        others = held or others
        caches[k] = swap(cache, "seq", k)
    heads = [heads[k] for k in range(nseq)]
    caches = [caches[k] for k in range(nseq)]
    state = pl.pallas_call(
        functools.partial(near_kernel, nseq),
        out_shape=[
            jax.ShapeDtypeStruct((qtok, HD), f32),
            jax.ShapeDtypeStruct((qtok, HD), f32),
            jax.ShapeDtypeStruct((qtok, group * HD), f32),
        ],
        in_specs=[SMEM] * 2 + [VMEM] * (nseq + 3),
        out_specs=[VMEM] * 3,
        compiler_params=params(NEAR_MIB),
        name="attend_near",
    )(me, length, *heads, *caches[:2], out_weight)

    def project(ks, state):
        shape = (len(ks) // 2 * tokens, width)
        return pl.pallas_call(
            functools.partial(far_kernel, nseq, ks),
            out_shape=[jax.ShapeDtypeStruct(shape, f32), jax.ShapeDtypeStruct(shape, bf16)],
            in_specs=[SMEM] * 2 + [VMEM] * (len(ks) + nseq + 2),
            out_specs=[VMEM] * 2,
            scratch_shapes=[pltpu.VMEM((len(ks) * tokens, group * HD), bf16)],
            compiler_params=params(FAR_MIB),
            name="attend_far",
        )(me, length, *[heads[k] for k in ks], *caches[2:], *state, out_weight)

    even, odd = project(list(range(nseq)), state)
    got = swap(odd, "seq", 1)
    got, rest = lax.optimization_barrier((got, weights[2:]))
    others += [swap(w, "seq", 1) for w in rest]
    terms = [even[:tokens], got[:tokens]]
    for at in range(tokens, got.shape[0], tokens):
        both = add(even[at : at + tokens], got[at : at + tokens])
        terms.append(swap(both.astype(bf16), "seq", 2 * at // tokens))
    return terms, [*weights, *others]


def norm_kernel(nterms, res_ref, *refs):
    gain_ref, router_ref, ids_ref, mixed_ref, rows_ref = refs[nterms:]
    tokens, width = res_ref.shape
    mixed = res_ref[...].astype(f32)
    for ref in refs[:nterms]:
        mixed += ref[...].astype(f32)
    mixed_ref[...] = mixed
    meansq = jnp.mean(mixed * mixed, axis=1, keepdims=True)
    normed = (mixed / jnp.sqrt(meansq + 1e-06) * gain_ref[...]).astype(bf16)
    rows_ref[:, :width] = normed
    logits = lax.dot_general(router_ref[...], normed, NT, preferred_element_type=f32)
    nexp = logits.shape[0]
    expert = lax.broadcasted_iota(jnp.int32, (nexp, tokens), 0)
    chosen = expert == ids_ref[0:1, :]
    for k in range(1, ids_ref.shape[0]):
        chosen = jnp.logical_or(chosen, expert == ids_ref[k : k + 1, :])
    expo = jnp.where(chosen, jnp.exp(logits), f32(0.0))
    gates = expo / jnp.sum(expo, axis=0, keepdims=True)
    high = gates.astype(bf16)
    low = (gates - high.astype(f32)).astype(bf16)
    extra = rows_ref.shape[1] - width
    row = lax.broadcasted_iota(jnp.int32, (nexp, extra), 0)
    col = lax.broadcasted_iota(jnp.int32, (nexp, extra), 1)
    spread = lax.dot_general(high, (col == row).astype(bf16), TN, preferred_element_type=f32)
    spread += lax.dot_general(low, (col == row + nexp).astype(bf16), TN, preferred_element_type=f32)
    rows_ref[:, width:] = spread.astype(bf16)


def norm_rows(residual, terms, gain, router, ids):
    tokens, width = residual.shape
    extra = -(-2 * router.shape[1] // 128) * 128
    return pl.pallas_call(
        functools.partial(norm_kernel, len(terms)),
        out_shape=[
            jax.ShapeDtypeStruct((tokens, width), f32),
            jax.ShapeDtypeStruct((tokens, width + extra), bf16),
        ],
        in_specs=[VMEM] * (4 + len(terms)),
        out_specs=[VMEM] * 2,
        compiler_params=params(NORM_MIB),
        name="norm_and_route",
    )(residual, *terms, gain.reshape(1, width), router.T, ids.T)


def gather_rows(rows, planes, sides):
    at = {("c", 0): [rows]}
    steps = [(kind, kz) for kz in range(planes) for kind in "cxyd" if (kind, kz) not in at]
    if planes == 4:
        steps = [(step[0], int(step[1])) for step in GATHER]
    for i, (kind, kz) in enumerate(steps):
        if i == FIRST:
            at = lax.optimization_barrier(at)
        near = kz > 1 and kz % 2
        if kind == "c":
            got = [swap(at["c", kz - 1][0], "exp", 2) if near else swap(rows, "exp", 2 * kz)]
        elif kind == "x":
            got = [swap(at["c", kz][0], "seq", 2 * kx) for kx in range(1, sides)]
        elif kind == "y":
            got = [swap(at["c", kz][0], "exp", 1)]
        elif kz in DIRECT:
            got = [swap_both(at["c", kz][0], 2 * kx, 1) for kx in range(1, sides)]
        elif kz % 2:
            got = [swap(block, "exp", 2) for block in at["d", kz - 1]]
        elif RELAY:
            got = [swap(block, "exp", 1) for block in at["x", kz]]
        else:
            got = [swap(block, "exp", 2 * kz) for block in at["d", 0]]
        at[kind, kz] = got
    return [[block for kind in "cxyd" for block in at[kind, kz]] for kz in range(planes)]


def plane_layout(sides, tokens):
    rows = [tokens, (sides - 1) * tokens, tokens, (sides - 1) * tokens]
    moves = []
    for ky in range(2):
        for kx in range(sides):
            to = (2 * ky + (kx > 0), max(kx - 1, 0) * tokens)
            moves.append(((ky * sides + kx) * tokens, tokens, *to))
    return rows, moves


def expert_kernel(layouts, take, per_group, tokens, cap, nexp, mine_ref, *refs):
    planes = len(layouts)
    pieces = planes * per_group
    blocks = [refs[take.index(i)] for i in range(pieces)]
    weights = (refs[pieces : pieces + 3], refs[pieces + 3 : pieces + 6])
    nouts = sum(len(rows) for rows, _ in layouts)
    outs = refs[pieces + 6 : pieces + 6 + nouts]
    got_ref, x_ref, act_ref, hot_ref, wide_ref, down_ref, sem, got_sem = refs[pieces + 6 + nouts :]
    copies = [
        pltpu.make_async_copy(
            blocks[g * per_group + i],
            got_ref.at[g, i * tokens : (i + 1) * tokens],
            got_sem.at[g, i],
        )
        for g in range(planes)
        for i in range(per_group)
    ]
    for copy in copies:
        copy.start()
    loads = [
        [
            pltpu.make_async_copy(ws[0].at[0], wide_ref.at[i, 0], sem.at[i, 0]),
            pltpu.make_async_copy(ws[1].at[0], wide_ref.at[i, 1], sem.at[i, 1]),
            pltpu.make_async_copy(ws[2].at[0], down_ref.at[i], sem.at[i, 2]),
        ]
        for i, ws in enumerate(weights)
    ]
    loads[0][0].start()
    loads[0][1].start()
    width = x_ref.shape[2]
    hidden = act_ref.shape[1]
    ext = got_ref.shape[2] - width
    gtok = per_group * tokens
    grows = per_group * cap
    step = 256
    ecol = lax.broadcasted_iota(jnp.int32, (8, ext), 1)
    erow = lax.broadcasted_iota(jnp.int32, (8, ext), 0)
    want = jnp.where(erow == 0, mine_ref[0], jnp.where(erow == 1, mine_ref[1], -ext))
    pick = jnp.logical_or(ecol == want, ecol == want + nexp).astype(bf16)
    trow = lax.broadcasted_iota(jnp.int32, (gtok, gtok), 0)
    tcol = lax.broadcasted_iota(jnp.int32, (gtok, gtok), 1)
    before = jnp.logical_and(trow < tcol, trow // tokens == tcol // tokens).astype(bf16)
    block = lax.broadcasted_iota(jnp.int32, (8, gtok), 1) // tokens
    slot = lax.broadcasted_iota(jnp.int32, (grows, gtok), 0).astype(f32)
    row_gates = [[], []]
    for g in range(planes):
        for copy in copies[g * per_group : (g + 1) * per_group]:
            copy.wait()
        tail = got_ref[g, :, width:]
        gates = lax.dot_general(pick, tail, NT, preferred_element_type=f32)
        chosen = gates > 0.0
        rank = jnp.dot(chosen.astype(bf16), before, preferred_element_type=f32)
        target = jnp.where(chosen, (block * cap).astype(f32) + rank, f32(-1.0))
        hot = jnp.concatenate(
            [(slot == target[i : i + 1, :]).astype(f32) for i in range(2)], 0
        ).astype(bf16)
        hot_ref[g] = hot
        for at in range(0, width, step):
            part = got_ref[g, :, at : at + step]
            got = jnp.dot(hot, part, preferred_element_type=f32).astype(bf16)
            for i in range(2):
                x_ref[i, g * grows : (g + 1) * grows, at : at + step] = got[
                    i * grows : (i + 1) * grows
                ]
        got = jnp.dot(hot, tail, preferred_element_type=f32)
        for i in range(2):
            sel = pick[i : i + 1, :].astype(f32)
            row_gates[i].append(
                jnp.sum(got[i * grows : (i + 1) * grows] * sel, axis=1, keepdims=True)
            )
    loads[0][2].start()
    for i in range(2):
        x = x_ref[i]
        loads[i][0].wait()
        loads[i][1].wait()
        if i == 0:
            loads[1][0].start()
            loads[1][1].start()
        for at in range(0, hidden, step):
            cols = slice(at, at + step)
            gate = jnp.dot(x, wide_ref[i, 0, :, cols], preferred_element_type=f32)
            upv = jnp.dot(x, wide_ref[i, 1, :, cols], preferred_element_type=f32)
            act_ref[:, cols] = (gate / (1.0 + jnp.exp(-gate)) * upv).astype(bf16)
        loads[i][2].wait()
        if i == 0:
            loads[1][2].start()
        row_gate = jnp.concatenate(row_gates[i], 0)
        for at in range(0, width, step):
            cols = slice(at, at + step)
            y = jnp.dot(act_ref[...], down_ref[i, :, cols], preferred_element_type=f32)
            x_ref[i, :, cols] = (y * row_gate).astype(bf16)
    first = 0
    for g, (rows, moves) in enumerate(layouts):
        for at in range(0, width, step):
            cols = slice(at, at + step)
            y = jnp.concatenate(
                [x_ref[i, g * grows : (g + 1) * grows, cols] for i in range(2)], 0
            )
            total = lax.dot_general(hot_ref[g], y, TN, preferred_element_type=f32).astype(bf16)
            for row, count, out, to in moves:
                outs[first + out][to : to + count, cols] = total[row : row + count]
        first += len(rows)


def expert_terms(blocks, sides, mine, weights, cap, nexp):
    planes, per_group = len(blocks), len(blocks[0])
    tokens, wide = blocks[0][0].shape
    _, width, hidden = weights[0].shape
    grows = per_group * cap
    rows = planes * grows
    layouts = [plane_layout(sides, tokens)] * planes
    out_shape = [jax.ShapeDtypeStruct((n, width), bf16) for ns, _ in layouts for n in ns]
    flat = [block for plane in blocks for block in plane]
    take = TAKE if len(flat) == len(TAKE) else tuple(range(len(flat)))
    outs = pl.pallas_call(
        functools.partial(expert_kernel, layouts, take, per_group, tokens, cap, nexp),
        out_shape=out_shape,
        in_specs=[SMEM] + [ANY] * (planes * per_group + len(weights)),
        out_specs=[VMEM] * len(out_shape),
        scratch_shapes=[
            pltpu.VMEM((planes, per_group * tokens, wide), bf16),
            pltpu.VMEM((2, rows, width), bf16),
            pltpu.VMEM((rows, hidden), bf16),
            pltpu.VMEM((planes, 2 * grows, per_group * tokens), bf16),
            pltpu.VMEM((2, 2, width, hidden), bf16),
            pltpu.VMEM((2, hidden, width), bf16),
            pltpu.SemaphoreType.DMA((2, 3)),
            pltpu.SemaphoreType.DMA((planes, per_group)),
        ],
        compiler_params=params(EXPERT_MIB),
        cost_estimate=pl.CostEstimate(
            flops=12 * rows * width * hidden, bytes_accessed=8 * rows * width, transcendentals=0
        ),
        name="experts",
    )(mine, *[flat[i] for i in take], *weights)
    terms, at = [], 0
    for ns, _ in layouts:
        terms.append(outs[at : at + len(ns)])
        at += len(ns)
    return terms


def add(*terms):
    total = terms[0].astype(f32)
    for term in terms[1:]:
        total = total + term.astype(f32)
    return total


def pair_sum(even, odd, later, sides):
    size = even[0].shape[0]
    parts = [slice(i * size, (i + 1) * size) for i in range(sides - 1)]
    over = [swap(odd[3][at], "exp", 2) for at in parts]
    odd_got = [swap(odd[1][at], "seq", 2 * i + 2) for i, at in enumerate(parts)]
    odd_got.append(swap(odd[2], "exp", 1))
    even_got = [swap(even[1][at], "seq", 2 * i + 2) for i, at in enumerate(parts)]
    even_got.append(swap(even[2], "exp", 1))
    if later:
        over, odd_got, later = lax.optimization_barrier((over, odd_got, later))
    over = [add(even[3][at], o).astype(bf16) for at, o in zip(parts, over)]
    if WAIT and later:
        over, later = lax.optimization_barrier((over, later))
    even_got += [swap_both(o, 2 * i + 2, 1) for i, o in enumerate(over)]
    return add(even[0], *even_got), add(odd[0], *odd_got), later


def return_terms(terms, sides):
    own = []
    for kz in reversed(range(0, len(terms), 2)):
        even, odd, terms[:kz] = pair_sum(terms[kz], terms[kz + 1], terms[:kz], sides)
        got = swap(odd.astype(bf16), "exp", 2)
        if kz and GATE:
            got, terms[:kz] = lax.optimization_barrier((got, terms[:kz]))
        own += [swap(add(even, got).astype(bf16), "exp", 2 * kz)] if kz else [even, got]
    return own


def experts_by_chip(rows, width, weights, nexp):
    nseq, nplace = lax.axis_size("seq"), lax.axis_size("exp")
    cap = 3 * rows.shape[0] * TOPK // (2 * nexp)
    planes, sides = nplace // 2, nseq // 2
    me = lax.axis_index("seq") * nplace + lax.axis_index("exp")
    other = (lax.axis_index("seq") ^ 1) * nplace + lax.axis_index("exp")
    mine = jnp.stack([me, other]).astype(jnp.int32)
    blocks = gather_rows(rows, planes, sides)
    terms = []
    for at in range(0, planes, CALL):
        terms += expert_terms(blocks[at : at + CALL], sides, mine, weights, cap, nexp)
    return return_terms(terms, sides)


def experts_by_device(rows, width, ids, gate_proj, up_proj, down_proj, nexp):
    tokens = rows.shape[0]
    normed = rows[:, :width]
    gates = rows[:, width : width + nexp].astype(f32) + rows[
        :, width + nexp : width + 2 * nexp
    ].astype(f32)
    gates = jnp.take_along_axis(gates, ids, axis=1)
    capacity = 3 * tokens * TOPK // (2 * nexp)
    flat = ids.reshape(-1)
    member = (flat[:, None] == jnp.arange(nexp, dtype=jnp.int32)[None, :]).astype(jnp.int32)
    rank = jnp.sum((jnp.cumsum(member, axis=0) - 1) * member, axis=1)
    slot = flat * capacity + rank
    place = slot[:, None] == jnp.arange(nexp * capacity, dtype=jnp.int32)[None, :]
    route = jnp.any(place.reshape(tokens, TOPK, nexp * capacity), axis=1).astype(bf16)
    packed = jnp.einsum("ts,td->sd", route, normed, preferred_element_type=f32).astype(bf16)
    outgoing = packed.reshape(nexp, capacity, width)
    taken = lax.all_to_all(outgoing, ("seq", "exp"), split_axis=0, concat_axis=0, tiled=True)
    taken = taken.reshape(-1, width)
    gate = jnp.dot(taken, gate_proj[0], preferred_element_type=f32)
    upv = jnp.dot(taken, up_proj[0], preferred_element_type=f32)
    act = (jax.nn.silu(gate) * upv).astype(bf16)
    result = jnp.dot(act, down_proj[0], preferred_element_type=f32).astype(bf16)
    result = result.reshape(nexp, capacity, width)
    back = lax.all_to_all(result, ("seq", "exp"), split_axis=0, concat_axis=0, tiled=True)
    gathered = back.reshape(nexp * capacity, width)[slot].reshape(tokens, TOPK, width)
    return [jnp.sum(gates[:, :, None] * gathered.astype(f32), axis=1)]


def body(
    queries,
    new_keys,
    new_values,
    cache_keys,
    cache_values,
    cache_len,
    residual_in,
    out_weight,
    norm_gain,
    router_weight,
    expert_ids,
    gate_proj,
    up_proj,
    down_proj,
):
    nseq, nplace = lax.axis_size("seq"), lax.axis_size("exp")
    tokens, width = residual_in.shape[1:]
    nexp = router_weight.shape[1]
    by_chip = nseq * nplace <= 32
    me = lax.axis_index("seq").astype(jnp.int32).reshape(1)
    weights = [gate_proj, up_proj, down_proj]
    parts, pairs = project_attention(
        me,
        cache_len,
        queries[0],
        new_keys[0],
        new_values[0],
        cache_keys[0],
        cache_values[0],
        out_weight,
        weights if by_chip else [],
    )
    mixed, rows = norm_rows(
        residual_in[0], parts, norm_gain, router_weight, expert_ids[0]
    )
    if by_chip:
        rows, pairs = lax.optimization_barrier((rows, pairs))
        terms = experts_by_chip(rows, width, pairs, nexp)
    else:
        terms = experts_by_device(rows, width, expert_ids[0], *weights, nexp)
    return add(mixed, *terms).astype(bf16).reshape(1, tokens, width)


def solution(mesh):
    in_specs = (
        P("exp", "seq", None),
        P("exp", "seq", None),
        P("exp", "seq", None),
        P("exp", "seq", None),
        P("exp", "seq", None),
        P("exp"),
        P("exp", "seq", None),
        P("seq", None),
        P(),
        P(),
        P("exp", "seq", None),
        P(("seq", "exp"), None, None),
        P(("seq", "exp"), None, None),
        P(("seq", "exp"), None, None),
    )
    out_specs = P("exp", "seq", None)
    return jax.shard_map(body, mesh=mesh, in_specs=in_specs, out_specs=out_specs, check_vma=False)
```

```python
import functools
import math

import jax
import jax.numpy as jnp
from jax import lax
from jax.experimental import pallas as pl
from jax.experimental.pallas import tpu as pltpu
from jax.sharding import PartitionSpec as P

QH = 32
KVH = 4
HD = 128
TOPK = 8
MASKED = -1e30
EXPERT_MIB = 46
GATHER = ("c2", "c1", "d0", "y0", "x0", "c3", "d2", "x2", "y2", "y1", "x1", "d1", "y3", "x3", "d3")
TAKE = (3, 14, 4, 9, 13, 11, 7, 2, 12, 8, 1, 0, 15, 6, 5, 10)
NEAR_MIB = 14
FAR_MIB = 14
EXP2_SCALE = math.log2(math.e) / math.sqrt(HD)
NT = (((1,), (1,)), ((), ()))
TN = (((0,), (0,)), ((), ()))
VMEM = pl.BlockSpec(memory_space=pltpu.VMEM)
SMEM = pl.BlockSpec(memory_space=pltpu.SMEM)
ANY = pl.BlockSpec(memory_space=pl.ANY)
f32 = jnp.float32
bf16 = jnp.bfloat16


def swap(rows, axis, bits):
    return lax.ppermute(rows, axis, [(i, i ^ bits) for i in range(lax.axis_size(axis))])


def swap_both(rows, seq_bits, exp_bits):
    nseq, nplace = lax.axis_size("seq"), lax.axis_size("exp")
    bits = seq_bits * nplace + exp_bits
    return lax.ppermute(rows, ("seq", "exp"), [(i, i ^ bits) for i in range(nseq * nplace)])


def params(mib):
    return pltpu.CompilerParams(vmem_limit_bytes=mib << 20)


def pack_kernel(nseq, widths, me_ref, *refs):
    ins, outs, sem = refs[: len(widths)], refs[len(widths) : -1], refs[-1]
    copies = []
    for k in range(nseq):
        dest, to = me_ref[0] ^ k, 0
        for i, cols in enumerate(widths):
            start = dest * cols if ins[i].shape[1] == cols * nseq else dest * KVH // nseq * HD
            start = pl.ds(pl.multiple_of(start, HD), cols)
            pair = ins[i].at[:, start], outs[k].at[:, to : to + cols]
            copies.append(pltpu.make_async_copy(*pair, sem.at[k, i]))
            to += cols
    for copy in copies:
        copy.start()
    for copy in copies:
        copy.wait()


def pack(me, arrays, widths, nseq):
    shape = jax.ShapeDtypeStruct((arrays[0].shape[0], sum(widths)), bf16)
    return pl.pallas_call(
        functools.partial(pack_kernel, nseq, widths),
        out_shape=[shape] * nseq,
        in_specs=[SMEM] + [ANY] * len(arrays),
        out_specs=[VMEM] * nseq,
        scratch_shapes=[pltpu.SemaphoreType.DMA((nseq, len(arrays)))],
        compiler_params=params(61),
        name="pack_heads",
    )(me, *arrays)


def head_rows(heads, start):
    return jnp.concatenate([ref[:, start : start + HD] for ref in heads], 0)


def slot_bias(me, length, ks, slots):
    parts = []
    for k in ks:
        pos = (me ^ k) * slots + lax.broadcasted_iota(jnp.int32, (1, slots), 1)
        parts.append(jnp.where(pos < length, f32(0.0), f32(MASKED)))
    return jnp.concatenate(parts, 1)


def near_kernel(nseq, me_ref, len_ref, *refs):
    heads, caches = refs[:nseq], refs[nseq : nseq + 2]
    peak_ref, sum_ref, acc_ref = refs[nseq + 3 :]
    group = QH // nseq
    qcols = group * HD
    me = me_ref[0]
    slots, tokens = caches[0].shape[0], heads[0].shape[0]
    qtok = nseq * tokens
    bias = slot_bias(me, len_ref[0], (0, 1), slots)
    keys = jnp.concatenate([ref[:, :HD] for ref in caches], 0)
    vals = jnp.concatenate([ref[:, HD:] for ref in caches], 0)
    new_keys, new_vals = head_rows(heads, qcols), head_rows(heads, qcols + HD)
    row = lax.broadcasted_iota(jnp.int32, (qtok, qtok), 0)
    col = lax.broadcasted_iota(jnp.int32, (qtok, qtok), 1)
    qpos = (me ^ (row // tokens)) * tokens + row % tokens
    kpos = (me ^ (col // tokens)) * tokens + col % tokens
    new_bias = jnp.where(kpos <= qpos, f32(0.0), f32(MASKED))
    for g in range(group):
        q = head_rows(heads, g * HD)
        s = lax.dot_general(q, keys, NT, preferred_element_type=f32) + bias
        t = lax.dot_general(q, new_keys, NT, preferred_element_type=f32) + new_bias
        peak = jnp.maximum(jnp.max(s, axis=1, keepdims=True), jnp.max(t, axis=1, keepdims=True))
        p = jnp.exp2((s - peak) * f32(EXP2_SCALE))
        r = jnp.exp2((t - peak) * f32(EXP2_SCALE))
        peak_ref[:, g : g + 1] = peak
        sum_ref[:, g : g + 1] = jnp.sum(p, axis=1, keepdims=True) + jnp.sum(r, axis=1, keepdims=True)
        acc = jnp.dot(p.astype(bf16), vals, preferred_element_type=f32)
        acc += jnp.dot(r.astype(bf16), new_vals, preferred_element_type=f32)
        acc_ref[:, g * HD : (g + 1) * HD] = acc


def far_kernel(nseq, ks, me_ref, len_ref, *refs):
    heads, caches = refs[: len(ks)], refs[len(ks) : len(ks) + nseq - 2]
    peak_ref, sum_ref, acc_ref, w_ref, even_ref, odd_ref, attn_ref = refs[len(ks) + nseq - 2 :]
    group = QH // nseq
    slots, tokens = caches[0].shape[0], heads[0].shape[0]
    mine = slice(ks[0] * tokens, (ks[-1] + 1) * tokens)
    bias = slot_bias(me_ref[0], len_ref[0], range(2, nseq), slots)
    keys = jnp.concatenate([ref[:, :HD] for ref in caches], 0)
    vals = jnp.concatenate([ref[:, HD:] for ref in caches], 0)
    for g in range(group):
        at = slice(g * HD, (g + 1) * HD)
        q = head_rows(heads, g * HD)
        s = lax.dot_general(q, keys, NT, preferred_element_type=f32) + bias
        old = peak_ref[mine, g : g + 1]
        peak = jnp.maximum(jnp.max(s, axis=1, keepdims=True), old)
        fade = jnp.exp2((old - peak) * f32(EXP2_SCALE))
        p = jnp.exp2((s - peak) * f32(EXP2_SCALE))
        total = sum_ref[mine, g : g + 1] * fade + jnp.sum(p, axis=1, keepdims=True)
        acc = acc_ref[mine, at] * fade + jnp.dot(p.astype(bf16), vals, preferred_element_type=f32)
        attn_ref[:, at] = (acc / total).astype(bf16)
    step = 512
    for at in range(0, w_ref.shape[1], step):
        cols = slice(at, at + step)
        total = jnp.dot(attn_ref[...], w_ref[:, cols], preferred_element_type=f32)
        for i in range(len(ks)):
            to = slice(i // 2 * tokens, (i // 2 + 1) * tokens)
            out = odd_ref if i % 2 else even_ref
            out[to, cols] = total[i * tokens : (i + 1) * tokens].astype(out.dtype)


def project_attention(
    me, length, queries, new_keys, new_values, cache_keys, cache_values, out_weight, weights
):
    nseq = lax.axis_size("seq")
    tokens = queries.shape[0]
    width = out_weight.shape[1]
    group = QH // nseq
    qtok = nseq * tokens
    heads = pack(me, (queries, new_keys, new_values), (group * HD, HD, HD), nseq)
    order = sorted(range(1, nseq), reverse=True)
    heads = {0: heads[0]} | {k: swap(heads[k], "seq", k) for k in order}
    others = [swap(w, "seq", 1) for w in weights[:2]]
    held = heads[1], cache_keys, cache_values
    heads[1], cache_keys, cache_values = lax.optimization_barrier(held)
    caches = pack(me, (cache_keys, cache_values), (HD, HD), nseq)
    caches = {0: caches[0], 1: swap(caches[1], "seq", 1)} | dict(enumerate(caches[2:], 2))
    for k in range(2, nseq):
        held = (heads[k], caches[k], others if k == 3 else [])
        heads[k], cache, held = lax.optimization_barrier(held)
        others = held or others
        caches[k] = swap(cache, "seq", k)
    heads = [heads[k] for k in range(nseq)]
    caches = [caches[k] for k in range(nseq)]
    state = pl.pallas_call(
        functools.partial(near_kernel, nseq),
        out_shape=[
            jax.ShapeDtypeStruct((qtok, HD), f32),
            jax.ShapeDtypeStruct((qtok, HD), f32),
            jax.ShapeDtypeStruct((qtok, group * HD), f32),
        ],
        in_specs=[SMEM] * 2 + [VMEM] * (nseq + 3),
        out_specs=[VMEM] * 3,
        compiler_params=params(NEAR_MIB),
        name="attend_near",
    )(me, length, *heads, *caches[:2], out_weight)

    def project(ks, state):
        shape = (len(ks) // 2 * tokens, width)
        return pl.pallas_call(
            functools.partial(far_kernel, nseq, ks),
            out_shape=[jax.ShapeDtypeStruct(shape, f32), jax.ShapeDtypeStruct(shape, bf16)],
            in_specs=[SMEM] * 2 + [VMEM] * (len(ks) + nseq + 2),
            out_specs=[VMEM] * 2,
            scratch_shapes=[pltpu.VMEM((len(ks) * tokens, group * HD), bf16)],
            compiler_params=params(FAR_MIB),
            name="attend_far",
        )(me, length, *[heads[k] for k in ks], *caches[2:], *state, out_weight)

    even, odd = project(list(range(nseq)), state)
    got = swap(odd, "seq", 1)
    got, rest = lax.optimization_barrier((got, weights[2:]))
    others += [swap(w, "seq", 1) for w in rest]
    terms = [even[:tokens], got[:tokens]]
    for at in range(tokens, got.shape[0], tokens):
        both = add(even[at : at + tokens], got[at : at + tokens])
        terms.append(swap(both.astype(bf16), "seq", 2 * at // tokens))
    return terms, [*weights, *others]


def norm_kernel(nterms, res_ref, *refs):
    gain_ref, router_ref, ids_ref, mixed_ref, rows_ref = refs[nterms:]
    tokens, width = res_ref.shape
    mixed = res_ref[...].astype(f32)
    for ref in refs[:nterms]:
        mixed += ref[...].astype(f32)
    mixed_ref[...] = mixed
    meansq = jnp.mean(mixed * mixed, axis=1, keepdims=True)
    normed = (mixed / jnp.sqrt(meansq + 1e-06) * gain_ref[...]).astype(bf16)
    rows_ref[:, :width] = normed
    logits = lax.dot_general(router_ref[...], normed, NT, preferred_element_type=f32)
    nexp = logits.shape[0]
    expert = lax.broadcasted_iota(jnp.int32, (nexp, tokens), 0)
    chosen = expert == ids_ref[0:1, :]
    for k in range(1, ids_ref.shape[0]):
        chosen = jnp.logical_or(chosen, expert == ids_ref[k : k + 1, :])
    expo = jnp.where(chosen, jnp.exp(logits), f32(0.0))
    gates = expo / jnp.sum(expo, axis=0, keepdims=True)
    high = gates.astype(bf16)
    low = (gates - high.astype(f32)).astype(bf16)
    extra = rows_ref.shape[1] - width
    row = lax.broadcasted_iota(jnp.int32, (nexp, extra), 0)
    col = lax.broadcasted_iota(jnp.int32, (nexp, extra), 1)
    spread = lax.dot_general(high, (col == row).astype(bf16), TN, preferred_element_type=f32)
    spread += lax.dot_general(low, (col == row + nexp).astype(bf16), TN, preferred_element_type=f32)
    rows_ref[:, width:] = spread.astype(bf16)


def norm_rows(residual, terms, gain, router, ids):
    tokens, width = residual.shape
    extra = -(-2 * router.shape[1] // 128) * 128
    return pl.pallas_call(
        functools.partial(norm_kernel, len(terms)),
        out_shape=[
            jax.ShapeDtypeStruct((tokens, width), f32),
            jax.ShapeDtypeStruct((tokens, width + extra), bf16),
        ],
        in_specs=[VMEM] * (4 + len(terms)),
        out_specs=[VMEM] * 2,
        compiler_params=params(16),
        name="norm_and_route",
    )(residual, *terms, gain.reshape(1, width), router.T, ids.T)


def gather_rows(rows, planes, sides):
    at = {("c", 0): [rows]}
    steps = [(kind, kz) for kz in range(planes) for kind in "cxyd" if (kind, kz) not in at]
    if planes == 4:
        steps = [(step[0], int(step[1])) for step in GATHER]
    for kind, kz in steps:
        if kind == "x":
            got = [swap(at["c", kz][0], "seq", 2 * kx) for kx in range(1, sides)]
        elif kind == "y":
            got = [swap(at["c", kz][0], "exp", 1)]
        elif kz == 0:
            got = [swap_both(rows, 2 * kx, 1) for kx in range(1, sides)]
        elif kz > 1 and kz % 2:
            got = [swap(block, "exp", 2) for block in at[kind, kz - 1]]
        else:
            got = [swap(block, "exp", 2 * kz) for block in at[kind, 0]]
        at[kind, kz] = got
    return [[block for kind in "cxyd" for block in at[kind, kz]] for kz in range(planes)]


def plane_layout(sides, tokens):
    rows = [tokens, (sides - 1) * tokens, tokens, (sides - 1) * tokens]
    moves = []
    for ky in range(2):
        for kx in range(sides):
            to = (2 * ky + (kx > 0), max(kx - 1, 0) * tokens)
            moves.append(((ky * sides + kx) * tokens, tokens, *to))
    return rows, moves


def expert_kernel(layouts, take, per_group, tokens, cap, nexp, mine_ref, *refs):
    planes = len(layouts)
    pieces = planes * per_group
    blocks = [refs[take.index(i)] for i in range(pieces)]
    weights = (refs[pieces : pieces + 3], refs[pieces + 3 : pieces + 6])
    nouts = sum(len(rows) for rows, _ in layouts)
    outs = refs[pieces + 6 : pieces + 6 + nouts]
    got_ref, x_ref, act_ref, hot_ref, wide_ref, down_ref, sem, got_sem = refs[pieces + 6 + nouts :]
    copies = [
        pltpu.make_async_copy(
            blocks[g * per_group + i],
            got_ref.at[g, i * tokens : (i + 1) * tokens],
            got_sem.at[g, i],
        )
        for g in range(planes)
        for i in range(per_group)
    ]
    for copy in copies:
        copy.start()
    loads = [
        [
            pltpu.make_async_copy(ws[0].at[0], wide_ref.at[i, 0], sem.at[i, 0]),
            pltpu.make_async_copy(ws[1].at[0], wide_ref.at[i, 1], sem.at[i, 1]),
            pltpu.make_async_copy(ws[2].at[0], down_ref.at[i], sem.at[i, 2]),
        ]
        for i, ws in enumerate(weights)
    ]
    loads[0][0].start()
    loads[0][1].start()
    width = x_ref.shape[2]
    hidden = act_ref.shape[1]
    ext = got_ref.shape[2] - width
    gtok = per_group * tokens
    grows = per_group * cap
    step = 256
    ecol = lax.broadcasted_iota(jnp.int32, (8, ext), 1)
    erow = lax.broadcasted_iota(jnp.int32, (8, ext), 0)
    want = jnp.where(erow == 0, mine_ref[0], jnp.where(erow == 1, mine_ref[1], -ext))
    pick = jnp.logical_or(ecol == want, ecol == want + nexp).astype(bf16)
    trow = lax.broadcasted_iota(jnp.int32, (gtok, gtok), 0)
    tcol = lax.broadcasted_iota(jnp.int32, (gtok, gtok), 1)
    before = jnp.logical_and(trow < tcol, trow // tokens == tcol // tokens).astype(bf16)
    block = lax.broadcasted_iota(jnp.int32, (8, gtok), 1) // tokens
    slot = lax.broadcasted_iota(jnp.int32, (grows, gtok), 0).astype(f32)
    row_gates = [[], []]
    for g in range(planes):
        for copy in copies[g * per_group : (g + 1) * per_group]:
            copy.wait()
        tail = got_ref[g, :, width:]
        gates = lax.dot_general(pick, tail, NT, preferred_element_type=f32)
        chosen = gates > 0.0
        rank = jnp.dot(chosen.astype(bf16), before, preferred_element_type=f32)
        target = jnp.where(chosen, (block * cap).astype(f32) + rank, f32(-1.0))
        hot = jnp.concatenate(
            [(slot == target[i : i + 1, :]).astype(f32) for i in range(2)], 0
        ).astype(bf16)
        hot_ref[g] = hot
        for at in range(0, width, step):
            part = got_ref[g, :, at : at + step]
            got = jnp.dot(hot, part, preferred_element_type=f32).astype(bf16)
            for i in range(2):
                x_ref[i, g * grows : (g + 1) * grows, at : at + step] = got[
                    i * grows : (i + 1) * grows
                ]
        got = jnp.dot(hot, tail, preferred_element_type=f32)
        for i in range(2):
            sel = pick[i : i + 1, :].astype(f32)
            row_gates[i].append(
                jnp.sum(got[i * grows : (i + 1) * grows] * sel, axis=1, keepdims=True)
            )
    loads[0][2].start()
    for i in range(2):
        x = x_ref[i]
        loads[i][0].wait()
        loads[i][1].wait()
        if i == 0:
            loads[1][0].start()
            loads[1][1].start()
        for at in range(0, hidden, step):
            cols = slice(at, at + step)
            gate = jnp.dot(x, wide_ref[i, 0, :, cols], preferred_element_type=f32)
            upv = jnp.dot(x, wide_ref[i, 1, :, cols], preferred_element_type=f32)
            act_ref[:, cols] = (gate / (1.0 + jnp.exp(-gate)) * upv).astype(bf16)
        loads[i][2].wait()
        if i == 0:
            loads[1][2].start()
        row_gate = jnp.concatenate(row_gates[i], 0)
        for at in range(0, width, step):
            cols = slice(at, at + step)
            y = jnp.dot(act_ref[...], down_ref[i, :, cols], preferred_element_type=f32)
            x_ref[i, :, cols] = (y * row_gate).astype(bf16)
    first = 0
    for g, (rows, moves) in enumerate(layouts):
        for at in range(0, width, step):
            cols = slice(at, at + step)
            y = jnp.concatenate(
                [x_ref[i, g * grows : (g + 1) * grows, cols] for i in range(2)], 0
            )
            total = lax.dot_general(hot_ref[g], y, TN, preferred_element_type=f32).astype(bf16)
            for row, count, out, to in moves:
                outs[first + out][to : to + count, cols] = total[row : row + count]
        first += len(rows)


def expert_terms(blocks, sides, mine, weights, cap, nexp):
    planes, per_group = len(blocks), len(blocks[0])
    tokens, wide = blocks[0][0].shape
    _, width, hidden = weights[0].shape
    grows = per_group * cap
    rows = planes * grows
    layouts = [plane_layout(sides, tokens)] * planes
    out_shape = [jax.ShapeDtypeStruct((n, width), bf16) for ns, _ in layouts for n in ns]
    flat = [block for plane in blocks for block in plane]
    take = TAKE if len(flat) == len(TAKE) else tuple(range(len(flat)))
    outs = pl.pallas_call(
        functools.partial(expert_kernel, layouts, take, per_group, tokens, cap, nexp),
        out_shape=out_shape,
        in_specs=[SMEM] + [ANY] * (planes * per_group + len(weights)),
        out_specs=[VMEM] * len(out_shape),
        scratch_shapes=[
            pltpu.VMEM((planes, per_group * tokens, wide), bf16),
            pltpu.VMEM((2, rows, width), bf16),
            pltpu.VMEM((rows, hidden), bf16),
            pltpu.VMEM((planes, 2 * grows, per_group * tokens), bf16),
            pltpu.VMEM((2, 2, width, hidden), bf16),
            pltpu.VMEM((2, hidden, width), bf16),
            pltpu.SemaphoreType.DMA((2, 3)),
            pltpu.SemaphoreType.DMA((planes, per_group)),
        ],
        compiler_params=params(EXPERT_MIB),
        cost_estimate=pl.CostEstimate(
            flops=12 * rows * width * hidden, bytes_accessed=8 * rows * width, transcendentals=0
        ),
        name="experts",
    )(mine, *[flat[i] for i in take], *weights)
    terms, at = [], 0
    for ns, _ in layouts:
        terms.append(outs[at : at + len(ns)])
        at += len(ns)
    return terms


def add(*terms):
    total = terms[0].astype(f32)
    for term in terms[1:]:
        total = total + term.astype(f32)
    return total


def pair_sum(even, odd, later, sides):
    size = even[0].shape[0]
    parts = [slice(i * size, (i + 1) * size) for i in range(sides - 1)]
    over = [swap(odd[3][at], "exp", 2) for at in parts]
    odd_got = [swap(odd[1][at], "seq", 2 * i + 2) for i, at in enumerate(parts)]
    odd_got.append(swap(odd[2], "exp", 1))
    even_got = [swap(even[1][at], "seq", 2 * i + 2) for i, at in enumerate(parts)]
    even_got.append(swap(even[2], "exp", 1))
    if later:
        over, odd_got, later = lax.optimization_barrier((over, odd_got, later))
    over = [add(even[3][at], o).astype(bf16) for at, o in zip(parts, over)]
    even_got += [swap_both(o, 2 * i + 2, 1) for i, o in enumerate(over)]
    return add(even[0], *even_got), add(odd[0], *odd_got), later


def return_terms(terms, sides):
    own = []
    for kz in reversed(range(0, len(terms), 2)):
        even, odd, terms[:kz] = pair_sum(terms[kz], terms[kz + 1], terms[:kz], sides)
        got = swap(odd.astype(bf16), "exp", 2)
        own += [swap(add(even, got).astype(bf16), "exp", 2 * kz)] if kz else [even, got]
    return own


def experts_by_chip(rows, width, weights, nexp):
    nseq, nplace = lax.axis_size("seq"), lax.axis_size("exp")
    cap = 3 * rows.shape[0] * TOPK // (2 * nexp)
    planes, sides = nplace // 2, nseq // 2
    me = lax.axis_index("seq") * nplace + lax.axis_index("exp")
    other = (lax.axis_index("seq") ^ 1) * nplace + lax.axis_index("exp")
    mine = jnp.stack([me, other]).astype(jnp.int32)
    blocks = gather_rows(rows, planes, sides)
    return return_terms(expert_terms(blocks, sides, mine, weights, cap, nexp), sides)


def experts_by_device(rows, width, ids, gate_proj, up_proj, down_proj, nexp):
    tokens = rows.shape[0]
    normed = rows[:, :width]
    gates = rows[:, width : width + nexp].astype(f32) + rows[
        :, width + nexp : width + 2 * nexp
    ].astype(f32)
    gates = jnp.take_along_axis(gates, ids, axis=1)
    capacity = 3 * tokens * TOPK // (2 * nexp)
    flat = ids.reshape(-1)
    member = (flat[:, None] == jnp.arange(nexp, dtype=jnp.int32)[None, :]).astype(jnp.int32)
    rank = jnp.sum((jnp.cumsum(member, axis=0) - 1) * member, axis=1)
    slot = flat * capacity + rank
    place = slot[:, None] == jnp.arange(nexp * capacity, dtype=jnp.int32)[None, :]
    route = jnp.any(place.reshape(tokens, TOPK, nexp * capacity), axis=1).astype(bf16)
    packed = jnp.einsum("ts,td->sd", route, normed, preferred_element_type=f32).astype(bf16)
    outgoing = packed.reshape(nexp, capacity, width)
    taken = lax.all_to_all(outgoing, ("seq", "exp"), split_axis=0, concat_axis=0, tiled=True)
    taken = taken.reshape(-1, width)
    gate = jnp.dot(taken, gate_proj[0], preferred_element_type=f32)
    upv = jnp.dot(taken, up_proj[0], preferred_element_type=f32)
    act = (jax.nn.silu(gate) * upv).astype(bf16)
    result = jnp.dot(act, down_proj[0], preferred_element_type=f32).astype(bf16)
    result = result.reshape(nexp, capacity, width)
    back = lax.all_to_all(result, ("seq", "exp"), split_axis=0, concat_axis=0, tiled=True)
    gathered = back.reshape(nexp * capacity, width)[slot].reshape(tokens, TOPK, width)
    return [jnp.sum(gates[:, :, None] * gathered.astype(f32), axis=1)]


def body(
    queries,
    new_keys,
    new_values,
    cache_keys,
    cache_values,
    cache_len,
    residual_in,
    out_weight,
    norm_gain,
    router_weight,
    expert_ids,
    gate_proj,
    up_proj,
    down_proj,
):
    nseq, nplace = lax.axis_size("seq"), lax.axis_size("exp")
    tokens, width = residual_in.shape[1:]
    nexp = router_weight.shape[1]
    by_chip = nseq * nplace <= 32
    me = lax.axis_index("seq").astype(jnp.int32).reshape(1)
    weights = [gate_proj, up_proj, down_proj]
    parts, pairs = project_attention(
        me,
        cache_len,
        queries[0],
        new_keys[0],
        new_values[0],
        cache_keys[0],
        cache_values[0],
        out_weight,
        weights if by_chip else [],
    )
    mixed, rows = norm_rows(
        residual_in[0], parts, norm_gain, router_weight, expert_ids[0]
    )
    if by_chip:
        rows, pairs = lax.optimization_barrier((rows, pairs))
        terms = experts_by_chip(rows, width, pairs, nexp)
    else:
        terms = experts_by_device(rows, width, expert_ids[0], *weights, nexp)
    return add(mixed, *terms).astype(bf16).reshape(1, tokens, width)


def solution(mesh):
    in_specs = (
        P("exp", "seq", None),
        P("exp", "seq", None),
        P("exp", "seq", None),
        P("exp", "seq", None),
        P("exp", "seq", None),
        P("exp"),
        P("exp", "seq", None),
        P("seq", None),
        P(),
        P(),
        P("exp", "seq", None),
        P(("seq", "exp"), None, None),
        P(("seq", "exp"), None, None),
        P(("seq", "exp"), None, None),
    )
    out_specs = P("exp", "seq", None)
    return jax.shard_map(body, mesh=mesh, in_specs=in_specs, out_specs=out_specs, check_vma=False)
```

```python
import functools
import math

import jax
import jax.numpy as jnp
from jax import lax
from jax.experimental import pallas as pl
from jax.experimental.pallas import tpu as pltpu
from jax.sharding import PartitionSpec as P

QH = 32
KVH = 4
HD = 128
TOPK = 8
MASKED = -1e30
EXPERT_MIB = 46
GATHER = ("c2", "c1", "d0", "y0", "x0", "c3", "d2", "x2", "y2", "y1", "x1", "d1", "y3", "x3", "d3")
TAKE = (3, 14, 4, 9, 13, 11, 7, 2, 12, 8, 1, 0, 15, 6, 5, 10)
NEAR_MIB = 24
FAR_MIB = 24
EXP2_SCALE = math.log2(math.e) / math.sqrt(HD)
NT = (((1,), (1,)), ((), ()))
TN = (((0,), (0,)), ((), ()))
VMEM = pl.BlockSpec(memory_space=pltpu.VMEM)
SMEM = pl.BlockSpec(memory_space=pltpu.SMEM)
ANY = pl.BlockSpec(memory_space=pl.ANY)
f32 = jnp.float32
bf16 = jnp.bfloat16


def swap(rows, axis, bits):
    return lax.ppermute(rows, axis, [(i, i ^ bits) for i in range(lax.axis_size(axis))])


def swap_both(rows, seq_bits, exp_bits):
    nseq, nplace = lax.axis_size("seq"), lax.axis_size("exp")
    bits = seq_bits * nplace + exp_bits
    return lax.ppermute(rows, ("seq", "exp"), [(i, i ^ bits) for i in range(nseq * nplace)])


def params(mib):
    return pltpu.CompilerParams(vmem_limit_bytes=mib << 20)


def pack_kernel(nseq, widths, me_ref, *refs):
    ins, outs, sem = refs[: len(widths)], refs[len(widths) : -1], refs[-1]
    copies = []
    for k in range(nseq):
        dest, to = me_ref[0] ^ k, 0
        for i, cols in enumerate(widths):
            start = dest * cols if ins[i].shape[1] == cols * nseq else dest * KVH // nseq * HD
            start = pl.ds(pl.multiple_of(start, HD), cols)
            pair = ins[i].at[:, start], outs[k].at[:, to : to + cols]
            copies.append(pltpu.make_async_copy(*pair, sem.at[k, i]))
            to += cols
    for copy in copies:
        copy.start()
    for copy in copies:
        copy.wait()


def pack(me, arrays, widths, nseq):
    shape = jax.ShapeDtypeStruct((arrays[0].shape[0], sum(widths)), bf16)
    return pl.pallas_call(
        functools.partial(pack_kernel, nseq, widths),
        out_shape=[shape] * nseq,
        in_specs=[SMEM] + [ANY] * len(arrays),
        out_specs=[VMEM] * nseq,
        scratch_shapes=[pltpu.SemaphoreType.DMA((nseq, len(arrays)))],
        compiler_params=params(61),
        name="pack_heads",
    )(me, *arrays)


def head_rows(heads, start):
    return jnp.concatenate([ref[:, start : start + HD] for ref in heads], 0)


def slot_bias(me, length, ks, slots):
    parts = []
    for k in ks:
        pos = (me ^ k) * slots + lax.broadcasted_iota(jnp.int32, (1, slots), 1)
        parts.append(jnp.where(pos < length, f32(0.0), f32(MASKED)))
    return jnp.concatenate(parts, 1)


def near_kernel(nseq, me_ref, len_ref, *refs):
    heads, caches = refs[:nseq], refs[nseq : nseq + 2]
    peak_ref, sum_ref, acc_ref = refs[nseq + 3 :]
    group = QH // nseq
    qcols = group * HD
    me = me_ref[0]
    slots, tokens = caches[0].shape[0], heads[0].shape[0]
    qtok = nseq * tokens
    bias = slot_bias(me, len_ref[0], (0, 1), slots)
    keys = jnp.concatenate([ref[:, :HD] for ref in caches], 0)
    vals = jnp.concatenate([ref[:, HD:] for ref in caches], 0)
    new_keys, new_vals = head_rows(heads, qcols), head_rows(heads, qcols + HD)
    row = lax.broadcasted_iota(jnp.int32, (qtok, qtok), 0)
    col = lax.broadcasted_iota(jnp.int32, (qtok, qtok), 1)
    qpos = (me ^ (row // tokens)) * tokens + row % tokens
    kpos = (me ^ (col // tokens)) * tokens + col % tokens
    new_bias = jnp.where(kpos <= qpos, f32(0.0), f32(MASKED))
    for g in range(group):
        q = head_rows(heads, g * HD)
        s = lax.dot_general(q, keys, NT, preferred_element_type=f32) + bias
        t = lax.dot_general(q, new_keys, NT, preferred_element_type=f32) + new_bias
        peak = jnp.maximum(jnp.max(s, axis=1, keepdims=True), jnp.max(t, axis=1, keepdims=True))
        p = jnp.exp2((s - peak) * f32(EXP2_SCALE))
        r = jnp.exp2((t - peak) * f32(EXP2_SCALE))
        peak_ref[:, g : g + 1] = peak
        sum_ref[:, g : g + 1] = jnp.sum(p, axis=1, keepdims=True) + jnp.sum(r, axis=1, keepdims=True)
        acc = jnp.dot(p.astype(bf16), vals, preferred_element_type=f32)
        acc += jnp.dot(r.astype(bf16), new_vals, preferred_element_type=f32)
        acc_ref[:, g * HD : (g + 1) * HD] = acc


def far_kernel(nseq, ks, me_ref, len_ref, *refs):
    heads, caches = refs[: len(ks)], refs[len(ks) : len(ks) + nseq - 2]
    peak_ref, sum_ref, acc_ref, w_ref, even_ref, odd_ref, attn_ref = refs[len(ks) + nseq - 2 :]
    group = QH // nseq
    slots, tokens = caches[0].shape[0], heads[0].shape[0]
    mine = slice(ks[0] * tokens, (ks[-1] + 1) * tokens)
    bias = slot_bias(me_ref[0], len_ref[0], range(2, nseq), slots)
    keys = jnp.concatenate([ref[:, :HD] for ref in caches], 0)
    vals = jnp.concatenate([ref[:, HD:] for ref in caches], 0)
    for g in range(group):
        at = slice(g * HD, (g + 1) * HD)
        q = head_rows(heads, g * HD)
        s = lax.dot_general(q, keys, NT, preferred_element_type=f32) + bias
        old = peak_ref[mine, g : g + 1]
        peak = jnp.maximum(jnp.max(s, axis=1, keepdims=True), old)
        fade = jnp.exp2((old - peak) * f32(EXP2_SCALE))
        p = jnp.exp2((s - peak) * f32(EXP2_SCALE))
        total = sum_ref[mine, g : g + 1] * fade + jnp.sum(p, axis=1, keepdims=True)
        acc = acc_ref[mine, at] * fade + jnp.dot(p.astype(bf16), vals, preferred_element_type=f32)
        attn_ref[:, at] = (acc / total).astype(bf16)
    step = 512
    for at in range(0, w_ref.shape[1], step):
        cols = slice(at, at + step)
        total = jnp.dot(attn_ref[...], w_ref[:, cols], preferred_element_type=f32)
        for i in range(len(ks)):
            to = slice(i // 2 * tokens, (i // 2 + 1) * tokens)
            out = odd_ref if i % 2 else even_ref
            out[to, cols] = total[i * tokens : (i + 1) * tokens].astype(out.dtype)


def project_attention(
    me, length, queries, new_keys, new_values, cache_keys, cache_values, out_weight, weights
):
    nseq = lax.axis_size("seq")
    tokens = queries.shape[0]
    width = out_weight.shape[1]
    group = QH // nseq
    qtok = nseq * tokens
    heads = pack(me, (queries, new_keys, new_values), (group * HD, HD, HD), nseq)
    order = sorted(range(1, nseq), reverse=True)
    heads = {0: heads[0]} | {k: swap(heads[k], "seq", k) for k in order}
    others = [swap(w, "seq", 1) for w in weights[:2]]
    held = heads[1], cache_keys, cache_values
    heads[1], cache_keys, cache_values = lax.optimization_barrier(held)
    caches = pack(me, (cache_keys, cache_values), (HD, HD), nseq)
    caches = {0: caches[0], 1: swap(caches[1], "seq", 1)} | dict(enumerate(caches[2:], 2))
    for k in range(2, nseq):
        held = (heads[k], caches[k], others if k == 3 else [])
        heads[k], cache, held = lax.optimization_barrier(held)
        others = held or others
        caches[k] = swap(cache, "seq", k)
    heads = [heads[k] for k in range(nseq)]
    caches = [caches[k] for k in range(nseq)]
    state = pl.pallas_call(
        functools.partial(near_kernel, nseq),
        out_shape=[
            jax.ShapeDtypeStruct((qtok, HD), f32),
            jax.ShapeDtypeStruct((qtok, HD), f32),
            jax.ShapeDtypeStruct((qtok, group * HD), f32),
        ],
        in_specs=[SMEM] * 2 + [VMEM] * (nseq + 3),
        out_specs=[VMEM] * 3,
        compiler_params=params(NEAR_MIB),
        name="attend_near",
    )(me, length, *heads, *caches[:2], out_weight)

    def project(ks, state):
        shape = (len(ks) // 2 * tokens, width)
        return pl.pallas_call(
            functools.partial(far_kernel, nseq, ks),
            out_shape=[jax.ShapeDtypeStruct(shape, f32), jax.ShapeDtypeStruct(shape, bf16)],
            in_specs=[SMEM] * 2 + [VMEM] * (len(ks) + nseq + 2),
            out_specs=[VMEM] * 2,
            scratch_shapes=[pltpu.VMEM((len(ks) * tokens, group * HD), bf16)],
            compiler_params=params(FAR_MIB),
            name="attend_far",
        )(me, length, *[heads[k] for k in ks], *caches[2:], *state, out_weight)

    even, odd = project(list(range(nseq)), state)
    got = swap(odd, "seq", 1)
    got, rest = lax.optimization_barrier((got, weights[2:]))
    others += [swap(w, "seq", 1) for w in rest]
    terms = [even[:tokens], got[:tokens]]
    for at in range(tokens, got.shape[0], tokens):
        both = add(even[at : at + tokens], got[at : at + tokens])
        terms.append(swap(both.astype(bf16), "seq", 2 * at // tokens))
    return terms, [*weights, *others]


def norm_kernel(nterms, res_ref, *refs):
    gain_ref, router_ref, ids_ref, mixed_ref, rows_ref = refs[nterms:]
    tokens, width = res_ref.shape
    mixed = res_ref[...].astype(f32)
    for ref in refs[:nterms]:
        mixed += ref[...].astype(f32)
    mixed_ref[...] = mixed
    meansq = jnp.mean(mixed * mixed, axis=1, keepdims=True)
    normed = (mixed / jnp.sqrt(meansq + 1e-06) * gain_ref[...]).astype(bf16)
    rows_ref[:, :width] = normed
    logits = lax.dot_general(router_ref[...], normed, NT, preferred_element_type=f32)
    nexp = logits.shape[0]
    expert = lax.broadcasted_iota(jnp.int32, (nexp, tokens), 0)
    chosen = expert == ids_ref[0:1, :]
    for k in range(1, ids_ref.shape[0]):
        chosen = jnp.logical_or(chosen, expert == ids_ref[k : k + 1, :])
    expo = jnp.where(chosen, jnp.exp(logits), f32(0.0))
    gates = expo / jnp.sum(expo, axis=0, keepdims=True)
    high = gates.astype(bf16)
    low = (gates - high.astype(f32)).astype(bf16)
    extra = rows_ref.shape[1] - width
    row = lax.broadcasted_iota(jnp.int32, (nexp, extra), 0)
    col = lax.broadcasted_iota(jnp.int32, (nexp, extra), 1)
    spread = lax.dot_general(high, (col == row).astype(bf16), TN, preferred_element_type=f32)
    spread += lax.dot_general(low, (col == row + nexp).astype(bf16), TN, preferred_element_type=f32)
    rows_ref[:, width:] = spread.astype(bf16)


def norm_rows(residual, terms, gain, router, ids):
    tokens, width = residual.shape
    extra = -(-2 * router.shape[1] // 128) * 128
    return pl.pallas_call(
        functools.partial(norm_kernel, len(terms)),
        out_shape=[
            jax.ShapeDtypeStruct((tokens, width), f32),
            jax.ShapeDtypeStruct((tokens, width + extra), bf16),
        ],
        in_specs=[VMEM] * (4 + len(terms)),
        out_specs=[VMEM] * 2,
        compiler_params=params(16),
        name="norm_and_route",
    )(residual, *terms, gain.reshape(1, width), router.T, ids.T)


def gather_rows(rows, planes, sides):
    at = {("c", 0): [rows]}
    steps = [(kind, kz) for kz in range(planes) for kind in "cxyd" if (kind, kz) not in at]
    if planes == 4:
        steps = [(step[0], int(step[1])) for step in GATHER]
    for kind, kz in steps:
        if kind == "x":
            got = [swap(at["c", kz][0], "seq", 2 * kx) for kx in range(1, sides)]
        elif kind == "y":
            got = [swap(at["c", kz][0], "exp", 1)]
        elif kz == 0:
            got = [swap_both(rows, 2 * kx, 1) for kx in range(1, sides)]
        elif kz > 1 and kz % 2:
            got = [swap(block, "exp", 2) for block in at[kind, kz - 1]]
        else:
            got = [swap(block, "exp", 2 * kz) for block in at[kind, 0]]
        at[kind, kz] = got
    return [[block for kind in "cxyd" for block in at[kind, kz]] for kz in range(planes)]


def plane_layout(sides, tokens):
    rows = [tokens, (sides - 1) * tokens, tokens, (sides - 1) * tokens]
    moves = []
    for ky in range(2):
        for kx in range(sides):
            to = (2 * ky + (kx > 0), max(kx - 1, 0) * tokens)
            moves.append(((ky * sides + kx) * tokens, tokens, *to))
    return rows, moves


def expert_kernel(layouts, take, per_group, tokens, cap, nexp, mine_ref, *refs):
    planes = len(layouts)
    pieces = planes * per_group
    blocks = [refs[take.index(i)] for i in range(pieces)]
    weights = (refs[pieces : pieces + 3], refs[pieces + 3 : pieces + 6])
    nouts = sum(len(rows) for rows, _ in layouts)
    outs = refs[pieces + 6 : pieces + 6 + nouts]
    got_ref, x_ref, act_ref, hot_ref, wide_ref, down_ref, sem, got_sem = refs[pieces + 6 + nouts :]
    copies = [
        pltpu.make_async_copy(
            blocks[g * per_group + i],
            got_ref.at[g, i * tokens : (i + 1) * tokens],
            got_sem.at[g, i],
        )
        for g in range(planes)
        for i in range(per_group)
    ]
    for copy in copies:
        copy.start()
    loads = [
        [
            pltpu.make_async_copy(ws[0].at[0], wide_ref.at[i, 0], sem.at[i, 0]),
            pltpu.make_async_copy(ws[1].at[0], wide_ref.at[i, 1], sem.at[i, 1]),
            pltpu.make_async_copy(ws[2].at[0], down_ref.at[i], sem.at[i, 2]),
        ]
        for i, ws in enumerate(weights)
    ]
    loads[0][0].start()
    loads[0][1].start()
    width = x_ref.shape[2]
    hidden = act_ref.shape[1]
    ext = got_ref.shape[2] - width
    gtok = per_group * tokens
    grows = per_group * cap
    step = 256
    ecol = lax.broadcasted_iota(jnp.int32, (8, ext), 1)
    erow = lax.broadcasted_iota(jnp.int32, (8, ext), 0)
    want = jnp.where(erow == 0, mine_ref[0], jnp.where(erow == 1, mine_ref[1], -ext))
    pick = jnp.logical_or(ecol == want, ecol == want + nexp).astype(bf16)
    trow = lax.broadcasted_iota(jnp.int32, (gtok, gtok), 0)
    tcol = lax.broadcasted_iota(jnp.int32, (gtok, gtok), 1)
    before = jnp.logical_and(trow < tcol, trow // tokens == tcol // tokens).astype(bf16)
    block = lax.broadcasted_iota(jnp.int32, (8, gtok), 1) // tokens
    slot = lax.broadcasted_iota(jnp.int32, (grows, gtok), 0).astype(f32)
    row_gates = [[], []]
    for g in range(planes):
        for copy in copies[g * per_group : (g + 1) * per_group]:
            copy.wait()
        tail = got_ref[g, :, width:]
        gates = lax.dot_general(pick, tail, NT, preferred_element_type=f32)
        chosen = gates > 0.0
        rank = jnp.dot(chosen.astype(bf16), before, preferred_element_type=f32)
        target = jnp.where(chosen, (block * cap).astype(f32) + rank, f32(-1.0))
        hot = jnp.concatenate(
            [(slot == target[i : i + 1, :]).astype(f32) for i in range(2)], 0
        ).astype(bf16)
        hot_ref[g] = hot
        for at in range(0, width, step):
            part = got_ref[g, :, at : at + step]
            got = jnp.dot(hot, part, preferred_element_type=f32).astype(bf16)
            for i in range(2):
                x_ref[i, g * grows : (g + 1) * grows, at : at + step] = got[
                    i * grows : (i + 1) * grows
                ]
        got = jnp.dot(hot, tail, preferred_element_type=f32)
        for i in range(2):
            sel = pick[i : i + 1, :].astype(f32)
            row_gates[i].append(
                jnp.sum(got[i * grows : (i + 1) * grows] * sel, axis=1, keepdims=True)
            )
    loads[0][2].start()
    for i in range(2):
        x = x_ref[i]
        loads[i][0].wait()
        loads[i][1].wait()
        if i == 0:
            loads[1][0].start()
            loads[1][1].start()
        for at in range(0, hidden, step):
            cols = slice(at, at + step)
            gate = jnp.dot(x, wide_ref[i, 0, :, cols], preferred_element_type=f32)
            upv = jnp.dot(x, wide_ref[i, 1, :, cols], preferred_element_type=f32)
            act_ref[:, cols] = (gate / (1.0 + jnp.exp(-gate)) * upv).astype(bf16)
        loads[i][2].wait()
        if i == 0:
            loads[1][2].start()
        row_gate = jnp.concatenate(row_gates[i], 0)
        for at in range(0, width, step):
            cols = slice(at, at + step)
            y = jnp.dot(act_ref[...], down_ref[i, :, cols], preferred_element_type=f32)
            x_ref[i, :, cols] = (y * row_gate).astype(bf16)
    first = 0
    for g, (rows, moves) in enumerate(layouts):
        for at in range(0, width, step):
            cols = slice(at, at + step)
            y = jnp.concatenate(
                [x_ref[i, g * grows : (g + 1) * grows, cols] for i in range(2)], 0
            )
            total = lax.dot_general(hot_ref[g], y, TN, preferred_element_type=f32).astype(bf16)
            for row, count, out, to in moves:
                outs[first + out][to : to + count, cols] = total[row : row + count]
        first += len(rows)


def expert_terms(blocks, sides, mine, weights, cap, nexp):
    planes, per_group = len(blocks), len(blocks[0])
    tokens, wide = blocks[0][0].shape
    _, width, hidden = weights[0].shape
    grows = per_group * cap
    rows = planes * grows
    layouts = [plane_layout(sides, tokens)] * planes
    out_shape = [jax.ShapeDtypeStruct((n, width), bf16) for ns, _ in layouts for n in ns]
    flat = [block for plane in blocks for block in plane]
    take = TAKE if len(flat) == len(TAKE) else tuple(range(len(flat)))
    outs = pl.pallas_call(
        functools.partial(expert_kernel, layouts, take, per_group, tokens, cap, nexp),
        out_shape=out_shape,
        in_specs=[SMEM] + [ANY] * (planes * per_group + len(weights)),
        out_specs=[VMEM] * len(out_shape),
        scratch_shapes=[
            pltpu.VMEM((planes, per_group * tokens, wide), bf16),
            pltpu.VMEM((2, rows, width), bf16),
            pltpu.VMEM((rows, hidden), bf16),
            pltpu.VMEM((planes, 2 * grows, per_group * tokens), bf16),
            pltpu.VMEM((2, 2, width, hidden), bf16),
            pltpu.VMEM((2, hidden, width), bf16),
            pltpu.SemaphoreType.DMA((2, 3)),
            pltpu.SemaphoreType.DMA((planes, per_group)),
        ],
        compiler_params=params(EXPERT_MIB),
        cost_estimate=pl.CostEstimate(
            flops=12 * rows * width * hidden, bytes_accessed=8 * rows * width, transcendentals=0
        ),
        name="experts",
    )(mine, *[flat[i] for i in take], *weights)
    terms, at = [], 0
    for ns, _ in layouts:
        terms.append(outs[at : at + len(ns)])
        at += len(ns)
    return terms


def add(*terms):
    total = terms[0].astype(f32)
    for term in terms[1:]:
        total = total + term.astype(f32)
    return total


def pair_sum(even, odd, later, sides):
    size = even[0].shape[0]
    parts = [slice(i * size, (i + 1) * size) for i in range(sides - 1)]
    over = [swap(odd[3][at], "exp", 2) for at in parts]
    odd_got = [swap(odd[1][at], "seq", 2 * i + 2) for i, at in enumerate(parts)]
    odd_got.append(swap(odd[2], "exp", 1))
    even_got = [swap(even[1][at], "seq", 2 * i + 2) for i, at in enumerate(parts)]
    even_got.append(swap(even[2], "exp", 1))
    if later:
        over, odd_got, later = lax.optimization_barrier((over, odd_got, later))
    over = [add(even[3][at], o).astype(bf16) for at, o in zip(parts, over)]
    even_got += [swap_both(o, 2 * i + 2, 1) for i, o in enumerate(over)]
    return add(even[0], *even_got), add(odd[0], *odd_got), later


def return_terms(terms, sides):
    own = []
    for kz in reversed(range(0, len(terms), 2)):
        even, odd, terms[:kz] = pair_sum(terms[kz], terms[kz + 1], terms[:kz], sides)
        got = swap(odd.astype(bf16), "exp", 2)
        own += [swap(add(even, got).astype(bf16), "exp", 2 * kz)] if kz else [even, got]
    return own


def experts_by_chip(rows, width, weights, nexp):
    nseq, nplace = lax.axis_size("seq"), lax.axis_size("exp")
    cap = 3 * rows.shape[0] * TOPK // (2 * nexp)
    planes, sides = nplace // 2, nseq // 2
    me = lax.axis_index("seq") * nplace + lax.axis_index("exp")
    other = (lax.axis_index("seq") ^ 1) * nplace + lax.axis_index("exp")
    mine = jnp.stack([me, other]).astype(jnp.int32)
    blocks = gather_rows(rows, planes, sides)
    return return_terms(expert_terms(blocks, sides, mine, weights, cap, nexp), sides)


def experts_by_device(rows, width, ids, gate_proj, up_proj, down_proj, nexp):
    tokens = rows.shape[0]
    normed = rows[:, :width]
    gates = rows[:, width : width + nexp].astype(f32) + rows[
        :, width + nexp : width + 2 * nexp
    ].astype(f32)
    gates = jnp.take_along_axis(gates, ids, axis=1)
    capacity = 3 * tokens * TOPK // (2 * nexp)
    flat = ids.reshape(-1)
    member = (flat[:, None] == jnp.arange(nexp, dtype=jnp.int32)[None, :]).astype(jnp.int32)
    rank = jnp.sum((jnp.cumsum(member, axis=0) - 1) * member, axis=1)
    slot = flat * capacity + rank
    place = slot[:, None] == jnp.arange(nexp * capacity, dtype=jnp.int32)[None, :]
    route = jnp.any(place.reshape(tokens, TOPK, nexp * capacity), axis=1).astype(bf16)
    packed = jnp.einsum("ts,td->sd", route, normed, preferred_element_type=f32).astype(bf16)
    outgoing = packed.reshape(nexp, capacity, width)
    taken = lax.all_to_all(outgoing, ("seq", "exp"), split_axis=0, concat_axis=0, tiled=True)
    taken = taken.reshape(-1, width)
    gate = jnp.dot(taken, gate_proj[0], preferred_element_type=f32)
    upv = jnp.dot(taken, up_proj[0], preferred_element_type=f32)
    act = (jax.nn.silu(gate) * upv).astype(bf16)
    result = jnp.dot(act, down_proj[0], preferred_element_type=f32).astype(bf16)
    result = result.reshape(nexp, capacity, width)
    back = lax.all_to_all(result, ("seq", "exp"), split_axis=0, concat_axis=0, tiled=True)
    gathered = back.reshape(nexp * capacity, width)[slot].reshape(tokens, TOPK, width)
    return [jnp.sum(gates[:, :, None] * gathered.astype(f32), axis=1)]


def body(
    queries,
    new_keys,
    new_values,
    cache_keys,
    cache_values,
    cache_len,
    residual_in,
    out_weight,
    norm_gain,
    router_weight,
    expert_ids,
    gate_proj,
    up_proj,
    down_proj,
):
    nseq, nplace = lax.axis_size("seq"), lax.axis_size("exp")
    tokens, width = residual_in.shape[1:]
    nexp = router_weight.shape[1]
    by_chip = nseq * nplace <= 32
    me = lax.axis_index("seq").astype(jnp.int32).reshape(1)
    weights = [gate_proj, up_proj, down_proj]
    parts, pairs = project_attention(
        me,
        cache_len,
        queries[0],
        new_keys[0],
        new_values[0],
        cache_keys[0],
        cache_values[0],
        out_weight,
        weights if by_chip else [],
    )
    mixed, rows = norm_rows(
        residual_in[0], parts, norm_gain, router_weight, expert_ids[0]
    )
    if by_chip:
        rows, pairs = lax.optimization_barrier((rows, pairs))
        terms = experts_by_chip(rows, width, pairs, nexp)
    else:
        terms = experts_by_device(rows, width, expert_ids[0], *weights, nexp)
    return add(mixed, *terms).astype(bf16).reshape(1, tokens, width)


def solution(mesh):
    in_specs = (
        P("exp", "seq", None),
        P("exp", "seq", None),
        P("exp", "seq", None),
        P("exp", "seq", None),
        P("exp", "seq", None),
        P("exp"),
        P("exp", "seq", None),
        P("seq", None),
        P(),
        P(),
        P("exp", "seq", None),
        P(("seq", "exp"), None, None),
        P(("seq", "exp"), None, None),
        P(("seq", "exp"), None, None),
    )
    out_specs = P("exp", "seq", None)
    return jax.shard_map(body, mesh=mesh, in_specs=in_specs, out_specs=out_specs, check_vma=False)
```

```python
import functools
import math

import jax
import jax.numpy as jnp
from jax import lax
from jax.experimental import pallas as pl
from jax.experimental.pallas import tpu as pltpu
from jax.sharding import PartitionSpec as P

QH = 32
KVH = 4
HD = 128
TOPK = 8
MASKED = -1e30
EXPERT_MIB = 46
GATHER = ("c2", "c1", "d0", "y0", "x0", "c3", "d2", "x2", "y2", "y1", "x1", "d1", "y3", "x3", "d3")
TAKE = (3, 14, 4, 9, 13, 11, 7, 2, 0, 8, 1, 15, 12, 6, 5, 10)
NEAR_MIB = 14
FAR_MIB = 14
EXP2_SCALE = math.log2(math.e) / math.sqrt(HD)
NT = (((1,), (1,)), ((), ()))
TN = (((0,), (0,)), ((), ()))
VMEM = pl.BlockSpec(memory_space=pltpu.VMEM)
SMEM = pl.BlockSpec(memory_space=pltpu.SMEM)
ANY = pl.BlockSpec(memory_space=pl.ANY)
f32 = jnp.float32
bf16 = jnp.bfloat16


def swap(rows, axis, bits):
    return lax.ppermute(rows, axis, [(i, i ^ bits) for i in range(lax.axis_size(axis))])


def swap_both(rows, seq_bits, exp_bits):
    nseq, nplace = lax.axis_size("seq"), lax.axis_size("exp")
    bits = seq_bits * nplace + exp_bits
    return lax.ppermute(rows, ("seq", "exp"), [(i, i ^ bits) for i in range(nseq * nplace)])


def params(mib):
    return pltpu.CompilerParams(vmem_limit_bytes=mib << 20)


def pack_kernel(nseq, widths, me_ref, *refs):
    ins, outs, sem = refs[: len(widths)], refs[len(widths) : -1], refs[-1]
    copies = []
    for k in range(nseq):
        dest, to = me_ref[0] ^ k, 0
        for i, cols in enumerate(widths):
            start = dest * cols if ins[i].shape[1] == cols * nseq else dest * KVH // nseq * HD
            start = pl.ds(pl.multiple_of(start, HD), cols)
            pair = ins[i].at[:, start], outs[k].at[:, to : to + cols]
            copies.append(pltpu.make_async_copy(*pair, sem.at[k, i]))
            to += cols
    for copy in copies:
        copy.start()
    for copy in copies:
        copy.wait()


def pack(me, arrays, widths, nseq):
    shape = jax.ShapeDtypeStruct((arrays[0].shape[0], sum(widths)), bf16)
    return pl.pallas_call(
        functools.partial(pack_kernel, nseq, widths),
        out_shape=[shape] * nseq,
        in_specs=[SMEM] + [ANY] * len(arrays),
        out_specs=[VMEM] * nseq,
        scratch_shapes=[pltpu.SemaphoreType.DMA((nseq, len(arrays)))],
        compiler_params=params(61),
        name="pack_heads",
    )(me, *arrays)


def head_rows(heads, start):
    return jnp.concatenate([ref[:, start : start + HD] for ref in heads], 0)


def slot_bias(me, length, ks, slots):
    parts = []
    for k in ks:
        pos = (me ^ k) * slots + lax.broadcasted_iota(jnp.int32, (1, slots), 1)
        parts.append(jnp.where(pos < length, f32(0.0), f32(MASKED)))
    return jnp.concatenate(parts, 1)


def near_kernel(nseq, me_ref, len_ref, *refs):
    heads, caches = refs[:nseq], refs[nseq : nseq + 2]
    peak_ref, sum_ref, acc_ref = refs[nseq + 3 :]
    group = QH // nseq
    qcols = group * HD
    me = me_ref[0]
    slots, tokens = caches[0].shape[0], heads[0].shape[0]
    qtok = nseq * tokens
    bias = slot_bias(me, len_ref[0], (0, 1), slots)
    keys = jnp.concatenate([ref[:, :HD] for ref in caches], 0)
    vals = jnp.concatenate([ref[:, HD:] for ref in caches], 0)
    new_keys, new_vals = head_rows(heads, qcols), head_rows(heads, qcols + HD)
    row = lax.broadcasted_iota(jnp.int32, (qtok, qtok), 0)
    col = lax.broadcasted_iota(jnp.int32, (qtok, qtok), 1)
    qpos = (me ^ (row // tokens)) * tokens + row % tokens
    kpos = (me ^ (col // tokens)) * tokens + col % tokens
    new_bias = jnp.where(kpos <= qpos, f32(0.0), f32(MASKED))
    for g in range(group):
        q = head_rows(heads, g * HD)
        s = lax.dot_general(q, keys, NT, preferred_element_type=f32) + bias
        t = lax.dot_general(q, new_keys, NT, preferred_element_type=f32) + new_bias
        peak = jnp.maximum(jnp.max(s, axis=1, keepdims=True), jnp.max(t, axis=1, keepdims=True))
        p = jnp.exp2((s - peak) * f32(EXP2_SCALE))
        r = jnp.exp2((t - peak) * f32(EXP2_SCALE))
        peak_ref[:, g : g + 1] = peak
        sum_ref[:, g : g + 1] = jnp.sum(p, axis=1, keepdims=True) + jnp.sum(r, axis=1, keepdims=True)
        acc = jnp.dot(p.astype(bf16), vals, preferred_element_type=f32)
        acc += jnp.dot(r.astype(bf16), new_vals, preferred_element_type=f32)
        acc_ref[:, g * HD : (g + 1) * HD] = acc


def far_kernel(nseq, ks, me_ref, len_ref, *refs):
    heads, caches = refs[: len(ks)], refs[len(ks) : len(ks) + nseq - 2]
    peak_ref, sum_ref, acc_ref, w_ref, even_ref, odd_ref, attn_ref = refs[len(ks) + nseq - 2 :]
    group = QH // nseq
    slots, tokens = caches[0].shape[0], heads[0].shape[0]
    mine = slice(ks[0] * tokens, (ks[-1] + 1) * tokens)
    bias = slot_bias(me_ref[0], len_ref[0], range(2, nseq), slots)
    keys = jnp.concatenate([ref[:, :HD] for ref in caches], 0)
    vals = jnp.concatenate([ref[:, HD:] for ref in caches], 0)
    for g in range(group):
        at = slice(g * HD, (g + 1) * HD)
        q = head_rows(heads, g * HD)
        s = lax.dot_general(q, keys, NT, preferred_element_type=f32) + bias
        old = peak_ref[mine, g : g + 1]
        peak = jnp.maximum(jnp.max(s, axis=1, keepdims=True), old)
        fade = jnp.exp2((old - peak) * f32(EXP2_SCALE))
        p = jnp.exp2((s - peak) * f32(EXP2_SCALE))
        total = sum_ref[mine, g : g + 1] * fade + jnp.sum(p, axis=1, keepdims=True)
        acc = acc_ref[mine, at] * fade + jnp.dot(p.astype(bf16), vals, preferred_element_type=f32)
        attn_ref[:, at] = (acc / total).astype(bf16)
    step = 512
    for at in range(0, w_ref.shape[1], step):
        cols = slice(at, at + step)
        total = jnp.dot(attn_ref[...], w_ref[:, cols], preferred_element_type=f32)
        for i in range(len(ks)):
            to = slice(i // 2 * tokens, (i // 2 + 1) * tokens)
            out = odd_ref if i % 2 else even_ref
            out[to, cols] = total[i * tokens : (i + 1) * tokens].astype(out.dtype)


def project_attention(
    me, length, queries, new_keys, new_values, cache_keys, cache_values, out_weight, weights
):
    nseq = lax.axis_size("seq")
    tokens = queries.shape[0]
    width = out_weight.shape[1]
    group = QH // nseq
    qtok = nseq * tokens
    heads = pack(me, (queries, new_keys, new_values), (group * HD, HD, HD), nseq)
    order = sorted(range(1, nseq), reverse=True)
    heads = {0: heads[0]} | {k: swap(heads[k], "seq", k) for k in order}
    others = [swap(w, "seq", 1) for w in weights[:2]]
    held = heads[1], cache_keys, cache_values
    heads[1], cache_keys, cache_values = lax.optimization_barrier(held)
    caches = pack(me, (cache_keys, cache_values), (HD, HD), nseq)
    caches = {0: caches[0], 1: swap(caches[1], "seq", 1)} | dict(enumerate(caches[2:], 2))
    for k in range(2, nseq):
        held = (heads[k], caches[k], others if k == 3 else [])
        heads[k], cache, held = lax.optimization_barrier(held)
        others = held or others
        caches[k] = swap(cache, "seq", k)
    heads = [heads[k] for k in range(nseq)]
    caches = [caches[k] for k in range(nseq)]
    state = pl.pallas_call(
        functools.partial(near_kernel, nseq),
        out_shape=[
            jax.ShapeDtypeStruct((qtok, HD), f32),
            jax.ShapeDtypeStruct((qtok, HD), f32),
            jax.ShapeDtypeStruct((qtok, group * HD), f32),
        ],
        in_specs=[SMEM] * 2 + [VMEM] * (nseq + 3),
        out_specs=[VMEM] * 3,
        compiler_params=params(NEAR_MIB),
        name="attend_near",
    )(me, length, *heads, *caches[:2], out_weight)

    def project(ks, state):
        shape = (len(ks) // 2 * tokens, width)
        return pl.pallas_call(
            functools.partial(far_kernel, nseq, ks),
            out_shape=[jax.ShapeDtypeStruct(shape, f32), jax.ShapeDtypeStruct(shape, bf16)],
            in_specs=[SMEM] * 2 + [VMEM] * (len(ks) + nseq + 2),
            out_specs=[VMEM] * 2,
            scratch_shapes=[pltpu.VMEM((len(ks) * tokens, group * HD), bf16)],
            compiler_params=params(FAR_MIB),
            name="attend_far",
        )(me, length, *[heads[k] for k in ks], *caches[2:], *state, out_weight)

    even, odd = project(list(range(nseq)), state)
    got = swap(odd, "seq", 1)
    got, rest = lax.optimization_barrier((got, weights[2:]))
    others += [swap(w, "seq", 1) for w in rest]
    terms = [even[:tokens], got[:tokens]]
    for at in range(tokens, got.shape[0], tokens):
        both = add(even[at : at + tokens], got[at : at + tokens])
        terms.append(swap(both.astype(bf16), "seq", 2 * at // tokens))
    return terms, [*weights, *others]


def norm_kernel(nterms, res_ref, *refs):
    gain_ref, router_ref, ids_ref, mixed_ref, rows_ref = refs[nterms:]
    tokens, width = res_ref.shape
    mixed = res_ref[...].astype(f32)
    for ref in refs[:nterms]:
        mixed += ref[...].astype(f32)
    mixed_ref[...] = mixed
    meansq = jnp.mean(mixed * mixed, axis=1, keepdims=True)
    normed = (mixed / jnp.sqrt(meansq + 1e-06) * gain_ref[...]).astype(bf16)
    rows_ref[:, :width] = normed
    logits = lax.dot_general(router_ref[...], normed, NT, preferred_element_type=f32)
    nexp = logits.shape[0]
    expert = lax.broadcasted_iota(jnp.int32, (nexp, tokens), 0)
    chosen = expert == ids_ref[0:1, :]
    for k in range(1, ids_ref.shape[0]):
        chosen = jnp.logical_or(chosen, expert == ids_ref[k : k + 1, :])
    expo = jnp.where(chosen, jnp.exp(logits), f32(0.0))
    gates = expo / jnp.sum(expo, axis=0, keepdims=True)
    high = gates.astype(bf16)
    low = (gates - high.astype(f32)).astype(bf16)
    extra = rows_ref.shape[1] - width
    row = lax.broadcasted_iota(jnp.int32, (nexp, extra), 0)
    col = lax.broadcasted_iota(jnp.int32, (nexp, extra), 1)
    spread = lax.dot_general(high, (col == row).astype(bf16), TN, preferred_element_type=f32)
    spread += lax.dot_general(low, (col == row + nexp).astype(bf16), TN, preferred_element_type=f32)
    rows_ref[:, width:] = spread.astype(bf16)


def norm_rows(residual, terms, gain, router, ids):
    tokens, width = residual.shape
    extra = -(-2 * router.shape[1] // 128) * 128
    return pl.pallas_call(
        functools.partial(norm_kernel, len(terms)),
        out_shape=[
            jax.ShapeDtypeStruct((tokens, width), f32),
            jax.ShapeDtypeStruct((tokens, width + extra), bf16),
        ],
        in_specs=[VMEM] * (4 + len(terms)),
        out_specs=[VMEM] * 2,
        compiler_params=params(16),
        name="norm_and_route",
    )(residual, *terms, gain.reshape(1, width), router.T, ids.T)


def gather_rows(rows, planes, sides):
    at = {("c", 0): [rows]}
    steps = [(kind, kz) for kz in range(planes) for kind in "cxyd" if (kind, kz) not in at]
    if planes == 4:
        steps = [(step[0], int(step[1])) for step in GATHER]
    for kind, kz in steps:
        if kind == "x":
            got = [swap(at["c", kz][0], "seq", 2 * kx) for kx in range(1, sides)]
        elif kind == "y":
            got = [swap(at["c", kz][0], "exp", 1)]
        elif kz == 0:
            got = [swap_both(rows, 2 * kx, 1) for kx in range(1, sides)]
        elif kz > 1 and kz % 2:
            got = [swap(block, "exp", 2) for block in at[kind, kz - 1]]
        else:
            got = [swap(block, "exp", 2 * kz) for block in at[kind, 0]]
        at[kind, kz] = got
    return [[block for kind in "cxyd" for block in at[kind, kz]] for kz in range(planes)]


def plane_layout(sides, tokens):
    rows = [tokens, (sides - 1) * tokens, tokens, (sides - 1) * tokens]
    moves = []
    for ky in range(2):
        for kx in range(sides):
            to = (2 * ky + (kx > 0), max(kx - 1, 0) * tokens)
            moves.append(((ky * sides + kx) * tokens, tokens, *to))
    return rows, moves


def expert_kernel(layouts, take, per_group, tokens, cap, nexp, mine_ref, *refs):
    planes = len(layouts)
    pieces = planes * per_group
    blocks = [refs[take.index(i)] for i in range(pieces)]
    weights = (refs[pieces : pieces + 3], refs[pieces + 3 : pieces + 6])
    nouts = sum(len(rows) for rows, _ in layouts)
    outs = refs[pieces + 6 : pieces + 6 + nouts]
    got_ref, x_ref, act_ref, hot_ref, wide_ref, down_ref, sem, got_sem = refs[pieces + 6 + nouts :]
    copies = [
        pltpu.make_async_copy(
            blocks[g * per_group + i],
            got_ref.at[g, i * tokens : (i + 1) * tokens],
            got_sem.at[g, i],
        )
        for g in range(planes)
        for i in range(per_group)
    ]
    for copy in copies:
        copy.start()
    loads = [
        [
            pltpu.make_async_copy(ws[0].at[0], wide_ref.at[i, 0], sem.at[i, 0]),
            pltpu.make_async_copy(ws[1].at[0], wide_ref.at[i, 1], sem.at[i, 1]),
            pltpu.make_async_copy(ws[2].at[0], down_ref.at[i], sem.at[i, 2]),
        ]
        for i, ws in enumerate(weights)
    ]
    loads[0][0].start()
    loads[0][1].start()
    width = x_ref.shape[2]
    hidden = act_ref.shape[1]
    ext = got_ref.shape[2] - width
    gtok = per_group * tokens
    grows = per_group * cap
    step = 256
    ecol = lax.broadcasted_iota(jnp.int32, (8, ext), 1)
    erow = lax.broadcasted_iota(jnp.int32, (8, ext), 0)
    want = jnp.where(erow == 0, mine_ref[0], jnp.where(erow == 1, mine_ref[1], -ext))
    pick = jnp.logical_or(ecol == want, ecol == want + nexp).astype(bf16)
    trow = lax.broadcasted_iota(jnp.int32, (gtok, gtok), 0)
    tcol = lax.broadcasted_iota(jnp.int32, (gtok, gtok), 1)
    before = jnp.logical_and(trow < tcol, trow // tokens == tcol // tokens).astype(bf16)
    block = lax.broadcasted_iota(jnp.int32, (8, gtok), 1) // tokens
    slot = lax.broadcasted_iota(jnp.int32, (grows, gtok), 0).astype(f32)
    row_gates = [[], []]
    for g in range(planes):
        for copy in copies[g * per_group : (g + 1) * per_group]:
            copy.wait()
        tail = got_ref[g, :, width:]
        gates = lax.dot_general(pick, tail, NT, preferred_element_type=f32)
        chosen = gates > 0.0
        rank = jnp.dot(chosen.astype(bf16), before, preferred_element_type=f32)
        target = jnp.where(chosen, (block * cap).astype(f32) + rank, f32(-1.0))
        hot = jnp.concatenate(
            [(slot == target[i : i + 1, :]).astype(f32) for i in range(2)], 0
        ).astype(bf16)
        hot_ref[g] = hot
        for at in range(0, width, step):
            part = got_ref[g, :, at : at + step]
            got = jnp.dot(hot, part, preferred_element_type=f32).astype(bf16)
            for i in range(2):
                x_ref[i, g * grows : (g + 1) * grows, at : at + step] = got[
                    i * grows : (i + 1) * grows
                ]
        got = jnp.dot(hot, tail, preferred_element_type=f32)
        for i in range(2):
            sel = pick[i : i + 1, :].astype(f32)
            row_gates[i].append(
                jnp.sum(got[i * grows : (i + 1) * grows] * sel, axis=1, keepdims=True)
            )
    loads[0][2].start()
    for i in range(2):
        x = x_ref[i]
        loads[i][0].wait()
        loads[i][1].wait()
        if i == 0:
            loads[1][0].start()
            loads[1][1].start()
        for at in range(0, hidden, step):
            cols = slice(at, at + step)
            gate = jnp.dot(x, wide_ref[i, 0, :, cols], preferred_element_type=f32)
            upv = jnp.dot(x, wide_ref[i, 1, :, cols], preferred_element_type=f32)
            act_ref[:, cols] = (gate / (1.0 + jnp.exp(-gate)) * upv).astype(bf16)
        loads[i][2].wait()
        if i == 0:
            loads[1][2].start()
        row_gate = jnp.concatenate(row_gates[i], 0)
        for at in range(0, width, step):
            cols = slice(at, at + step)
            y = jnp.dot(act_ref[...], down_ref[i, :, cols], preferred_element_type=f32)
            x_ref[i, :, cols] = (y * row_gate).astype(bf16)
    first = 0
    for g, (rows, moves) in enumerate(layouts):
        for at in range(0, width, step):
            cols = slice(at, at + step)
            y = jnp.concatenate(
                [x_ref[i, g * grows : (g + 1) * grows, cols] for i in range(2)], 0
            )
            total = lax.dot_general(hot_ref[g], y, TN, preferred_element_type=f32).astype(bf16)
            for row, count, out, to in moves:
                outs[first + out][to : to + count, cols] = total[row : row + count]
        first += len(rows)


def expert_terms(blocks, sides, mine, weights, cap, nexp):
    planes, per_group = len(blocks), len(blocks[0])
    tokens, wide = blocks[0][0].shape
    _, width, hidden = weights[0].shape
    grows = per_group * cap
    rows = planes * grows
    layouts = [plane_layout(sides, tokens)] * planes
    out_shape = [jax.ShapeDtypeStruct((n, width), bf16) for ns, _ in layouts for n in ns]
    flat = [block for plane in blocks for block in plane]
    take = TAKE if len(flat) == len(TAKE) else tuple(range(len(flat)))
    outs = pl.pallas_call(
        functools.partial(expert_kernel, layouts, take, per_group, tokens, cap, nexp),
        out_shape=out_shape,
        in_specs=[SMEM] + [ANY] * (planes * per_group + len(weights)),
        out_specs=[VMEM] * len(out_shape),
        scratch_shapes=[
            pltpu.VMEM((planes, per_group * tokens, wide), bf16),
            pltpu.VMEM((2, rows, width), bf16),
            pltpu.VMEM((rows, hidden), bf16),
            pltpu.VMEM((planes, 2 * grows, per_group * tokens), bf16),
            pltpu.VMEM((2, 2, width, hidden), bf16),
            pltpu.VMEM((2, hidden, width), bf16),
            pltpu.SemaphoreType.DMA((2, 3)),
            pltpu.SemaphoreType.DMA((planes, per_group)),
        ],
        compiler_params=params(EXPERT_MIB),
        cost_estimate=pl.CostEstimate(
            flops=12 * rows * width * hidden, bytes_accessed=8 * rows * width, transcendentals=0
        ),
        name="experts",
    )(mine, *[flat[i] for i in take], *weights)
    terms, at = [], 0
    for ns, _ in layouts:
        terms.append(outs[at : at + len(ns)])
        at += len(ns)
    return terms


def add(*terms):
    total = terms[0].astype(f32)
    for term in terms[1:]:
        total = total + term.astype(f32)
    return total


def pair_sum(even, odd, later, sides):
    size = even[0].shape[0]
    parts = [slice(i * size, (i + 1) * size) for i in range(sides - 1)]
    over = [swap(odd[3][at], "exp", 2) for at in parts]
    odd_got = [swap(odd[1][at], "seq", 2 * i + 2) for i, at in enumerate(parts)]
    odd_got.append(swap(odd[2], "exp", 1))
    even_got = [swap(even[1][at], "seq", 2 * i + 2) for i, at in enumerate(parts)]
    even_got.append(swap(even[2], "exp", 1))
    if later:
        over, odd_got, later = lax.optimization_barrier((over, odd_got, later))
    over = [add(even[3][at], o).astype(bf16) for at, o in zip(parts, over)]
    even_got += [swap_both(o, 2 * i + 2, 1) for i, o in enumerate(over)]
    return add(even[0], *even_got), add(odd[0], *odd_got), later


def return_terms(terms, sides):
    own = []
    for kz in reversed(range(0, len(terms), 2)):
        even, odd, terms[:kz] = pair_sum(terms[kz], terms[kz + 1], terms[:kz], sides)
        got = swap(odd.astype(bf16), "exp", 2)
        own += [swap(add(even, got).astype(bf16), "exp", 2 * kz)] if kz else [even, got]
    return own


def experts_by_chip(rows, width, weights, nexp):
    nseq, nplace = lax.axis_size("seq"), lax.axis_size("exp")
    cap = 3 * rows.shape[0] * TOPK // (2 * nexp)
    planes, sides = nplace // 2, nseq // 2
    me = lax.axis_index("seq") * nplace + lax.axis_index("exp")
    other = (lax.axis_index("seq") ^ 1) * nplace + lax.axis_index("exp")
    mine = jnp.stack([me, other]).astype(jnp.int32)
    blocks = gather_rows(rows, planes, sides)
    return return_terms(expert_terms(blocks, sides, mine, weights, cap, nexp), sides)


def experts_by_device(rows, width, ids, gate_proj, up_proj, down_proj, nexp):
    tokens = rows.shape[0]
    normed = rows[:, :width]
    gates = rows[:, width : width + nexp].astype(f32) + rows[
        :, width + nexp : width + 2 * nexp
    ].astype(f32)
    gates = jnp.take_along_axis(gates, ids, axis=1)
    capacity = 3 * tokens * TOPK // (2 * nexp)
    flat = ids.reshape(-1)
    member = (flat[:, None] == jnp.arange(nexp, dtype=jnp.int32)[None, :]).astype(jnp.int32)
    rank = jnp.sum((jnp.cumsum(member, axis=0) - 1) * member, axis=1)
    slot = flat * capacity + rank
    place = slot[:, None] == jnp.arange(nexp * capacity, dtype=jnp.int32)[None, :]
    route = jnp.any(place.reshape(tokens, TOPK, nexp * capacity), axis=1).astype(bf16)
    packed = jnp.einsum("ts,td->sd", route, normed, preferred_element_type=f32).astype(bf16)
    outgoing = packed.reshape(nexp, capacity, width)
    taken = lax.all_to_all(outgoing, ("seq", "exp"), split_axis=0, concat_axis=0, tiled=True)
    taken = taken.reshape(-1, width)
    gate = jnp.dot(taken, gate_proj[0], preferred_element_type=f32)
    upv = jnp.dot(taken, up_proj[0], preferred_element_type=f32)
    act = (jax.nn.silu(gate) * upv).astype(bf16)
    result = jnp.dot(act, down_proj[0], preferred_element_type=f32).astype(bf16)
    result = result.reshape(nexp, capacity, width)
    back = lax.all_to_all(result, ("seq", "exp"), split_axis=0, concat_axis=0, tiled=True)
    gathered = back.reshape(nexp * capacity, width)[slot].reshape(tokens, TOPK, width)
    return [jnp.sum(gates[:, :, None] * gathered.astype(f32), axis=1)]


def body(
    queries,
    new_keys,
    new_values,
    cache_keys,
    cache_values,
    cache_len,
    residual_in,
    out_weight,
    norm_gain,
    router_weight,
    expert_ids,
    gate_proj,
    up_proj,
    down_proj,
):
    nseq, nplace = lax.axis_size("seq"), lax.axis_size("exp")
    tokens, width = residual_in.shape[1:]
    nexp = router_weight.shape[1]
    by_chip = nseq * nplace <= 32
    me = lax.axis_index("seq").astype(jnp.int32).reshape(1)
    weights = [gate_proj, up_proj, down_proj]
    parts, pairs = project_attention(
        me,
        cache_len,
        queries[0],
        new_keys[0],
        new_values[0],
        cache_keys[0],
        cache_values[0],
        out_weight,
        weights if by_chip else [],
    )
    mixed, rows = norm_rows(
        residual_in[0], parts, norm_gain, router_weight, expert_ids[0]
    )
    if by_chip:
        rows, pairs = lax.optimization_barrier((rows, pairs))
        terms = experts_by_chip(rows, width, pairs, nexp)
    else:
        terms = experts_by_device(rows, width, expert_ids[0], *weights, nexp)
    return add(mixed, *terms).astype(bf16).reshape(1, tokens, width)


def solution(mesh):
    in_specs = (
        P("exp", "seq", None),
        P("exp", "seq", None),
        P("exp", "seq", None),
        P("exp", "seq", None),
        P("exp", "seq", None),
        P("exp"),
        P("exp", "seq", None),
        P("seq", None),
        P(),
        P(),
        P("exp", "seq", None),
        P(("seq", "exp"), None, None),
        P(("seq", "exp"), None, None),
        P(("seq", "exp"), None, None),
    )
    out_specs = P("exp", "seq", None)
    return jax.shard_map(body, mesh=mesh, in_specs=in_specs, out_specs=out_specs, check_vma=False)
```
